32 devices in a mesh: band: 2 (over x), wide: 16 (over z, y, core).
Axes of the slice: x: 2, y: 2, z: 4, core: 2. Of those that a mesh axis runs over, the one named last changes fastest.
Arguments:
- visibilities: bfloat16 [2, 1, 256, 40960], P(None, None, ('band', 'wide')), parts along dimension 2, may hold values from -1 to 2.5, as said below
- kept_baseline_mask: int32 [81920], P('band'), parts along dimension 0, may hold values 0 or 1
- fitted_mode_count: int32 [40960], P('wide'), may hold values from 4 to 16
- station_order: int32 [256], replicated, may hold values from 0 to 255, each once
- station_xy: float32 [1, 2, 256], replicated, may hold values from -8 to 8
- comp_lm: float32 [2, 512], replicated, may hold values from -0.5 to 0.5
- comp_flux: float32 [512], replicated, may hold values from 0.2 to 2
- centre_flux: float32 [256], P(('band', 'wide')), parts along dimension 0, may hold values from 1 to 3
Outputs:
- gains: float32 [2, 512], P(None, 'band'), parts along dimension 1
- residual: bfloat16 [2, 1, 256, 40960], P(None, None, 'band', 'wide'), parts along dimension 2
The draws below stay inside these ranges and needn't reach their ends.
There are 2 independent parts, one for each index of `band`. The reference program is written for one: setup_inputs(seed, part) draws one part's arguments, and reference() takes and returns one part's arrays. A program takes and returns all parts, laid end to end along the dimension named above; an argument that names none is the same for every part. Nothing has to cross between parts.
Inputs may be any that keep to these rules, and one draw needn't show every extreme that they name: `visibilities`: real parts lie in 0.5 to 2.5, imaginary parts in -1 to 1. Each baseline fits its fitted_mode_count lowest modes.
All inputs are finite; a program needn't handle non-finite values.
Results may differ from the reference program's by a relative error of at most 0.011.
Values may be sent and summed in bfloat16 or wider, within the bound.
No kernel may reach another device: no remote copies, remote signals or barrier semaphores. Data moves between devices by JAX's collectives and lax.ppermute only.
A program may use at most 128 MiB of HBM per device.

```python
import math
import jax
import jax.numpy as jnp
import numpy as np
from jax import lax

STATIONS = 256
GROUP = 64
COMPS = 512
FREQ_CHANNELS = 128
FOREGROUND_MODES = 16
TIME_SLABS = 1
CAL_ITERS = 3
ROUNDS = 3
BASELINE_SLOTS = 40960


def draw_visibilities(key, part):
    key = jax.random.fold_in(key, 17)
    real_key, imag_key = jax.random.split(key)
    lattice_dimensions = (TIME_SLABS, FREQ_CHANNELS, BASELINE_SLOTS)
    real_part = jax.random.uniform(real_key, lattice_dimensions, jnp.float32, 0.5, 2.5)
    imag_part = jnp.clip(0.3 * jax.random.normal(imag_key, lattice_dimensions, jnp.float32), -1.0, 1.0)
    return jnp.stack([real_part, imag_part]).astype(jnp.bfloat16)


def touch_ends(entries, stream_key, smallest, high):
    shape = entries.shape
    index_at = [jax.random.randint(jax.random.fold_in(stream_key, axis), (), 0, shape[axis]) for axis in range(len(shape))]
    entries = entries.at[tuple(index_at)].set(smallest)
    longest = shape.index(max(shape))
    index_at[longest] = (index_at[longest] + 1) % shape[longest]
    return entries.at[tuple(index_at)].set(high)


def shard_levels(stream_key, dims, shards, low, high):
    loudness = 1.0
    for dim, blocks in shards:
        heights = jax.random.uniform(jax.random.fold_in(jax.random.fold_in(stream_key, 6), dim), (blocks,), jnp.float32, low / len(shards), high / len(shards))
        loudness = loudness * jnp.repeat(jnp.exp(heights), dims[dim] // blocks).reshape((-1,) + (1,) * (len(dims) - 1 - dim))
    return loudness


def setup_inputs(seed: int = 0, part: int = 0) -> dict:
    splits = jax.random.split(jax.random.key(seed), 9)
    part_keys = jax.random.split(jax.random.fold_in(splits[8], part), 9)
    return {
        "visibilities": draw_visibilities(jax.random.fold_in(jax.random.fold_in(splits[8], part), 71), part),
        "kept_baseline_mask": touch_ends((jax.random.randint(part_keys[1], (BASELINE_SLOTS,), 0, 10) < 9).astype(jnp.int32), jax.random.fold_in(part_keys[1], 1), 0, 1),
        "fitted_mode_count": touch_ends(jax.random.randint(splits[2], (BASELINE_SLOTS,), 4, FOREGROUND_MODES + 1), jax.random.fold_in(splits[2], 1), 4, FOREGROUND_MODES).astype(jnp.int32),
        "station_order": jax.random.permutation(splits[3], STATIONS).astype(jnp.int32),
        "station_xy": jnp.clip(jax.random.uniform(splits[4], (TIME_SLABS, 2, STATIONS), jnp.float32, -8.0, 8.0), -8.0, 8.0),
        "comp_lm": jnp.clip(jax.random.uniform(splits[5], (2, COMPS), jnp.float32, -0.5, 0.5), -0.5, 0.5),
        "comp_flux": jnp.clip(jnp.exp(jax.random.uniform(splits[6], (COMPS,), jnp.float32, math.log(0.2), math.log(2.0))), 0.2, 2.0),
        "centre_flux": jnp.clip(jnp.exp(math.log(3.0) - 1.0986123 * jax.random.uniform(part_keys[7], (FREQ_CHANNELS,), jnp.float32) ** shard_levels(part_keys[7], (FREQ_CHANNELS,), ((0, 16),), -0.2, 0.2)), 1.0, 3.0),
    }


def block_pairs(groups):
    row_list = []
    col_list = []
    for first_group in range(groups):
        for second_group in range(first_group, groups):
            row_list.append(first_group)
            col_list.append(second_group)
    return (np.array(row_list, np.int32), np.array(col_list, np.int32))

def baseline_tables(groups, group_size):
    row_groups, col_groups = block_pairs(groups)
    inside = np.arange(group_size * group_size)
    row_inside = inside // group_size
    col_inside = inside % group_size
    row_station = (row_groups[:, None] * group_size + row_inside[None, :]).reshape(-1).astype(np.int32)
    col_station = (col_groups[:, None] * group_size + col_inside[None, :]).reshape(-1).astype(np.int32)
    usable = ((row_groups[:, None] != col_groups[:, None]) | (row_inside[None, :] < col_inside[None, :])).reshape(-1)
    return (row_station, col_station, usable.astype(np.float32))

def cosine_basis(channels, mode_total):
    channel_mid = jnp.arange(channels, dtype=jnp.float32)[:, None] + 0.5
    mode_order = jnp.arange(mode_total, dtype=jnp.float32)[None, :]
    mode_scale = jnp.where(mode_order == 0, math.sqrt(1.0 / channels), math.sqrt(2.0 / channels))
    return mode_scale * jnp.cos(math.pi / channels * channel_mid * mode_order)

def predict_channel(xy_pair, comp_lm, flux_weight, centre, frequency, row_groups, col_groups, groups):
    offset = xy_pair[0][:, None] * comp_lm[0][None, :] + xy_pair[1][:, None] * comp_lm[1][None, :]
    phase_angle = 2.0 * math.pi * frequency * offset
    cosine = jnp.cos(phase_angle)
    sine_part = jnp.sin(phase_angle)
    rounded = lax.optimization_barrier((cosine.astype(jnp.bfloat16), sine_part.astype(jnp.bfloat16), (cosine * flux_weight[None, :]).astype(jnp.bfloat16), (sine_part * flux_weight[None, :]).astype(jnp.bfloat16)))
    plain_cos, plain_sin, bright_cos, bright_sin = [member.astype(jnp.float32).reshape(groups, GROUP, -1) for member in rounded]
    real_part = jnp.einsum('bik,bjk->bij', bright_cos[row_groups], plain_cos[col_groups]) + jnp.einsum('bik,bjk->bij', bright_sin[row_groups], plain_sin[col_groups])
    imag_part = jnp.einsum('bik,bjk->bij', bright_sin[row_groups], plain_cos[col_groups]) - jnp.einsum('bik,bjk->bij', bright_cos[row_groups], plain_sin[col_groups])
    return jnp.stack([real_part.reshape(-1) + centre, imag_part.reshape(-1)]).astype(jnp.bfloat16)

def channel_sums(observed, model_visibility, weights):
    obs_re = observed[0].astype(jnp.float32)
    obs_im = observed[1].astype(jnp.float32)
    mod_re = model_visibility[0].astype(jnp.float32)
    mod_im = model_visibility[1].astype(jnp.float32)
    cross_re = lax.optimization_barrier(jnp.sum(obs_re * mod_re + obs_im * mod_im, axis=(0, 1))) * weights
    cross_im = lax.optimization_barrier(jnp.sum(obs_im * mod_re - obs_re * mod_im, axis=(0, 1))) * weights
    model_power = lax.optimization_barrier(jnp.sum(mod_re * mod_re + mod_im * mod_im, axis=(0, 1))) * weights
    return jnp.stack([cross_re, cross_im, model_power])

def station_sums(baseline_totals, row_part, col_part, gain_pair, stations):
    cross_re = baseline_totals[0]
    cross_im = baseline_totals[1]
    model_power = baseline_totals[2]
    row_re = gain_pair[0][row_part]
    row_im = gain_pair[1][row_part]
    col_re = gain_pair[0][col_part]
    col_im = gain_pair[1][col_part]
    numerator_re = jax.ops.segment_sum(cross_re * col_re - cross_im * col_im, row_part, num_segments=stations) + jax.ops.segment_sum(cross_re * row_re + cross_im * row_im, col_part, num_segments=stations)
    numerator_im = jax.ops.segment_sum(cross_re * col_im + cross_im * col_re, row_part, num_segments=stations) + jax.ops.segment_sum(cross_re * row_im - cross_im * row_re, col_part, num_segments=stations)
    denominator = jax.ops.segment_sum(model_power * (col_re * col_re + col_im * col_im), row_part, num_segments=stations) + jax.ops.segment_sum(model_power * (row_re * row_re + row_im * row_im), col_part, num_segments=stations)
    return jnp.stack([numerator_re, numerator_im, denominator])

def gain_update(station_terms, gain_pair, iteration):
    updated = jnp.stack([station_terms[0] / station_terms[2], station_terms[1] / station_terms[2]])
    if iteration % 2 == 1:
        updated = 0.5 * (updated + gain_pair)
    return updated

def corrupted_gap(observed, model_visibility, gain_pair, row_part, col_part, weights):
    row_re = gain_pair[0][row_part]
    row_im = gain_pair[1][row_part]
    col_re = gain_pair[0][col_part]
    col_im = gain_pair[1][col_part]
    prod_re = row_re * col_re + row_im * col_im
    prod_im = row_im * col_re - row_re * col_im
    mod_re = model_visibility[0].astype(jnp.float32)
    mod_im = model_visibility[1].astype(jnp.float32)
    pred_re = prod_re * mod_re - prod_im * mod_im
    pred_im = prod_re * mod_im + prod_im * mod_re
    data_gap = jnp.stack([observed[0].astype(jnp.float32) - pred_re, observed[1].astype(jnp.float32) - pred_im]) * weights
    return lax.optimization_barrier(data_gap.astype(jnp.bfloat16))

def fit_modes(data_gap, counts, weights):
    channels = data_gap.shape[2]
    mode_basis = cosine_basis(channels, FOREGROUND_MODES)
    coefficients = jnp.einsum('fk,csfb->cskb', mode_basis, data_gap.astype(jnp.float32), precision=lax.Precision.HIGHEST)
    kept_modes = (jnp.arange(FOREGROUND_MODES, dtype=jnp.int32)[:, None] < counts[None, :]).astype(jnp.float32)
    fitted = jnp.einsum('fk,cskb->csfb', mode_basis, coefficients * kept_modes, precision=lax.Precision.HIGHEST)
    return lax.optimization_barrier((fitted * weights).astype(jnp.bfloat16))

def reference(visibilities, kept_baseline_mask, fitted_mode_count, station_order, station_xy, comp_lm, comp_flux, centre_flux):
    groups = STATIONS // GROUP
    row_groups, col_groups = block_pairs(groups)
    row_np, col_np, usable_np = baseline_tables(groups, GROUP)
    row_station = jnp.asarray(row_np)
    col_station = jnp.asarray(col_np)
    weights = kept_baseline_mask.astype(jnp.float32) * jnp.asarray(usable_np).astype(jnp.float32)
    xy_ordered = station_xy[:, :, station_order]
    flux_weight = comp_flux * (1.0 / math.sqrt(COMPS))

    def predict_item(item_index):
        slab_id = item_index // FREQ_CHANNELS
        channel = item_index % FREQ_CHANNELS
        frequency = 1.0 + 0.25 * channel.astype(jnp.float32) / FREQ_CHANNELS
        return predict_channel(xy_ordered[slab_id], comp_lm, flux_weight, centre_flux[channel], frequency, row_groups, col_groups, groups)
    model_visibility = lax.map(predict_item, jnp.arange(TIME_SLABS * FREQ_CHANNELS, dtype=jnp.int32))
    model_visibility = model_visibility.reshape(TIME_SLABS, FREQ_CHANNELS, 2, BASELINE_SLOTS).transpose(2, 0, 1, 3)
    gain_pair = jnp.stack([jnp.ones((STATIONS,), jnp.float32), jnp.zeros((STATIONS,), jnp.float32)])
    for round_id in range(ROUNDS):
        baseline_totals = channel_sums(visibilities, model_visibility, weights)
        for iteration in range(CAL_ITERS):
            gain_pair = gain_update(station_sums(baseline_totals, row_station, col_station, gain_pair, STATIONS), gain_pair, iteration)
        if round_id + 1 < ROUNDS:
            data_gap = corrupted_gap(visibilities, model_visibility, gain_pair, row_station, col_station, weights)
            fitted = fit_modes(data_gap, fitted_mode_count, weights)
            model_visibility = (model_visibility.astype(jnp.float32) + fitted.astype(jnp.float32)).astype(jnp.bfloat16)
    residual = corrupted_gap(visibilities, model_visibility, gain_pair, row_station, col_station, weights)
    gains = jnp.zeros((2, STATIONS), jnp.float32).at[:, station_order].set(gain_pair)
    return (gains, residual)
```

```python
import math

import jax
import jax.numpy as jnp
import numpy as np
from jax import lax
from jax.experimental import pallas as pl
from jax.experimental.pallas import tpu as pltpu
from jax.sharding import PartitionSpec as P

GROUP = 64
FREQ_CHANNELS = 128
MODES = 16
CAL_ITERS = 3
ROUNDS = 3
STATS = 7
LANES = 128
UNROLL = 4
VMEM = pltpu.MemorySpace.VMEM
SMEM = pltpu.MemorySpace.SMEM
F32 = jnp.float32
BF16 = jnp.bfloat16


def row_groups_of(row, groups):
    block = row >> 6
    first = jnp.zeros_like(block)
    start = jnp.zeros_like(block)
    edge = 0
    for group in range(1, groups):
        edge += groups - group + 1
        past = (block >= edge).astype(jnp.int32)
        first = first + past
        start = start + past * (groups - group + 1)
    return first, block - start + first


def basis_tables():
    mid = np.arange(FREQ_CHANNELS)[:, None] + 0.5
    order = np.arange(MODES)[None, :]
    scale = np.where(order == 0, math.sqrt(1.0 / FREQ_CHANNELS), math.sqrt(2.0 / FREQ_CHANNELS))
    basis = (scale * np.cos(math.pi / FREQ_CHANNELS * mid * order)).astype(np.float32)
    high = np.asarray(jnp.dtype(BF16).type(0)).dtype
    basis_hi = basis.astype(high)
    basis_lo = (basis - basis_hi.astype(np.float32)).astype(high)
    rows = 2 * FREQ_CHANNELS
    blank = np.zeros((rows, MODES), np.float32)
    parts = {}
    for name, table in (("hi", basis_hi), ("lo", basis_lo)):
        for side in range(2):
            spread = blank.copy().reshape(FREQ_CHANNELS // 8, 2, 8, MODES)
            spread[:, side] = table.astype(np.float32).reshape(FREQ_CHANNELS // 8, 8, MODES)
            parts[name, side] = spread.reshape(rows, MODES)
    fit = np.concatenate(
        [parts["hi", 0], parts["lo", 0], parts["hi", 1], parts["lo", 1]], axis=1
    ).T.astype(high)
    expand = np.concatenate(
        [parts["hi", 0], parts["hi", 0], parts["hi", 1], parts["hi", 1], parts["lo", 0], parts["lo", 1]],
        axis=1,
    ).astype(high)
    return fit, expand


def turn_trig(turns):
    quarter = jnp.floor(turns * 4.0 + 0.5)
    angle = (turns - 0.25 * quarter) * (2.0 * math.pi)
    square = angle * angle
    sine = angle * (
        1.0
        + square
        * (-1.0 / 6 + square * (1.0 / 120 + square * (-1.0 / 5040 + square * (1.0 / 362880))))
    )
    cosine = 1.0 + square * (
        -0.5
        + square
        * (1.0 / 24 + square * (-1.0 / 720 + square * (1.0 / 40320 + square * (-1.0 / 3628800))))
    )
    phase = quarter - 4.0 * jnp.floor(quarter * 0.25)
    odd = (phase == 1.0) | (phase == 3.0)
    cos_out = jnp.where(odd, sine, cosine)
    sin_out = jnp.where(odd, cosine, sine)
    cos_out = jnp.where((phase == 1.0) | (phase == 2.0), -cos_out, cos_out)
    sin_out = jnp.where(phase >= 2.0, -sin_out, sin_out)
    return cos_out, sin_out


def pack_kernel(wide, base, source, centre, target):
    chan = centre.shape[0]
    row = lax.broadcasted_iota(jnp.int32, (2 * chan, LANES), 0)
    lane = lax.broadcasted_iota(jnp.int32, (2 * chan, LANES), 1)
    value = jnp.zeros(row.shape, F32)
    for c in range(chan):
        value = jnp.where(row == c, centre[c], value)
    high = value.astype(BF16).astype(F32)
    middle = (value - high).astype(BF16).astype(F32)
    low = value - high - middle
    tail = jnp.where(lane == 0, high, jnp.where(lane == 1, middle, jnp.where(lane == 2, low, 0.0)))
    tail = tail.astype(BF16)
    for peer in range(wide):
        target[peer, :, 0:base] = source[:, peer * base : (peer + 1) * base]
        target[peer, :, base : base + LANES] = tail


def predict_kernel(
    groups,
    tiles,
    padded,
    order,
    xy,
    lm,
    flux,
    model,
    pos_x,
    pos_y,
    row_c,
    row_s,
    row_dc,
    row_ds,
    col_c,
    col_s,
    col_dc,
    col_ds,
    left_a,
    right_a,
    left_b,
    right_b,
):
    comps = lm.shape[1]
    rank = lax.axis_index("wide")
    first_row = rank * (2 * tiles)
    last_row = first_row + (2 * tiles - 1)
    col_a = row_groups_of(first_row, groups)[1] * GROUP
    col_b = row_groups_of(last_row, groups)[1] * GROUP
    edge = jnp.minimum((((first_row >> 6) + 1) * GROUP - first_row) >> 1, tiles)
    pos_x[...] = jnp.zeros_like(pos_x)
    pos_y[...] = jnp.zeros_like(pos_y)

    def place(slot, position):
        station = order[position]
        pos_x[pl.ds(slot, 1), :] = jnp.full((1, LANES), xy[0, station], F32)
        pos_y[pl.ds(slot, 1), :] = jnp.full((1, LANES), xy[1, station], F32)

    def place_row(t, carry):
        for half in range(2):
            row = first_row + 2 * t + half
            place(half * padded + t, row_groups_of(row, groups)[0] * GROUP + (row & 63))
        return carry

    def place_col(j, carry):
        place(2 * padded + j, col_a + j)
        place(2 * padded + GROUP + j, col_b + j)
        return carry

    lax.fori_loop(0, tiles, place_row, 0, unroll=2)
    lax.fori_loop(0, GROUP, place_col, 0, unroll=4)
    step = 0.25 / FREQ_CHANNELS
    rows = 2 * padded
    weight = flux[...] * (1.0 / math.sqrt(comps))
    for k in range(0, comps, LANES):
        lane = slice(k, k + LANES)
        axis_l = lm[0:1, lane]
        axis_m = lm[1:2, lane]
        turns = pos_x[0:rows, :] * axis_l + pos_y[0:rows, :] * axis_m
        cosine, sine = turn_trig(turns)
        row_c[:, lane] = cosine * weight[:, lane]
        row_s[:, lane] = sine * weight[:, lane]
        row_dc[:, lane], row_ds[:, lane] = turn_trig(turns * step)
        turns = (
            pos_x[rows : rows + LANES, :] * axis_l + pos_y[rows : rows + LANES, :] * axis_m
        ).T
        col_c[lane, :], col_s[lane, :] = turn_trig(turns)
        col_dc[lane, :], col_ds[lane, :] = turn_trig(turns * step)

    def fill(left, right):
        for k in range(0, comps, 16):
            part = slice(k, k + 16)
            c, s, dc, ds = col_c[part, :], col_s[part, :], col_dc[part, :], col_ds[part, :]
            for u in range(UNROLL):
                right[u, part, :] = c.astype(BF16)
                right[u, comps + k : comps + k + 16, :] = s.astype(BF16)
                c, s = c * dc - s * ds, s * dc + c * ds
            col_c[part, :], col_s[part, :] = c, s
        for r in range(0, rows, 16):
            part = slice(r, r + 16)
            low = slice(rows + r, rows + r + 16)
            for k in range(0, comps, LANES):
                lane = slice(k, k + LANES)
                high = slice(comps + k, comps + k + LANES)
                c, s, dc, ds = row_c[part, lane], row_s[part, lane], row_dc[part, lane], row_ds[part, lane]
                for u in range(UNROLL):
                    c16, s16 = c.astype(BF16), s.astype(BF16)
                    left[u, part, lane] = c16
                    left[u, part, high] = s16
                    left[u, low, lane] = s16
                    left[u, low, high] = -c16
                    c, s = c * dc - s * ds, s * dc + c * ds
                row_c[part, lane], row_s[part, lane] = c, s

    lane_id = lax.broadcasted_iota(jnp.int32, (padded, LANES), 1)
    first_half = lane_id < GROUP
    in_a = lax.broadcasted_iota(jnp.int32, (padded, LANES), 0) < edge

    def multiply(left, right, group):
        for u in range(UNROLL):
            product = jnp.dot(left[u], right[u], preferred_element_type=F32)
            channel = group * UNROLL + u
            base = (channel >> 3) * 16 + (channel & 7)
            for side in range(2):
                even = product[side * rows : side * rows + padded]
                odd = product[side * rows + padded : side * rows + 2 * padded]
                even = jnp.where(in_a, even, pltpu.roll(even, GROUP, 1))
                odd = jnp.where(in_a, pltpu.roll(odd, GROUP, 1), odd)
                model[pl.ds(base + 8 * side, padded, stride=256), :] = jnp.where(
                    first_half, even, odd
                )

    fill(left_a, right_a)

    def two_groups(pair, carry):
        fill(left_b, right_b)
        multiply(left_a, right_a, 2 * pair)
        fill(left_a, right_a)
        multiply(left_b, right_b, 2 * pair + 1)
        return carry

    lax.fori_loop(0, FREQ_CHANNELS // (2 * UNROLL), two_groups, 0)


def coefficients(fit, block):
    raw = jnp.dot(fit, block, preferred_element_type=F32)
    return raw[0:16] + raw[16:32], raw[32:48] + raw[48:64]


def tile_weights(groups, tiles, first_row, t, kept):
    lane = lax.broadcasted_iota(jnp.int32, (1, LANES), 1)
    row = first_row + 2 * t
    first, second = row_groups_of(row, groups)
    inside = (row & 63) + (lane >> 6)
    usable = (first != second) | (inside < (lane & 63))
    mask = kept[pl.ds((first_row >> 1) + t, 1), :].astype(F32)
    return jnp.where(usable, mask, 0.0)


def stats_kernel(
    groups, tiles, observed, predicted, kept, counts, fit, stats, model, model_modes, data_modes, shift
):
    rank = lax.axis_index("wide")
    first_row = rank * (2 * tiles)
    mode = lax.broadcasted_iota(jnp.int32, (MODES, LANES), 0)
    tail = observed[:, :, tiles * LANES : (tiles + 1) * LANES].reshape(256, LANES).astype(F32)
    shift[...] = jnp.broadcast_to(jnp.sum(tail, axis=1, keepdims=True), (256, LANES))

    def one(t):
        data = observed[:, :, pl.ds(pl.multiple_of(t * LANES, LANES), LANES)].reshape(256, LANES)
        part = pl.ds(pl.multiple_of(t * 256, 256), 256)
        block = (predicted[part, :] + shift[...]).astype(BF16)
        model[part, :] = block
        data_parts = data.astype(F32).reshape(FREQ_CHANNELS // 8, 2, 8, LANES)
        mod_parts = block.astype(F32).reshape(FREQ_CHANNELS // 8, 2, 8, LANES)
        obs_re, obs_im = data_parts[:, 0], data_parts[:, 1]
        mod_re, mod_im = mod_parts[:, 0], mod_parts[:, 1]

        def total(terms):
            return jnp.sum(jnp.sum(terms, axis=0), axis=0, keepdims=True)

        cross_re = total(obs_re * mod_re + obs_im * mod_im)
        cross_im = total(obs_im * mod_re - obs_re * mod_im)
        power = total(mod_re * mod_re + mod_im * mod_im)
        v_re, v_im = coefficients(fit[...], data)
        m_re, m_im = coefficients(fit[...], block)
        part32 = pl.ds(pl.multiple_of(t * 32, 32), 32)
        data_modes[part32, :] = jnp.concatenate([v_re, v_im])
        model_modes[part32, :] = jnp.concatenate([m_re, m_im])
        inside = (mode < counts[pl.ds(t, 1), :]).astype(F32)
        vv = jnp.sum(inside * (v_re * v_re + v_im * v_im), axis=0, keepdims=True)
        vm_re = jnp.sum(inside * (v_re * m_re + v_im * m_im), axis=0, keepdims=True)
        vm_im = jnp.sum(inside * (v_im * m_re - v_re * m_im), axis=0, keepdims=True)
        mm = jnp.sum(inside * (m_re * m_re + m_im * m_im), axis=0, keepdims=True)
        weight = tile_weights(groups, tiles, first_row, t, kept)
        rows = jnp.concatenate(
            [cross_re, cross_im, vv, vm_re, vm_im, power, mm, jnp.zeros((1, LANES), F32)]
        )
        return rows * weight

    def two(pair, carry):
        stats[pl.ds(pl.multiple_of(pair * 16, 16), 16), :] = jnp.concatenate(
            [one(2 * pair), one(2 * pair + 1)]
        ).astype(BF16)
        return carry

    lax.fori_loop(0, tiles // 2, two, 0)


def split_rows(values):
    row = lax.broadcasted_iota(jnp.int32, (16, values[0].shape[1]), 0)
    out = jnp.zeros(row.shape, F32)
    for at, value in enumerate(values):
        high = value.astype(BF16).astype(F32)
        out = jnp.where(row == 2 * at, high, out)
        out = jnp.where(row == 2 * at + 1, value - high, out)
    return out.astype(BF16)


def solve_kernel(
    groups,
    tiles,
    wide,
    gathered,
    observed,
    model,
    model_modes,
    data_modes,
    kept,
    counts,
    order,
    expand,
    gains,
    residual,
    flat,
    upper,
    full,
    state,
    weights,
    row_gain_re,
    row_gain_im,
    col_gain_re,
    col_gain_im,
):
    stations = groups * GROUP
    rank = lax.axis_index("wide")
    first_row = rank * (2 * tiles)
    chunk = 8 * tiles
    for k in range(wide):
        flip = 0
        bit, distance = 1, wide // 2
        while distance:
            flip += distance if k & bit else 0
            bit, distance = bit * 2, distance // 2
        owner = rank ^ flip
        flat[pl.ds(pl.multiple_of(owner * chunk, 16), chunk), :] = gathered[k].astype(F32)
    halves = stations // LANES
    lane32 = lax.broadcasted_iota(jnp.int32, (32, LANES), 1) < GROUP
    block_id = {}
    for first in range(groups):
        for second in range(first, groups):
            block_id[first, second] = len(block_id)
    for stat in range(STATS):
        for first in range(groups):
            for half in range(halves):
                pair = []
                for side in range(2):
                    index = block_id.get((first, 2 * half + side))
                    pair.append(
                        jnp.zeros((32, LANES), F32)
                        if index is None
                        else flat[pl.ds(256 * index + stat, 32, stride=8), :]
                    )
                if block_id.get((first, 2 * half + 1)) is None:
                    continue
                even = jnp.where(lane32, pair[0], pltpu.roll(pair[1], GROUP, 1))
                odd = jnp.where(lane32, pltpu.roll(pair[0], GROUP, 1), pair[1])
                upper[half, pl.ds(GROUP * first, 32, stride=2), :] = even
                upper[half, pl.ds(GROUP * first + 1, 32, stride=2), :] = odd
        sign = -1.0 if stat in (1, 4) else 1.0
        for a in range(halves):
            rows_a = slice(LANES * a, LANES * (a + 1))
            for b in range(a, halves):
                rows_b = slice(LANES * b, LANES * (b + 1))
                block = upper[b, rows_a, :]
                turned = block.T * sign
                if a == b:
                    full[stat, rows_a, rows_a] = block + turned
                else:
                    full[stat, rows_a, rows_b] = block
                    full[stat, rows_b, rows_a] = turned

    def put_weights(part, chunk_rows, value):
        high = value.astype(BF16)
        low = (value - high.astype(F32)).astype(BF16)
        weights[chunk_rows, (2 * part) * stations : (2 * part + 1) * stations] = high
        weights[chunk_rows, (2 * part + 1) * stations : (2 * part + 2) * stations] = low

    gain_re = jnp.ones((1, stations), F32)
    gain_im = jnp.zeros((1, stations), F32)
    for round_id in range(ROUNDS):

        def build(step, carry):
            rows = pl.ds(pl.multiple_of(step * 16, 16), 16)
            cross_re, cross_im, power = full[0, rows, :], full[1, rows, :], full[5, rows, :]
            if round_id:
                vv, vm_re, vm_im, mm = (full[i, rows, :] for i in (2, 3, 4, 6))
                col_re = jnp.concatenate([col_gain_re[rows, round_id - 1, :]] * halves, axis=1)
                col_im = jnp.concatenate([col_gain_im[rows, round_id - 1, :]] * halves, axis=1)
                rest_re = 1.0 - (col_re * gain_re + col_im * gain_im)
                rest_im = -(col_im * gain_re - col_re * gain_im)
                if round_id == 1:
                    a_re, a_im = jnp.ones_like(rest_re), jnp.zeros_like(rest_re)
                    b_re, b_im = rest_re, rest_im
                else:
                    a_re, a_im, b_re, b_im = (state[i, rows, :] for i in range(4))
                    a_re, a_im = 1.0 + rest_re * a_re - rest_im * a_im, rest_re * a_im + rest_im * a_re
                    b_re, b_im = rest_re * b_re - rest_im * b_im, rest_re * b_im + rest_im * b_re
                if round_id + 1 < ROUNDS:
                    for i, value in enumerate((a_re, a_im, b_re, b_im)):
                        state[i, rows, :] = value
                turn_re = b_re - 1.0
                cross_re = cross_re + a_re * vv + turn_re * vm_re + b_im * vm_im
                cross_im = cross_im - a_im * vv + turn_re * vm_im - b_im * vm_re
                mix_re = a_re * b_re + a_im * b_im
                mix_im = a_im * b_re - a_re * b_im
                power = (
                    power
                    + (a_re * a_re + a_im * a_im) * vv
                    + (b_re * b_re + b_im * b_im - 1.0) * mm
                    + 2.0 * (mix_re * vm_re - mix_im * vm_im)
                )
            put_weights(0, rows, cross_re)
            put_weights(1, rows, cross_im)
            put_weights(2, rows, power)
            return carry

        lax.fori_loop(0, stations // 16, build, 0)
        for iteration in range(CAL_ITERS):
            left = split_rows([gain_re, gain_im, gain_re * gain_re + gain_im * gain_im])
            raw = jnp.dot(left, weights[...], preferred_element_type=F32)

            def product(vector, part):
                at = 2 * part * stations
                high = raw[2 * vector : 2 * vector + 1, at : at + stations]
                low = raw[2 * vector + 1 : 2 * vector + 2, at : at + stations]
                return high + low + raw[2 * vector : 2 * vector + 1, at + stations : at + 2 * stations]

            below = product(2, 2)
            next_re = (product(0, 0) + product(1, 1)) / below
            next_im = (product(1, 0) - product(0, 1)) / below
            if iteration % 2 == 1:
                next_re = 0.5 * (next_re + gain_re)
                next_im = 0.5 * (next_im + gain_im)
            gain_re, gain_im = next_re, next_im
        lane1 = lax.broadcasted_iota(jnp.int32, (1, LANES), 1) < GROUP
        for value, row_gain, col_gain in (
            (gain_re, row_gain_re, col_gain_re),
            (gain_im, row_gain_im, col_gain_im),
        ):
            for half in range(halves):
                part = value[:, LANES * half : LANES * (half + 1)]
                turned = pltpu.roll(jnp.broadcast_to(part, (8, LANES)), GROUP, 1)[0:1]
                row_gain[2 * half, round_id : round_id + 1, :] = jnp.where(lane1, part, turned)
                row_gain[2 * half + 1, round_id : round_id + 1, :] = jnp.where(lane1, turned, part)
                col_gain[LANES * half : LANES * (half + 1), round_id, :] = jnp.broadcast_to(
                    part, (LANES, LANES)
                ).T

    hot = (
        lax.broadcasted_iota(jnp.int32, (stations, stations), 0) == order[...]
    ).astype(BF16)
    pieces = []
    for value in (gain_re, gain_im):
        high = value.astype(BF16).astype(F32)
        middle = (value - high).astype(BF16).astype(F32)
        pieces += [high, middle, value - high - middle]
    row16 = lax.broadcasted_iota(jnp.int32, (16, stations), 0)
    left = jnp.zeros((16, stations), F32)
    for at, piece in enumerate(pieces):
        left = jnp.where(row16 == at, piece, left)
    spread = lax.dot_general(
        left.astype(BF16), hot, (((1,), (1,)), ((), ())), preferred_element_type=F32
    )
    gains[0:1, :] = spread[0:1] + spread[1:2] + spread[2:3]
    gains[1:2, :] = spread[3:4] + spread[4:5] + spread[5:6]

    mode = lax.broadcasted_iota(jnp.int32, (MODES, LANES), 0)
    lane8 = lax.broadcasted_iota(jnp.int32, (8, LANES), 1) < GROUP

    def tile(t, carry):
        row = first_row + 2 * t
        first, second = row_groups_of(row, groups)
        station = first * GROUP + (row & 63)
        p_re = jnp.where(lane8, col_gain_re[station], col_gain_re[station + 1])
        p_im = jnp.where(lane8, col_gain_im[station], col_gain_im[station + 1])
        q_re, q_im = row_gain_re[second], row_gain_im[second]
        prod_re = p_re * q_re + p_im * q_im
        prod_im = p_im * q_re - p_re * q_im
        a_re, a_im = jnp.zeros((1, LANES), F32), jnp.zeros((1, LANES), F32)
        b_re, b_im = jnp.ones((1, LANES), F32), jnp.zeros((1, LANES), F32)
        for round_id in range(ROUNDS - 1):
            rest_re = 1.0 - prod_re[round_id : round_id + 1]
            rest_im = -prod_im[round_id : round_id + 1]
            a_re, a_im = 1.0 + rest_re * a_re - rest_im * a_im, rest_re * a_im + rest_im * a_re
            b_re, b_im = rest_re * b_re - rest_im * b_im, rest_re * b_im + rest_im * b_re
        b_re = b_re - 1.0
        inside = (mode < counts[pl.ds(t, 1), :]).astype(F32)
        part32 = pl.ds(pl.multiple_of(t * 32, 32), 32)
        v_re, v_im = data_modes[part32, :][0:16], data_modes[part32, :][16:32]
        m_re, m_im = model_modes[part32, :][0:16], model_modes[part32, :][16:32]
        f_re = inside * (a_re * v_re - a_im * v_im + b_re * m_re - b_im * m_im)
        f_im = inside * (a_re * v_im + a_im * v_re + b_re * m_im + b_im * m_re)
        f_re16, f_im16 = f_re.astype(BF16), f_im.astype(BF16)
        stack = jnp.concatenate(
            [
                f_re16,
                (f_re - f_re16.astype(F32)).astype(BF16),
                f_im16,
                (f_im - f_im16.astype(F32)).astype(BF16),
                f_re16,
                f_im16,
            ]
        )
        fitted = jnp.dot(expand[...], stack, preferred_element_type=F32)
        current = model[pl.ds(pl.multiple_of(t * 256, 256), 256), :].astype(F32) + fitted
        current = current.reshape(FREQ_CHANNELS // 8, 2, 8, LANES)
        lanes = pl.ds(pl.multiple_of(t * LANES, LANES), LANES)
        data = (
            observed[:, :, lanes]
            .reshape(256, LANES)
            .astype(F32)
            .reshape(FREQ_CHANNELS // 8, 2, 8, LANES)
        )
        weight = tile_weights(groups, tiles, first_row, t, kept)
        last_re, last_im = prod_re[ROUNDS - 1 : ROUNDS], prod_im[ROUNDS - 1 : ROUNDS]
        mod_re, mod_im = current[:, 0], current[:, 1]
        left_re = weight * (data[:, 0] - (last_re * mod_re - last_im * mod_im))
        left_im = weight * (data[:, 1] - (last_re * mod_im + last_im * mod_re))
        residual[0, 0, :, lanes] = left_re.reshape(FREQ_CHANNELS, LANES).astype(BF16)
        residual[1, 0, :, lanes] = left_im.reshape(FREQ_CHANNELS, LANES).astype(BF16)
        return carry

    lax.fori_loop(0, tiles, tile, 0)


def call(kernel, out_shape, scratch, name, in_spaces, mib, flops=0, moved=0):
    return pl.pallas_call(
        kernel,
        out_shape=out_shape,
        in_specs=[pl.BlockSpec(memory_space=space) for space in in_spaces],
        out_specs=jax.tree.map(lambda _: pl.BlockSpec(memory_space=VMEM), out_shape),
        scratch_shapes=scratch,
        compiler_params=pltpu.CompilerParams(vmem_limit_bytes=mib << 20),
        cost_estimate=pl.CostEstimate(flops=flops, bytes_accessed=moved, transcendentals=0),
        name=name,
    )


def gather_stats(stats, wide):
    held = stats[None]
    distance = wide // 2
    while distance:
        other = lax.ppermute(held, "wide", [(i, i ^ distance) for i in range(wide)])
        held = jnp.concatenate([held, other])
        distance //= 2
    return held


def body(
    visibilities,
    kept_baseline_mask,
    fitted_mode_count,
    station_order,
    station_xy,
    comp_lm,
    comp_flux,
    centre_flux,
):
    wide = lax.axis_size("wide")
    local_chan = visibilities.shape[2]
    total = visibilities.shape[3]
    base = total // wide
    tiles = base // LANES
    padded = -(-tiles // 8) * 8
    stations = station_order.shape[0]
    groups = stations // GROUP
    comps = comp_lm.shape[1]
    rows = 2 * padded
    fit, expand = (jnp.asarray(table) for table in basis_tables())
    kept = kept_baseline_mask.reshape(total // LANES, LANES)
    counts = fitted_mode_count.reshape(tiles, LANES)

    packed = call(
        lambda *refs: pack_kernel(wide, base, *refs),
        jax.ShapeDtypeStruct((wide, 2 * local_chan, base + LANES), BF16),
        [],
        "pack",
        [VMEM, SMEM],
        16,
        moved=8 * local_chan * total,
    )(visibilities.reshape(2 * local_chan, total), centre_flux)
    observed = lax.all_to_all(packed, "wide", 0, 0, tiled=True)
    if local_chan != 8:
        pairs = 8 // local_chan
        observed = observed.reshape(wide // pairs, pairs, 2, local_chan, base + LANES)
        observed = observed.transpose(0, 2, 1, 3, 4).reshape(wide // pairs, 16, base + LANES)

    state_row = pltpu.VMEM((rows, comps), F32)
    state_col = pltpu.VMEM((comps, LANES), F32)
    left = pltpu.VMEM((UNROLL, 2 * rows, 2 * comps), BF16)
    right = pltpu.VMEM((UNROLL, 2 * comps, LANES), BF16)
    predicted = call(
        lambda *refs: predict_kernel(groups, tiles, padded, *refs),
        jax.ShapeDtypeStruct((padded * 256, LANES), F32),
        [pltpu.VMEM((rows + LANES, LANES), F32)] * 2
        + [state_row] * 4
        + [state_col] * 4
        + [left, right, left, right],
        "predict",
        [SMEM, SMEM, VMEM, VMEM],
        24,
        FREQ_CHANNELS * 2 * 2 * rows * 2 * comps * 256,
        padded * 256 * LANES * 4,
    )(station_order, station_xy.reshape(2, stations), comp_lm, comp_flux.reshape(1, comps))
    stats, model, model_modes, data_modes = call(
        lambda *refs: stats_kernel(groups, tiles, *refs),
        (
            jax.ShapeDtypeStruct((tiles * 8, LANES), BF16),
            jax.ShapeDtypeStruct((tiles * 256, LANES), BF16),
            jax.ShapeDtypeStruct((tiles * 32, LANES), F32),
            jax.ShapeDtypeStruct((tiles * 32, LANES), F32),
        ),
        [pltpu.VMEM((256, LANES), F32)],
        "stats",
        [VMEM] * 5,
        16,
        moved=tiles * 256 * LANES * 8,
    )(observed, predicted, kept, counts, fit)
    gathered = gather_stats(stats, wide)
    gains, residual = call(
        lambda *refs: solve_kernel(groups, tiles, wide, *refs),
        (
            jax.ShapeDtypeStruct((2, stations), F32),
            jax.ShapeDtypeStruct((2, 1, FREQ_CHANNELS, base), BF16),
        ),
        [
            pltpu.VMEM((wide * tiles * 8, LANES), F32),
            pltpu.VMEM((stations // LANES, stations, LANES), F32),
            pltpu.VMEM((STATS, stations, stations), F32),
            pltpu.VMEM((4, stations, stations), F32),
            pltpu.VMEM((stations, 6 * stations), BF16),
            pltpu.VMEM((groups, 8, LANES), F32),
            pltpu.VMEM((groups, 8, LANES), F32),
            pltpu.VMEM((stations, 8, LANES), F32),
            pltpu.VMEM((stations, 8, LANES), F32),
        ],
        "solve",
        [VMEM] * 9,
        32,
        moved=tiles * 256 * LANES * 6,
    )(
        gathered,
        observed,
        model,
        model_modes,
        data_modes,
        kept,
        counts,
        station_order.reshape(1, stations),
        expand,
    )
    return gains, residual


def solution(mesh):
    placed = (
        P(None, None, ("band", "wide"), None),
        P("band"),
        P("wide"),
        P(),
        P(),
        P(),
        P(),
        P(("band", "wide")),
    )
    return jax.shard_map(
        body,
        mesh=mesh,
        in_specs=placed,
        out_specs=(P(None, "band"), P(None, None, "band", "wide")),
        check_vma=False,
    )
```

```python
import math

import jax
import jax.numpy as jnp
import numpy as np
from jax import lax
from jax.experimental import pallas as pl
from jax.experimental.pallas import tpu as pltpu
from jax.sharding import PartitionSpec as P

GROUP = 64
FREQ_CHANNELS = 128
MODES = 16
CAL_ITERS = 3
ROUNDS = 3
STATS = 7
LANES = 128
UNROLL = 4
VMEM = pltpu.MemorySpace.VMEM
SMEM = pltpu.MemorySpace.SMEM
F32 = jnp.float32
BF16 = jnp.bfloat16


def row_groups_of(row, groups):
    block = row >> 6
    first = jnp.zeros_like(block)
    start = jnp.zeros_like(block)
    edge = 0
    for group in range(1, groups):
        edge += groups - group + 1
        past = (block >= edge).astype(jnp.int32)
        first = first + past
        start = start + past * (groups - group + 1)
    return first, block - start + first


def basis_tables():
    mid = np.arange(FREQ_CHANNELS)[:, None] + 0.5
    order = np.arange(MODES)[None, :]
    scale = np.where(order == 0, math.sqrt(1.0 / FREQ_CHANNELS), math.sqrt(2.0 / FREQ_CHANNELS))
    basis = (scale * np.cos(math.pi / FREQ_CHANNELS * mid * order)).astype(np.float32)
    high = np.asarray(jnp.dtype(BF16).type(0)).dtype
    basis_hi = basis.astype(high)
    basis_lo = (basis - basis_hi.astype(np.float32)).astype(high)
    rows = 2 * FREQ_CHANNELS
    blank = np.zeros((rows, MODES), np.float32)
    parts = {}
    for name, table in (("hi", basis_hi), ("lo", basis_lo)):
        for side in range(2):
            spread = blank.copy().reshape(FREQ_CHANNELS // 8, 2, 8, MODES)
            spread[:, side] = table.astype(np.float32).reshape(FREQ_CHANNELS // 8, 8, MODES)
            parts[name, side] = spread.reshape(rows, MODES)
    fit = np.concatenate(
        [parts["hi", 0], parts["lo", 0], parts["hi", 1], parts["lo", 1]], axis=1
    ).T.astype(high)
    expand = np.concatenate(
        [parts["hi", 0], parts["hi", 0], parts["hi", 1], parts["hi", 1], parts["lo", 0], parts["lo", 1]],
        axis=1,
    ).astype(high)
    return fit, expand


def turn_trig(turns):
    quarter = jnp.floor(turns * 4.0 + 0.5)
    angle = (turns - 0.25 * quarter) * (2.0 * math.pi)
    square = angle * angle
    sine = angle * (
        1.0
        + square
        * (-1.0 / 6 + square * (1.0 / 120 + square * (-1.0 / 5040 + square * (1.0 / 362880))))
    )
    cosine = 1.0 + square * (
        -0.5
        + square
        * (1.0 / 24 + square * (-1.0 / 720 + square * (1.0 / 40320 + square * (-1.0 / 3628800))))
    )
    phase = quarter - 4.0 * jnp.floor(quarter * 0.25)
    odd = (phase == 1.0) | (phase == 3.0)
    cos_out = jnp.where(odd, sine, cosine)
    sin_out = jnp.where(odd, cosine, sine)
    cos_out = jnp.where((phase == 1.0) | (phase == 2.0), -cos_out, cos_out)
    sin_out = jnp.where(phase >= 2.0, -sin_out, sin_out)
    return cos_out, sin_out


def pack_kernel(wide, base, source, centre, target, held, tail, flux, in_sems, out_sems, flux_sem):
    chan = centre.shape[0]
    bring = [
        pltpu.make_async_copy(
            source.at[:, pl.ds(peer * base, base)], held.at[peer], in_sems.at[peer]
        )
        for peer in range(wide)
    ]
    send = [
        pltpu.make_async_copy(held.at[peer], target.at[peer, :, pl.ds(0, base)], out_sems.at[peer])
        for peer in range(wide)
    ]
    send_tail = [
        pltpu.make_async_copy(tail, target.at[peer, :, pl.ds(base, LANES)], out_sems.at[wide + peer])
        for peer in range(wide)
    ]
    fetch = pltpu.make_async_copy(centre, flux, flux_sem)
    fetch.start()
    for copy in bring:
        copy.start()
    fetch.wait()
    row = lax.broadcasted_iota(jnp.int32, (2 * chan, LANES), 0)
    lane = lax.broadcasted_iota(jnp.int32, (2 * chan, LANES), 1)
    value = jnp.zeros(row.shape, F32)
    for c in range(chan):
        value = jnp.where(row == c, flux[c], value)
    high = value.astype(BF16).astype(F32)
    middle = (value - high).astype(BF16).astype(F32)
    low = value - high - middle
    parts = jnp.where(lane == 0, high, jnp.where(lane == 1, middle, jnp.where(lane == 2, low, 0.0)))
    tail[...] = parts.astype(BF16)
    for copy in send_tail:
        copy.start()
    for came, copy in zip(bring, send):
        came.wait()
        copy.start()
    for copy in send + send_tail:
        copy.wait()


def predict_kernel(
    groups,
    tiles,
    padded,
    order,
    xy,
    lm,
    flux,
    real_out,
    imag_out,
    real,
    imag,
    pos_x,
    pos_y,
    row_c,
    row_s,
    row_dc,
    row_ds,
    col_c,
    col_s,
    col_dc,
    col_ds,
    left_a,
    right_a,
    left_b,
    right_b,
):
    comps = lm.shape[1]
    rank = lax.axis_index("wide")
    first_row = rank * (2 * tiles)
    last_row = first_row + (2 * tiles - 1)
    col_a = row_groups_of(first_row, groups)[1] * GROUP
    col_b = row_groups_of(last_row, groups)[1] * GROUP
    edge = jnp.minimum((((first_row >> 6) + 1) * GROUP - first_row) >> 1, tiles)
    pos_x[...] = jnp.zeros_like(pos_x)
    pos_y[...] = jnp.zeros_like(pos_y)

    def place(slot, position):
        station = order[position]
        pos_x[pl.ds(slot, 1), :] = jnp.full((1, LANES), xy[0, station], F32)
        pos_y[pl.ds(slot, 1), :] = jnp.full((1, LANES), xy[1, station], F32)

    def place_row(t, carry):
        for half in range(2):
            row = first_row + 2 * t + half
            place(half * padded + t, row_groups_of(row, groups)[0] * GROUP + (row & 63))
        return carry

    def place_col(j, carry):
        place(2 * padded + j, col_a + j)
        place(2 * padded + GROUP + j, col_b + j)
        return carry

    lax.fori_loop(0, tiles, place_row, 0, unroll=2)
    lax.fori_loop(0, GROUP, place_col, 0, unroll=4)
    step = 0.25 / FREQ_CHANNELS
    rows = 2 * padded
    weight = flux[...] * (1.0 / math.sqrt(comps))
    for k in range(0, comps, LANES):
        lane = slice(k, k + LANES)
        axis_l = lm[0:1, lane]
        axis_m = lm[1:2, lane]
        turns = pos_x[0:rows, :] * axis_l + pos_y[0:rows, :] * axis_m
        cosine, sine = turn_trig(turns)
        row_c[:, lane] = cosine * weight[:, lane]
        row_s[:, lane] = sine * weight[:, lane]
        row_dc[:, lane], row_ds[:, lane] = turn_trig(turns * step)
        turns = (
            pos_x[rows : rows + LANES, :] * axis_l + pos_y[rows : rows + LANES, :] * axis_m
        ).T
        col_c[lane, :], col_s[lane, :] = turn_trig(turns)
        col_dc[lane, :], col_ds[lane, :] = turn_trig(turns * step)

    def fill_col(right, k):
        part = slice(k, k + 16)
        c, s, dc, ds = col_c[part, :], col_s[part, :], col_dc[part, :], col_ds[part, :]
        for u in range(UNROLL):
            right[u, part, :] = c.astype(BF16)
            right[u, comps + k : comps + k + 16, :] = s.astype(BF16)
            c, s = c * dc - s * ds, s * dc + c * ds
        col_c[part, :], col_s[part, :] = c, s

    def fill_row(left, r, k):
        part, low = slice(r, r + 16), slice(rows + r, rows + r + 16)
        lane, high = slice(k, k + LANES), slice(comps + k, comps + k + LANES)
        c, s, dc, ds = row_c[part, lane], row_s[part, lane], row_dc[part, lane], row_ds[part, lane]
        for u in range(UNROLL):
            c16, s16 = c.astype(BF16), s.astype(BF16)
            left[u, part, lane] = c16
            left[u, part, high] = s16
            left[u, low, lane] = s16
            left[u, low, high] = -c16
            c, s = c * dc - s * ds, s * dc + c * ds
        row_c[part, lane], row_s[part, lane] = c, s

    def fill_steps(left, right):
        steps = [lambda k=k: fill_col(right, k) for k in range(0, comps, 16)]
        return steps + [
            lambda r=r, k=k: fill_row(left, r, k)
            for r in range(0, rows, 16)
            for k in range(0, comps, LANES)
        ]

    first_half = lax.broadcasted_iota(jnp.int32, (padded, LANES), 1) < GROUP
    in_a = lax.broadcasted_iota(jnp.int32, (padded, LANES), 0) < edge

    def multiply(left, right, group, u):
        product = jnp.dot(left[u], right[u], preferred_element_type=F32)
        channel = group * UNROLL + u
        for side, out in ((0, real), (1, imag)):
            even = product[side * rows : side * rows + padded]
            odd = product[side * rows + padded : side * rows + 2 * padded]
            even = jnp.where(in_a, even, pltpu.roll(even, GROUP, 1))
            odd = jnp.where(in_a, pltpu.roll(odd, GROUP, 1), odd)
            out[pl.ds(channel, padded, stride=FREQ_CHANNELS), :] = jnp.where(first_half, even, odd)

    for step in fill_steps(left_a, right_a):
        step()

    def group_pass(now, later, group):
        steps = fill_steps(*later)
        share = -(-len(steps) // UNROLL)
        for u in range(UNROLL):
            multiply(*now, group, u)
            for step in steps[u * share : (u + 1) * share]:
                step()

    def two_groups(pair, carry):
        group_pass((left_a, right_a), (left_b, right_b), 2 * pair)
        group_pass((left_b, right_b), (left_a, right_a), 2 * pair + 1)
        return carry

    lax.fori_loop(0, FREQ_CHANNELS // (2 * UNROLL), two_groups, 0)
    size = tiles * FREQ_CHANNELS
    real_out[...] = real[0:size, :]
    imag_out[...] = imag[0:size, :].astype(BF16)


def coefficients(fit, block):
    raw = jnp.dot(fit, block, preferred_element_type=F32)
    return raw[0:16] + raw[16:32], raw[32:48] + raw[48:64]


def tile_weights(groups, tiles, first_row, t, kept):
    lane = lax.broadcasted_iota(jnp.int32, (1, LANES), 1)
    row = first_row + 2 * t
    first, second = row_groups_of(row, groups)
    inside = (row & 63) + (lane >> 6)
    usable = (first != second) | (inside < (lane & 63))
    mask = kept[pl.ds((first_row >> 1) + t, 1), :].astype(F32)
    return jnp.where(usable, mask, 0.0)


def stats_kernel(
    groups, tiles, observed, real, imag, kept, counts, fit, stats, model, model_modes, data_modes, shift
):
    rank = lax.axis_index("wide")
    first_row = rank * (2 * tiles)
    mode = lax.broadcasted_iota(jnp.int32, (MODES, LANES), 0)
    tail = observed[:, :, tiles * LANES : (tiles + 1) * LANES].reshape(256, LANES).astype(F32)
    tail = tail.reshape(FREQ_CHANNELS // 8, 2, 8, LANES)[:, 0].reshape(FREQ_CHANNELS, LANES)
    shift[...] = jnp.broadcast_to(jnp.sum(tail, axis=1, keepdims=True), tail.shape)

    def one(t):
        data = observed[:, :, pl.ds(pl.multiple_of(t * LANES, LANES), LANES)].reshape(256, LANES)
        part = pl.ds(pl.multiple_of(t * 256, 256), 256)
        half = pl.ds(pl.multiple_of(t * FREQ_CHANNELS, FREQ_CHANNELS), FREQ_CHANNELS)
        sides = [real[half, :] + shift[...], imag[half, :].astype(F32)]
        sides = [side.reshape(FREQ_CHANNELS // 8, 1, 8, LANES) for side in sides]
        block = jnp.concatenate(sides, axis=1).reshape(256, LANES).astype(BF16)
        model[part, :] = block
        data_parts = data.astype(F32).reshape(FREQ_CHANNELS // 8, 2, 8, LANES)
        mod_parts = block.astype(F32).reshape(FREQ_CHANNELS // 8, 2, 8, LANES)
        obs_re, obs_im = data_parts[:, 0], data_parts[:, 1]
        mod_re, mod_im = mod_parts[:, 0], mod_parts[:, 1]

        def total(terms):
            return jnp.sum(jnp.sum(terms, axis=0), axis=0, keepdims=True)

        cross_re = total(obs_re * mod_re + obs_im * mod_im)
        cross_im = total(obs_im * mod_re - obs_re * mod_im)
        power = total(mod_re * mod_re + mod_im * mod_im)
        v_re, v_im = coefficients(fit[...], data)
        m_re, m_im = coefficients(fit[...], block)
        part32 = pl.ds(pl.multiple_of(t * 32, 32), 32)
        data_modes[part32, :] = jnp.concatenate([v_re, v_im])
        model_modes[part32, :] = jnp.concatenate([m_re, m_im])
        inside = (mode < counts[pl.ds(t, 1), :]).astype(F32)
        vv = jnp.sum(inside * (v_re * v_re + v_im * v_im), axis=0, keepdims=True)
        vm_re = jnp.sum(inside * (v_re * m_re + v_im * m_im), axis=0, keepdims=True)
        vm_im = jnp.sum(inside * (v_im * m_re - v_re * m_im), axis=0, keepdims=True)
        mm = jnp.sum(inside * (m_re * m_re + m_im * m_im), axis=0, keepdims=True)
        weight = tile_weights(groups, tiles, first_row, t, kept)
        rows = jnp.concatenate(
            [cross_re, cross_im, vv, vm_re, vm_im, power, mm, jnp.zeros((1, LANES), F32)]
        )
        return rows * weight

    def two(pair, carry):
        stats[pl.ds(pl.multiple_of(pair * 16, 16), 16), :] = jnp.concatenate(
            [one(2 * pair), one(2 * pair + 1)]
        ).astype(BF16)
        return carry

    lax.fori_loop(0, tiles // 2, two, 0, unroll=5)


def split_rows(values):
    row = lax.broadcasted_iota(jnp.int32, (16, values[0].shape[1]), 0)
    out = jnp.zeros(row.shape, F32)
    for at, value in enumerate(values):
        high = value.astype(BF16).astype(F32)
        out = jnp.where(row == 2 * at, high, out)
        out = jnp.where(row == 2 * at + 1, value - high, out)
    return out.astype(BF16)


def solve_kernel(
    groups,
    tiles,
    wide,
    gathered,
    observed,
    model,
    model_modes,
    data_modes,
    kept,
    counts,
    order,
    expand,
    gains,
    residual,
    flat,
    upper,
    full,
    state,
    weights,
    row_gain_re,
    row_gain_im,
    col_gain_re,
    col_gain_im,
):
    stations = groups * GROUP
    rank = lax.axis_index("wide")
    first_row = rank * (2 * tiles)
    chunk = 8 * tiles
    for k, flip in enumerate(gather_order(wide)):
        owner = rank ^ flip
        flat[pl.ds(pl.multiple_of(owner * chunk, 16), chunk), :] = gathered[k].astype(F32)
    halves = stations // LANES
    lane32 = lax.broadcasted_iota(jnp.int32, (32, LANES), 1) < GROUP
    block_id = {}
    for first in range(groups):
        for second in range(first, groups):
            block_id[first, second] = len(block_id)
    for stat in range(STATS):
        for first in range(groups):
            for half in range(halves):
                pair = []
                for side in range(2):
                    index = block_id.get((first, 2 * half + side))
                    pair.append(
                        jnp.zeros((32, LANES), F32)
                        if index is None
                        else flat[pl.ds(256 * index + stat, 32, stride=8), :]
                    )
                if block_id.get((first, 2 * half + 1)) is None:
                    continue
                even = jnp.where(lane32, pair[0], pltpu.roll(pair[1], GROUP, 1))
                odd = jnp.where(lane32, pltpu.roll(pair[0], GROUP, 1), pair[1])
                upper[half, pl.ds(GROUP * first, 32, stride=2), :] = even
                upper[half, pl.ds(GROUP * first + 1, 32, stride=2), :] = odd
        sign = -1.0 if stat in (1, 4) else 1.0
        for a in range(halves):
            rows_a = slice(LANES * a, LANES * (a + 1))
            for b in range(a, halves):
                rows_b = slice(LANES * b, LANES * (b + 1))
                block = upper[b, rows_a, :]
                turned = block.T * sign
                if a == b:
                    full[stat, rows_a, rows_a] = block + turned
                else:
                    full[stat, rows_a, rows_b] = block
                    full[stat, rows_b, rows_a] = turned

    def put_weights(part, chunk_rows, value):
        weights[chunk_rows, part * stations : (part + 1) * stations] = value.astype(BF16)

    gain_re = jnp.ones((1, stations), F32)
    gain_im = jnp.zeros((1, stations), F32)
    for round_id in range(ROUNDS):

        def build(step, carry):
            rows = pl.ds(pl.multiple_of(step * 16, 16), 16)
            cross_re, cross_im, power = full[0, rows, :], full[1, rows, :], full[5, rows, :]
            if round_id:
                vv, vm_re, vm_im, mm = (full[i, rows, :] for i in (2, 3, 4, 6))
                col_re = jnp.concatenate([col_gain_re[rows, round_id - 1, :]] * halves, axis=1)
                col_im = jnp.concatenate([col_gain_im[rows, round_id - 1, :]] * halves, axis=1)
                rest_re = 1.0 - (col_re * gain_re + col_im * gain_im)
                rest_im = -(col_im * gain_re - col_re * gain_im)
                if round_id == 1:
                    a_re, a_im = jnp.ones_like(rest_re), jnp.zeros_like(rest_re)
                    b_re, b_im = rest_re, rest_im
                else:
                    a_re, a_im, b_re, b_im = (state[i, rows, :] for i in range(4))
                    a_re, a_im = 1.0 + rest_re * a_re - rest_im * a_im, rest_re * a_im + rest_im * a_re
                    b_re, b_im = rest_re * b_re - rest_im * b_im, rest_re * b_im + rest_im * b_re
                if round_id + 1 < ROUNDS:
                    for i, value in enumerate((a_re, a_im, b_re, b_im)):
                        state[i, rows, :] = value
                turn_re = b_re - 1.0
                cross_re = cross_re + a_re * vv + turn_re * vm_re + b_im * vm_im
                cross_im = cross_im - a_im * vv + turn_re * vm_im - b_im * vm_re
                mix_re = a_re * b_re + a_im * b_im
                mix_im = a_im * b_re - a_re * b_im
                power = (
                    power
                    + (a_re * a_re + a_im * a_im) * vv
                    + (b_re * b_re + b_im * b_im - 1.0) * mm
                    + 2.0 * (mix_re * vm_re - mix_im * vm_im)
                )
            put_weights(0, rows, cross_re)
            put_weights(1, rows, cross_im)
            put_weights(2, rows, power)
            return carry

        lax.fori_loop(0, stations // 16, build, 0, unroll=4)
        for iteration in range(CAL_ITERS):
            left = split_rows([gain_re, gain_im, gain_re * gain_re + gain_im * gain_im])
            raw = jnp.dot(left, weights[...], preferred_element_type=F32)

            def product(vector, part):
                at = slice(part * stations, (part + 1) * stations)
                return raw[2 * vector : 2 * vector + 1, at] + raw[2 * vector + 1 : 2 * vector + 2, at]

            below = product(2, 2)
            next_re = (product(0, 0) + product(1, 1)) / below
            next_im = (product(1, 0) - product(0, 1)) / below
            if iteration % 2 == 1:
                next_re = 0.5 * (next_re + gain_re)
                next_im = 0.5 * (next_im + gain_im)
            gain_re, gain_im = next_re, next_im
        lane1 = lax.broadcasted_iota(jnp.int32, (1, LANES), 1) < GROUP
        for value, row_gain, col_gain in (
            (gain_re, row_gain_re, col_gain_re),
            (gain_im, row_gain_im, col_gain_im),
        ):
            for half in range(halves):
                part = value[:, LANES * half : LANES * (half + 1)]
                turned = pltpu.roll(jnp.broadcast_to(part, (8, LANES)), GROUP, 1)[0:1]
                row_gain[2 * half, round_id : round_id + 1, :] = jnp.where(lane1, part, turned)
                row_gain[2 * half + 1, round_id : round_id + 1, :] = jnp.where(lane1, turned, part)
                col_gain[LANES * half : LANES * (half + 1), round_id, :] = jnp.broadcast_to(
                    part, (LANES, LANES)
                ).T

    hot = (
        lax.broadcasted_iota(jnp.int32, (stations, stations), 0) == order[...]
    ).astype(BF16)
    pieces = []
    for value in (gain_re, gain_im):
        high = value.astype(BF16).astype(F32)
        middle = (value - high).astype(BF16).astype(F32)
        pieces += [high, middle, value - high - middle]
    row16 = lax.broadcasted_iota(jnp.int32, (16, stations), 0)
    left = jnp.zeros((16, stations), F32)
    for at, piece in enumerate(pieces):
        left = jnp.where(row16 == at, piece, left)
    spread = lax.dot_general(
        left.astype(BF16), hot, (((1,), (1,)), ((), ())), preferred_element_type=F32
    )
    gains[0:1, :] = spread[0:1] + spread[1:2] + spread[2:3]
    gains[1:2, :] = spread[3:4] + spread[4:5] + spread[5:6]

    mode = lax.broadcasted_iota(jnp.int32, (MODES, LANES), 0)
    lane8 = lax.broadcasted_iota(jnp.int32, (8, LANES), 1) < GROUP

    def tile(t, carry):
        row = first_row + 2 * t
        first, second = row_groups_of(row, groups)
        station = first * GROUP + (row & 63)
        p_re = jnp.where(lane8, col_gain_re[station], col_gain_re[station + 1])
        p_im = jnp.where(lane8, col_gain_im[station], col_gain_im[station + 1])
        q_re, q_im = row_gain_re[second], row_gain_im[second]
        prod_re = p_re * q_re + p_im * q_im
        prod_im = p_im * q_re - p_re * q_im
        a_re, a_im = jnp.zeros((1, LANES), F32), jnp.zeros((1, LANES), F32)
        b_re, b_im = jnp.ones((1, LANES), F32), jnp.zeros((1, LANES), F32)
        for round_id in range(ROUNDS - 1):
            rest_re = 1.0 - prod_re[round_id : round_id + 1]
            rest_im = -prod_im[round_id : round_id + 1]
            a_re, a_im = 1.0 + rest_re * a_re - rest_im * a_im, rest_re * a_im + rest_im * a_re
            b_re, b_im = rest_re * b_re - rest_im * b_im, rest_re * b_im + rest_im * b_re
        b_re = b_re - 1.0
        inside = (mode < counts[pl.ds(t, 1), :]).astype(F32)
        part32 = pl.ds(pl.multiple_of(t * 32, 32), 32)
        v_re, v_im = data_modes[part32, :][0:16], data_modes[part32, :][16:32]
        m_re, m_im = model_modes[part32, :][0:16], model_modes[part32, :][16:32]
        f_re = inside * (a_re * v_re - a_im * v_im + b_re * m_re - b_im * m_im)
        f_im = inside * (a_re * v_im + a_im * v_re + b_re * m_im + b_im * m_re)
        f_re16, f_im16 = f_re.astype(BF16), f_im.astype(BF16)
        stack = jnp.concatenate(
            [
                f_re16,
                (f_re - f_re16.astype(F32)).astype(BF16),
                f_im16,
                (f_im - f_im16.astype(F32)).astype(BF16),
                f_re16,
                f_im16,
            ]
        )
        fitted = jnp.dot(expand[...], stack, preferred_element_type=F32)
        current = model[pl.ds(pl.multiple_of(t * 256, 256), 256), :].astype(F32) + fitted
        current = current.reshape(FREQ_CHANNELS // 8, 2, 8, LANES)
        lanes = pl.ds(pl.multiple_of(t * LANES, LANES), LANES)
        data = (
            observed[:, :, lanes]
            .reshape(256, LANES)
            .astype(F32)
            .reshape(FREQ_CHANNELS // 8, 2, 8, LANES)
        )
        weight = tile_weights(groups, tiles, first_row, t, kept)
        last_re, last_im = prod_re[ROUNDS - 1 : ROUNDS], prod_im[ROUNDS - 1 : ROUNDS]
        mod_re, mod_im = current[:, 0], current[:, 1]
        left_re = weight * (data[:, 0] - (last_re * mod_re - last_im * mod_im))
        left_im = weight * (data[:, 1] - (last_re * mod_im + last_im * mod_re))
        residual[0, 0, :, lanes] = left_re.reshape(FREQ_CHANNELS, LANES).astype(BF16)
        residual[1, 0, :, lanes] = left_im.reshape(FREQ_CHANNELS, LANES).astype(BF16)
        return carry

    lax.fori_loop(0, tiles, tile, 0, unroll=5)


def call(kernel, out_shape, scratch, name, in_spaces, mib, flops=0, moved=0):
    return pl.pallas_call(
        kernel,
        out_shape=out_shape,
        in_specs=[pl.BlockSpec(memory_space=space) for space in in_spaces],
        out_specs=jax.tree.map(lambda _: pl.BlockSpec(memory_space=VMEM), out_shape),
        scratch_shapes=scratch,
        compiler_params=pltpu.CompilerParams(vmem_limit_bytes=mib << 20),
        cost_estimate=pl.CostEstimate(flops=flops, bytes_accessed=moved, transcendentals=0),
        name=name,
    )


def exchange(block, distance, wide):
    return lax.ppermute(block, "wide", [(i, i ^ distance) for i in range(wide)])


def gather_order(wide):
    order = [0, wide // 2, 3 * wide // 4, wide // 4]
    distance = wide // 8
    while distance:
        order += [place ^ distance for place in order]
        distance //= 2
    return order


def gather_stats(stats, wide):
    held = jnp.stack([stats] + [exchange(stats, flip, wide) for flip in gather_order(wide)[1:4]])
    distance = wide // 8
    while distance:
        held = jnp.concatenate([held, exchange(held, distance, wide)])
        distance //= 2
    return held


def body(
    visibilities,
    kept_baseline_mask,
    fitted_mode_count,
    station_order,
    station_xy,
    comp_lm,
    comp_flux,
    centre_flux,
):
    wide = lax.axis_size("wide")
    local_chan = visibilities.shape[2]
    total = visibilities.shape[3]
    base = total // wide
    tiles = base // LANES
    padded = -(-tiles // 8) * 8
    stations = station_order.shape[0]
    groups = stations // GROUP
    comps = comp_lm.shape[1]
    rows = 2 * padded
    fit, expand = (jnp.asarray(table) for table in basis_tables())
    kept = kept_baseline_mask.reshape(total // LANES, LANES)
    counts = fitted_mode_count.reshape(tiles, LANES)

    packed = pl.pallas_call(
        lambda *refs: pack_kernel(wide, base, *refs),
        out_shape=jax.ShapeDtypeStruct((wide, 2 * local_chan, base + LANES), BF16),
        in_specs=[pl.BlockSpec(memory_space=pltpu.MemorySpace.HBM)] * 2,
        out_specs=pl.BlockSpec(memory_space=pltpu.MemorySpace.HBM),
        scratch_shapes=[
            pltpu.VMEM((wide, 2 * local_chan, base), BF16),
            pltpu.VMEM((2 * local_chan, LANES), BF16),
            pltpu.SMEM((local_chan,), F32),
            pltpu.SemaphoreType.DMA((wide,)),
            pltpu.SemaphoreType.DMA((2 * wide,)),
            pltpu.SemaphoreType.DMA,
        ],
        compiler_params=pltpu.CompilerParams(vmem_limit_bytes=60 << 20),
        name="pack",
    )(visibilities.reshape(2 * local_chan, total), centre_flux)
    observed = lax.all_to_all(packed, "wide", 0, 0, tiled=True)
    if local_chan != 8:
        pairs = 8 // local_chan
        observed = observed.reshape(wide // pairs, pairs, 2, local_chan, base + LANES)
        observed = observed.transpose(0, 2, 1, 3, 4).reshape(wide // pairs, 16, base + LANES)

    state_row = pltpu.VMEM((rows, comps), F32)
    state_col = pltpu.VMEM((comps, LANES), F32)
    left = pltpu.VMEM((UNROLL, 2 * rows, 2 * comps), BF16)
    right = pltpu.VMEM((UNROLL, 2 * comps, LANES), BF16)
    real, imag = call(
        lambda *refs: predict_kernel(groups, tiles, padded, *refs),
        (
            jax.ShapeDtypeStruct((tiles * FREQ_CHANNELS, LANES), F32),
            jax.ShapeDtypeStruct((tiles * FREQ_CHANNELS, LANES), BF16),
        ),
        [pltpu.VMEM((padded * FREQ_CHANNELS, LANES), F32)] * 2
        + [pltpu.VMEM((rows + LANES, LANES), F32)] * 2
        + [state_row] * 4
        + [state_col] * 4
        + [left, right, left, right],
        "predict",
        [SMEM, SMEM, VMEM, VMEM],
        20,
        FREQ_CHANNELS * 2 * 2 * rows * 2 * comps * 256,
        padded * 256 * LANES * 4,
    )(station_order, station_xy.reshape(2, stations), comp_lm, comp_flux.reshape(1, comps))
    stats, model, model_modes, data_modes = call(
        lambda *refs: stats_kernel(groups, tiles, *refs),
        (
            jax.ShapeDtypeStruct((tiles * 8, LANES), BF16),
            jax.ShapeDtypeStruct((tiles * 256, LANES), BF16),
            jax.ShapeDtypeStruct((tiles * 32, LANES), F32),
            jax.ShapeDtypeStruct((tiles * 32, LANES), F32),
        ),
        [pltpu.VMEM((FREQ_CHANNELS, LANES), F32)],
        "stats",
        [VMEM] * 6,
        12,
        moved=tiles * 256 * LANES * 8,
    )(observed, real, imag, kept, counts, fit)
    gathered = gather_stats(stats, wide)
    gains, residual = call(
        lambda *refs: solve_kernel(groups, tiles, wide, *refs),
        (
            jax.ShapeDtypeStruct((2, stations), F32),
            jax.ShapeDtypeStruct((2, 1, FREQ_CHANNELS, base), BF16),
        ),
        [
            pltpu.VMEM((wide * tiles * 8, LANES), F32),
            pltpu.VMEM((stations // LANES, stations, LANES), F32),
            pltpu.VMEM((STATS, stations, stations), F32),
            pltpu.VMEM((4, stations, stations), F32),
            pltpu.VMEM((stations, 3 * stations), BF16),
            pltpu.VMEM((groups, 8, LANES), F32),
            pltpu.VMEM((groups, 8, LANES), F32),
            pltpu.VMEM((stations, 8, LANES), F32),
            pltpu.VMEM((stations, 8, LANES), F32),
        ],
        "solve",
        [VMEM] * 9,
        16,
        moved=tiles * 256 * LANES * 6,
    )(
        gathered,
        observed,
        model,
        model_modes,
        data_modes,
        kept,
        counts,
        station_order.reshape(1, stations),
        expand,
    )
    return gains, residual


def solution(mesh):
    placed = (
        P(None, None, ("band", "wide"), None),
        P("band"),
        P("wide"),
        P(),
        P(),
        P(),
        P(),
        P(("band", "wide")),
    )
    return jax.shard_map(
        body,
        mesh=mesh,
        in_specs=placed,
        out_specs=(P(None, "band"), P(None, None, "band", "wide")),
        check_vma=False,
    )
```

```python
import math

import jax
import jax.numpy as jnp
import numpy as np
from jax import lax
from jax.experimental import pallas as pl
from jax.experimental.pallas import tpu as pltpu
from jax.sharding import PartitionSpec as P

GROUP = 64
FREQ_CHANNELS = 128
MODES = 16
CAL_ITERS = 3
ROUNDS = 3
STATS = 7
LANES = 128
UNROLL = 4
PACK_PARTS = 4
VMEM = pltpu.MemorySpace.VMEM
SMEM = pltpu.MemorySpace.SMEM
F32 = jnp.float32
BF16 = jnp.bfloat16


def row_groups_of(row, groups):
    block = row >> 6
    first = jnp.zeros_like(block)
    start = jnp.zeros_like(block)
    edge = 0
    for group in range(1, groups):
        edge += groups - group + 1
        past = (block >= edge).astype(jnp.int32)
        first = first + past
        start = start + past * (groups - group + 1)
    return first, block - start + first


def basis_tables():
    mid = np.arange(FREQ_CHANNELS)[:, None] + 0.5
    order = np.arange(MODES)[None, :]
    scale = np.where(order == 0, math.sqrt(1.0 / FREQ_CHANNELS), math.sqrt(2.0 / FREQ_CHANNELS))
    basis = (scale * np.cos(math.pi / FREQ_CHANNELS * mid * order)).astype(np.float32)
    high = basis.astype(BF16)
    low = (basis - high.astype(np.float32)).astype(BF16)
    return np.concatenate([high, low], axis=1).T, np.concatenate([high, high, low], axis=1)


def output_parts(tiles):
    return 4 if tiles % 4 == 0 else 2


def stat_groups(tiles):
    return -(-tiles * STATS // 8)


def turn_trig(turns):
    quarter = jnp.floor(turns * 4.0 + 0.5)
    angle = (turns - 0.25 * quarter) * (2.0 * math.pi)
    square = angle * angle
    sine = angle * (
        1.0
        + square
        * (-1.0 / 6 + square * (1.0 / 120 + square * (-1.0 / 5040 + square * (1.0 / 362880))))
    )
    cosine = 1.0 + square * (
        -0.5
        + square
        * (1.0 / 24 + square * (-1.0 / 720 + square * (1.0 / 40320 + square * (-1.0 / 3628800))))
    )
    phase = quarter - 4.0 * jnp.floor(quarter * 0.25)
    odd = (phase == 1.0) | (phase == 3.0)
    cos_out = jnp.where(odd, sine, cosine)
    sin_out = jnp.where(odd, cosine, sine)
    cos_out = jnp.where((phase == 1.0) | (phase == 2.0), -cos_out, cos_out)
    sin_out = jnp.where(phase >= 2.0, -sin_out, sin_out)
    return cos_out, sin_out


def pack_kernel(wide, base, source, centre, target, held, flux, in_sems, out_sems, flux_sem):
    chan = centre.shape[0]
    share = wide // PACK_PARTS
    peers = [pl.ds(part * share, share) for part in range(PACK_PARTS)]
    bring = [
        [
            pltpu.make_async_copy(
                source.at[side, peers[part]],
                held.at[peers[part], :, pl.ds(side * base, base)],
                in_sems.at[part, side],
            )
            for side in range(2)
        ]
        for part in range(PACK_PARTS)
    ]
    send = [
        pltpu.make_async_copy(held.at[peers[part]], target.at[peers[part]], out_sems.at[part])
        for part in range(PACK_PARTS)
    ]
    fetch = pltpu.make_async_copy(centre, flux, flux_sem)
    fetch.start()
    for pair in bring:
        for copy in pair:
            copy.start()
    fetch.wait()
    row = lax.broadcasted_iota(jnp.int32, (chan, LANES), 0)
    lane = lax.broadcasted_iota(jnp.int32, (chan, LANES), 1)
    value = jnp.zeros(row.shape, F32)
    for c in range(chan):
        value = jnp.where(row == c, flux[c], value)
    high = value.astype(BF16).astype(F32)
    middle = (value - high).astype(BF16).astype(F32)
    low = value - high - middle
    parts = jnp.where(lane == 0, high, jnp.where(lane == 1, middle, jnp.where(lane == 2, low, 0.0)))
    held[:, :, 2 * base : 2 * base + LANES] = jnp.broadcast_to(
        parts.astype(BF16)[None], (wide, chan, LANES)
    )
    for pair, copy in zip(bring, send):
        for came in pair:
            came.wait()
        copy.start()
    for copy in send:
        copy.wait()


def predict_kernel(
    groups,
    tiles,
    padded,
    order,
    xy,
    lm,
    flux,
    real_out,
    imag_out,
    real,
    imag,
    pos_x,
    pos_y,
    row_c,
    row_s,
    row_dc,
    row_ds,
    col_c,
    col_s,
    col_dc,
    col_ds,
    left_a,
    right_a,
    left_b,
    right_b,
):
    comps = lm.shape[1]
    rank = lax.axis_index("wide")
    first_row = rank * (2 * tiles)
    last_row = first_row + (2 * tiles - 1)
    col_a = row_groups_of(first_row, groups)[1] * GROUP
    col_b = row_groups_of(last_row, groups)[1] * GROUP
    edge = jnp.minimum((((first_row >> 6) + 1) * GROUP - first_row) >> 1, tiles)
    pos_x[...] = jnp.zeros_like(pos_x)
    pos_y[...] = jnp.zeros_like(pos_y)

    def place(slot, position):
        station = order[position]
        pos_x[pl.ds(slot, 1), :] = jnp.full((1, LANES), xy[0, station], F32)
        pos_y[pl.ds(slot, 1), :] = jnp.full((1, LANES), xy[1, station], F32)

    def place_row(t, carry):
        for half in range(2):
            row = first_row + 2 * t + half
            place(half * padded + t, row_groups_of(row, groups)[0] * GROUP + (row & 63))
        return carry

    def place_col(j, carry):
        place(2 * padded + j, col_a + j)
        place(2 * padded + GROUP + j, col_b + j)
        return carry

    lax.fori_loop(0, tiles, place_row, 0, unroll=2)
    lax.fori_loop(0, GROUP, place_col, 0, unroll=4)
    step = 0.25 / FREQ_CHANNELS
    rows = 2 * padded
    weight = flux[...] * (1.0 / math.sqrt(comps))
    for k in range(0, comps, LANES):
        lane = slice(k, k + LANES)
        axis_l = lm[0:1, lane]
        axis_m = lm[1:2, lane]
        turns = pos_x[0:rows, :] * axis_l + pos_y[0:rows, :] * axis_m
        cosine, sine = turn_trig(turns)
        row_c[:, lane] = cosine * weight[:, lane]
        row_s[:, lane] = sine * weight[:, lane]
        row_dc[:, lane], row_ds[:, lane] = turn_trig(turns * step)
        turns = (
            pos_x[rows : rows + LANES, :] * axis_l + pos_y[rows : rows + LANES, :] * axis_m
        ).T
        col_c[lane, :], col_s[lane, :] = turn_trig(turns)
        col_dc[lane, :], col_ds[lane, :] = turn_trig(turns * step)

    def fill_col(right, k):
        part = slice(k, k + 16)
        c, s, dc, ds = col_c[part, :], col_s[part, :], col_dc[part, :], col_ds[part, :]
        for u in range(UNROLL):
            right[u, part, 0:LANES] = c.astype(BF16)
            right[u, part, LANES : 2 * LANES] = s.astype(BF16)
            c, s = c * dc - s * ds, s * dc + c * ds
        col_c[part, :], col_s[part, :] = c, s

    def fill_row(left, r, k):
        part, low = slice(r, r + 16), slice(rows + r, rows + r + 16)
        lane = slice(k, k + LANES)
        c, s, dc, ds = row_c[part, lane], row_s[part, lane], row_dc[part, lane], row_ds[part, lane]
        for u in range(UNROLL):
            left[u, part, lane] = c.astype(BF16)
            left[u, low, lane] = s.astype(BF16)
            c, s = c * dc - s * ds, s * dc + c * ds
        row_c[part, lane], row_s[part, lane] = c, s

    def fill_steps(left, right):
        steps = [lambda k=k: fill_col(right, k) for k in range(0, comps, 16)]
        return steps + [
            lambda r=r, k=k: fill_row(left, r, k)
            for r in range(0, rows, 16)
            for k in range(0, comps, LANES)
        ]

    first_half = lax.broadcasted_iota(jnp.int32, (padded, LANES), 1) < GROUP
    in_a = lax.broadcasted_iota(jnp.int32, (padded, LANES), 0) < edge

    def multiply(left, right, group, u):
        product = jnp.dot(left[u], right[u], preferred_element_type=F32)
        channel = group * UNROLL + u
        with_cos, with_sin = product[:, 0:LANES], product[:, LANES : 2 * LANES]
        sums = (
            (with_cos[0:rows] + with_sin[rows : 2 * rows], real),
            (with_cos[rows : 2 * rows] - with_sin[0:rows], imag),
        )
        for side, out in sums:
            even, odd = side[0:padded], side[padded : 2 * padded]
            even = jnp.where(in_a, even, pltpu.roll(even, GROUP, 1))
            odd = jnp.where(in_a, pltpu.roll(odd, GROUP, 1), odd)
            out[pl.ds(channel, padded, stride=FREQ_CHANNELS), :] = jnp.where(first_half, even, odd)

    for step in fill_steps(left_a, right_a):
        step()

    def group_pass(now, later, group):
        steps = fill_steps(*later)
        share = -(-len(steps) // UNROLL)
        for u in range(UNROLL):
            multiply(*now, group, u)
            for step in steps[u * share : (u + 1) * share]:
                step()

    def two_groups(pair, carry):
        group_pass((left_a, right_a), (left_b, right_b), 2 * pair)
        group_pass((left_b, right_b), (left_a, right_a), 2 * pair + 1)
        return carry

    lax.fori_loop(0, FREQ_CHANNELS // (2 * UNROLL), two_groups, 0)
    size = tiles * FREQ_CHANNELS
    real_out[...] = real[0:size, :]
    imag_out[...] = imag[0:size, :].astype(BF16)


def tile_weights(groups, tiles, first_row, t, kept):
    lane = lax.broadcasted_iota(jnp.int32, (1, LANES), 1)
    row = first_row + 2 * t
    first, second = row_groups_of(row, groups)
    inside = (row & 63) + (lane >> 6)
    usable = (first != second) | (inside < (lane & 63))
    mask = kept[pl.ds((first_row >> 1) + t, 1), :].astype(F32)
    return jnp.where(usable, mask, 0.0)


def tile_lanes(t, size=LANES, offset=0):
    return pl.ds(pl.multiple_of(offset + t * size, size), size)


def data_sides(observed, tiles, t):
    return [
        observed[:, :, tile_lanes(t, LANES, side * tiles * LANES)]
        .astype(F32)
        .reshape(FREQ_CHANNELS, LANES)
        for side in range(2)
    ]


def stats_kernel(
    groups, tiles, observed, real, imag, kept, counts, fit, stats, model, modes, shift, rows
):
    rank = lax.axis_index("wide")
    first_row = rank * (2 * tiles)
    mode = lax.broadcasted_iota(jnp.int32, (MODES, LANES), 0)
    tail = observed[:, :, 2 * tiles * LANES : (2 * tiles + 1) * LANES].astype(F32)
    tail = tail.reshape(FREQ_CHANNELS, LANES)
    shift[...] = jnp.broadcast_to(jnp.sum(tail, axis=1, keepdims=True), tail.shape)

    def one(t, carry):
        obs_re, obs_im = data_sides(observed, tiles, t)
        half = tile_lanes(t, FREQ_CHANNELS)
        mod_re16, mod_im16 = (real[half, :] + shift[...]).astype(BF16), imag[half, :]
        both = pl.multiple_of(2 * t * FREQ_CHANNELS, FREQ_CHANNELS)
        model[pl.ds(both, FREQ_CHANNELS), :] = mod_re16
        model[pl.ds(both + FREQ_CHANNELS, FREQ_CHANNELS), :] = mod_im16
        mod_re, mod_im = mod_re16.astype(F32), mod_im16.astype(F32)

        def total(terms):
            return jnp.sum(terms, axis=0, keepdims=True)

        cross_re = total(obs_re * mod_re + obs_im * mod_im)
        cross_im = total(obs_im * mod_re - obs_re * mod_im)
        power = total(mod_re * mod_re + mod_im * mod_im)
        sides = [obs_re.astype(BF16), obs_im.astype(BF16), mod_re16, mod_im16]
        raw = jnp.dot(fit[...], jnp.concatenate(sides, axis=1), preferred_element_type=F32)
        raw = raw[0:MODES] + raw[MODES : 2 * MODES]
        modes[tile_lanes(t, MODES), :] = raw
        v_re, v_im, m_re, m_im = (raw[:, LANES * i : LANES * (i + 1)] for i in range(4))
        inside = (mode < counts[pl.ds(t, 1), :]).astype(F32)
        vv = total(inside * (v_re * v_re + v_im * v_im))
        vm_re = total(inside * (v_re * m_re + v_im * m_im))
        vm_im = total(inside * (v_im * m_re - v_re * m_im))
        mm = total(inside * (m_re * m_re + m_im * m_im))
        weight = tile_weights(groups, tiles, first_row, t, kept)
        parts = [cross_re, cross_im, vv, vm_re, vm_im, power, mm, jnp.zeros((1, LANES), F32)]
        rows[tile_lanes(t, 8), :] = jnp.concatenate(parts) * weight
        return carry

    lax.fori_loop(0, tiles, one, 0, unroll=10)
    held = stat_groups(tiles)
    for extra in range(tiles - held):
        late = 8 * (held + extra)
        rows[pl.ds(7 + 8 * STATS * extra, STATS, stride=8), :] = rows[late : late + STATS, :]
    stats[...] = rows[0 : 8 * held, :].astype(BF16)


def solve_kernel(
    groups,
    tiles,
    wide,
    gathered,
    observed,
    model,
    modes,
    kept,
    counts,
    order,
    expand,
    gains,
    residual,
    flat,
    upper,
    full,
    weights,
    row_gain_re,
    row_gain_im,
    col_gain_re,
    col_gain_im,
    left_out,
    out_sems,
):
    stations = groups * GROUP
    rank = lax.axis_index("wide")
    first_row = rank * (2 * tiles)
    chunk = 8 * tiles
    held = stat_groups(tiles)
    for k, flip in enumerate(gather_order(wide)):
        start = pl.multiple_of((rank ^ flip) * chunk, 16)
        flat[pl.ds(start, 8 * held), :] = gathered[k].astype(F32)
        for extra in range(tiles - held):
            late = flat[pl.ds(start + (7 + 8 * STATS * extra), STATS, stride=8), :]
            flat[pl.ds(pl.multiple_of(start + 8 * (held + extra), 8), STATS), :] = late
    halves = stations // LANES
    lane32 = lax.broadcasted_iota(jnp.int32, (32, LANES), 1) < GROUP
    block_id = {}
    for first in range(groups):
        for second in range(first, groups):
            block_id[first, second] = len(block_id)
    for stat in range(STATS):
        for first in range(groups):
            for half in range(halves):
                pair = []
                for side in range(2):
                    index = block_id.get((first, 2 * half + side))
                    pair.append(
                        jnp.zeros((32, LANES), F32)
                        if index is None
                        else flat[pl.ds(256 * index + stat, 32, stride=8), :]
                    )
                if block_id.get((first, 2 * half + 1)) is None:
                    continue
                even = jnp.where(lane32, pair[0], pltpu.roll(pair[1], GROUP, 1))
                odd = jnp.where(lane32, pltpu.roll(pair[0], GROUP, 1), pair[1])
                upper[half, pl.ds(GROUP * first, 32, stride=2), :] = even
                upper[half, pl.ds(GROUP * first + 1, 32, stride=2), :] = odd
        sign = -1.0 if stat in (1, 4) else 1.0
        for a in range(halves):
            rows_a = slice(LANES * a, LANES * (a + 1))
            for b in range(a, halves):
                rows_b = slice(LANES * b, LANES * (b + 1))
                block = upper[b, rows_a, :]
                turned = block.T * sign
                if a == b:
                    full[stat, rows_a, rows_a] = block + turned
                else:
                    full[stat, rows_a, rows_b] = block
                    full[stat, rows_b, rows_a] = turned

    gain_re = jnp.ones((1, stations), F32)
    gain_im = jnp.zeros((1, stations), F32)
    for round_id in range(ROUNDS):

        def build(step, carry):
            rows = pl.ds(pl.multiple_of(step * 16, 16), 16)
            vm_re, vm_im, mm = full[3, rows, :], full[4, rows, :], full[6, rows, :]
            if round_id == 0:
                cross_re, cross_im, power = full[0, rows, :], full[1, rows, :], full[5, rows, :]
                full[0, rows, :] = cross_re - vm_re
                full[1, rows, :] = cross_im - vm_im
                full[5, rows, :] = power - mm
            else:
                vv = full[2, rows, :]
                col_re = jnp.concatenate([col_gain_re[round_id - 1, rows, :]] * halves, axis=1)
                col_im = jnp.concatenate([col_gain_im[round_id - 1, rows, :]] * halves, axis=1)
                rest_re = 1.0 - (col_re * gain_re + col_im * gain_im)
                rest_im = col_re * gain_im - col_im * gain_re
                turn_re = rest_re * vm_re + rest_im * vm_im
                turn_im = rest_re * vm_im - rest_im * vm_re
                mm = vv + (rest_re * rest_re + rest_im * rest_im) * mm + (turn_re + turn_re)
                vm_re, vm_im = vv + turn_re, turn_im
                if round_id + 1 < ROUNDS:
                    full[3, rows, :], full[4, rows, :], full[6, rows, :] = vm_re, vm_im, mm
                cross_re, cross_im = full[0, rows, :] + vm_re, full[1, rows, :] + vm_im
                power = full[5, rows, :] + mm
            for part, value in enumerate((cross_re, cross_im, power)):
                weights[rows, part * stations : (part + 1) * stations] = value.astype(BF16)
            return carry

        lax.fori_loop(0, stations // 16, build, 0, unroll=4)
        row8 = lax.broadcasted_iota(jnp.int32, (8, stations), 0)
        for iteration in range(CAL_ITERS):
            norm = gain_re * gain_re + gain_im * gain_im
            left = jnp.where(row8 == 0, gain_re, jnp.where(row8 == 1, gain_im, norm))
            high = left.astype(BF16).astype(F32)
            left = jnp.concatenate([high, left - high]).astype(BF16)
            raw = jnp.dot(left, weights[...], preferred_element_type=F32)
            raw = raw[0:8] + raw[8:16]
            with_re, with_im = raw[:, 0:stations], raw[:, stations : 2 * stations]
            below = raw[2:3, 2 * stations : 3 * stations]
            next_re = (with_re[0:1] + with_im[1:2]) / below
            next_im = (with_re[1:2] - with_im[0:1]) / below
            if iteration % 2 == 1:
                next_re = 0.5 * (next_re + gain_re)
                next_im = 0.5 * (next_im + gain_im)
            gain_re, gain_im = next_re, next_im
        lane1 = lax.broadcasted_iota(jnp.int32, (1, LANES), 1) < GROUP
        for value, row_gain, col_gain in (
            (gain_re, row_gain_re, col_gain_re),
            (gain_im, row_gain_im, col_gain_im),
        ):
            for half in range(halves):
                part = value[:, LANES * half : LANES * (half + 1)]
                turned = pltpu.roll(jnp.broadcast_to(part, (8, LANES)), GROUP, 1)[0:1]
                row_gain[2 * half, round_id : round_id + 1, :] = jnp.where(lane1, part, turned)
                row_gain[2 * half + 1, round_id : round_id + 1, :] = jnp.where(lane1, turned, part)
                col_gain[round_id, LANES * half : LANES * (half + 1), :] = jnp.broadcast_to(
                    part, (LANES, LANES)
                ).T

    hot = (
        lax.broadcasted_iota(jnp.int32, (stations, stations), 0) == order[...]
    ).astype(BF16)
    pieces = []
    for value in (gain_re, gain_im):
        high = value.astype(BF16).astype(F32)
        middle = (value - high).astype(BF16).astype(F32)
        pieces += [high, middle, value - high - middle]
    row16 = lax.broadcasted_iota(jnp.int32, (16, stations), 0)
    left = jnp.zeros((16, stations), F32)
    for at, piece in enumerate(pieces):
        left = jnp.where(row16 == at, piece, left)
    spread = lax.dot_general(
        left.astype(BF16), hot, (((1,), (1,)), ((), ())), preferred_element_type=F32
    )
    gains[0:1, :] = spread[0:1] + spread[1:2] + spread[2:3]
    gains[1:2, :] = spread[3:4] + spread[4:5] + spread[5:6]

    mode = lax.broadcasted_iota(jnp.int32, (MODES, LANES), 0)
    lane_half = lax.broadcasted_iota(jnp.int32, (1, LANES), 1) < GROUP

    def tile(t, carry):
        row = first_row + 2 * t
        first, second = row_groups_of(row, groups)
        station = first * GROUP + (row & 63)

        def row_side(table, round_id):
            low, high = table[round_id, pl.ds(station, 1), :], table[round_id, pl.ds(station + 1, 1), :]
            return jnp.where(lane_half, low, high)

        q_res, q_ims = row_gain_re[second], row_gain_im[second]
        a_re, a_im = jnp.zeros((1, LANES), F32), jnp.zeros((1, LANES), F32)
        b_re, b_im = jnp.ones((1, LANES), F32), jnp.zeros((1, LANES), F32)
        for round_id in range(ROUNDS):
            p_re, p_im = row_side(col_gain_re, round_id), row_side(col_gain_im, round_id)
            q_re, q_im = q_res[round_id : round_id + 1], q_ims[round_id : round_id + 1]
            prod_re = p_re * q_re + p_im * q_im
            prod_im = p_im * q_re - p_re * q_im
            if round_id + 1 == ROUNDS:
                break
            rest_re, rest_im = 1.0 - prod_re, -prod_im
            a_re, a_im = 1.0 + rest_re * a_re - rest_im * a_im, rest_re * a_im + rest_im * a_re
            b_re, b_im = rest_re * b_re - rest_im * b_im, rest_re * b_im + rest_im * b_re
        b_re = b_re - 1.0
        inside = (mode < counts[pl.ds(t, 1), :]).astype(F32)
        raw = modes[tile_lanes(t, MODES), :]
        v_re, v_im, m_re, m_im = (raw[:, LANES * i : LANES * (i + 1)] for i in range(4))
        f_re = inside * (a_re * v_re - a_im * v_im + b_re * m_re - b_im * m_im)
        f_im = inside * (a_re * v_im + a_im * v_re + b_re * m_im + b_im * m_re)
        both = jnp.concatenate([f_re, f_im], axis=1)
        high = both.astype(BF16)
        low = (both - high.astype(F32)).astype(BF16)
        fitted = jnp.dot(
            expand[...], jnp.concatenate([high, low, high]), preferred_element_type=F32
        )
        start = pl.multiple_of(2 * t * FREQ_CHANNELS, FREQ_CHANNELS)
        mod_re = model[pl.ds(start, FREQ_CHANNELS), :].astype(F32) + fitted[:, 0:LANES]
        mod_im = model[pl.ds(start + FREQ_CHANNELS, FREQ_CHANNELS), :].astype(F32)
        mod_im = mod_im + fitted[:, LANES : 2 * LANES]
        obs_re, obs_im = data_sides(observed, tiles, t)
        weight = tile_weights(groups, tiles, first_row, t, kept)
        left_re = weight * (obs_re - (prod_re * mod_re - prod_im * mod_im))
        left_im = weight * (obs_im - (prod_re * mod_im + prod_im * mod_re))
        left_out[0, 0, :, tile_lanes(t)] = left_re.astype(BF16)
        left_out[1, 0, :, tile_lanes(t)] = left_im.astype(BF16)
        return carry

    parts = output_parts(tiles)
    size = tiles // parts
    copies = []
    for part in range(parts):
        lax.fori_loop(part * size, (part + 1) * size, tile, 0, unroll=size)
        lanes = pl.ds(part * size * LANES, size * LANES)
        copies.append(
            pltpu.make_async_copy(
                left_out.at[:, :, :, lanes], residual.at[:, :, :, lanes], out_sems.at[part]
            )
        )
        copies[-1].start()
    for copy in copies:
        copy.wait()


def call(kernel, out_shape, scratch, name, in_spaces, mib, flops=0, moved=0, out_specs=None):
    return pl.pallas_call(
        kernel,
        out_shape=out_shape,
        in_specs=[pl.BlockSpec(memory_space=space) for space in in_spaces],
        out_specs=out_specs or jax.tree.map(lambda _: pl.BlockSpec(memory_space=VMEM), out_shape),
        scratch_shapes=scratch,
        compiler_params=pltpu.CompilerParams(vmem_limit_bytes=mib << 20),
        cost_estimate=pl.CostEstimate(flops=flops, bytes_accessed=moved, transcendentals=0),
        name=name,
    )


def exchange(block, distance, wide):
    return lax.ppermute(block, "wide", [(i, i ^ distance) for i in range(wide)])


def gather_order(wide):
    order = [0, wide // 2, 3 * wide // 4, wide // 4]
    distance = wide // 8
    while distance:
        order += [place ^ distance for place in order]
        distance //= 2
    return order


def gather_stats(stats, wide):
    held = jnp.stack([stats] + [exchange(stats, flip, wide) for flip in gather_order(wide)[1:4]])
    distance = wide // 8
    while distance:
        held = jnp.concatenate([held, exchange(held, distance, wide)])
        distance //= 2
    return held


def body(
    visibilities,
    kept_baseline_mask,
    fitted_mode_count,
    station_order,
    station_xy,
    comp_lm,
    comp_flux,
    centre_flux,
):
    wide = lax.axis_size("wide")
    local_chan = visibilities.shape[2]
    total = visibilities.shape[3]
    base = total // wide
    tiles = base // LANES
    padded = -(-tiles // 8) * 8
    stations = station_order.shape[0]
    groups = stations // GROUP
    comps = comp_lm.shape[1]
    rows = 2 * padded
    fit, expand = (jnp.asarray(table) for table in basis_tables())
    kept = kept_baseline_mask.reshape(total // LANES, LANES)
    counts = fitted_mode_count.reshape(tiles, LANES)

    packed = pl.pallas_call(
        lambda *refs: pack_kernel(wide, base, *refs),
        out_shape=jax.ShapeDtypeStruct((wide, local_chan, 2 * base + LANES), BF16),
        in_specs=[pl.BlockSpec(memory_space=pltpu.MemorySpace.HBM)] * 2,
        out_specs=pl.BlockSpec(memory_space=pltpu.MemorySpace.HBM),
        scratch_shapes=[
            pltpu.VMEM((wide, local_chan, 2 * base + LANES), BF16),
            pltpu.SMEM((local_chan,), F32),
            pltpu.SemaphoreType.DMA((PACK_PARTS, 2)),
            pltpu.SemaphoreType.DMA((PACK_PARTS,)),
            pltpu.SemaphoreType.DMA,
        ],
        compiler_params=pltpu.CompilerParams(vmem_limit_bytes=60 << 20),
        name="pack",
    )(visibilities.reshape(2, local_chan, wide, base).transpose(0, 2, 1, 3), centre_flux)
    observed = lax.all_to_all(packed, "wide", 0, 0, tiled=True)
    observed = observed.reshape(FREQ_CHANNELS // 8, 8, 2 * base + LANES)

    state_row = pltpu.VMEM((rows, comps), F32)
    state_col = pltpu.VMEM((comps, LANES), F32)
    left = pltpu.VMEM((UNROLL, 2 * rows, comps), BF16)
    right = pltpu.VMEM((UNROLL, comps, 2 * LANES), BF16)
    real, imag = call(
        lambda *refs: predict_kernel(groups, tiles, padded, *refs),
        (
            jax.ShapeDtypeStruct((tiles * FREQ_CHANNELS, LANES), F32),
            jax.ShapeDtypeStruct((tiles * FREQ_CHANNELS, LANES), BF16),
        ),
        [pltpu.VMEM((padded * FREQ_CHANNELS, LANES), F32)] * 2
        + [pltpu.VMEM((rows + LANES, LANES), F32)] * 2
        + [state_row] * 4
        + [state_col] * 4
        + [left, right, left, right],
        "predict",
        [SMEM, SMEM, VMEM, VMEM],
        20,
        FREQ_CHANNELS * 2 * 2 * rows * 2 * comps * 256,
        padded * 256 * LANES * 4,
    )(station_order, station_xy.reshape(2, stations), comp_lm, comp_flux.reshape(1, comps))
    stats, model, modes = call(
        lambda *refs: stats_kernel(groups, tiles, *refs),
        (
            jax.ShapeDtypeStruct((stat_groups(tiles) * 8, LANES), BF16),
            jax.ShapeDtypeStruct((tiles * 2 * FREQ_CHANNELS, LANES), BF16),
            jax.ShapeDtypeStruct((tiles * MODES, 4 * LANES), F32),
        ),
        [pltpu.VMEM((FREQ_CHANNELS, LANES), F32), pltpu.VMEM((tiles * 8, LANES), F32)],
        "stats",
        [VMEM] * 6,
        12,
        moved=tiles * 256 * LANES * 8,
    )(observed, real, imag, kept, counts, fit)
    gathered = gather_stats(stats, wide)
    gains, residual = call(
        lambda *refs: solve_kernel(groups, tiles, wide, *refs),
        (
            jax.ShapeDtypeStruct((2, stations), F32),
            jax.ShapeDtypeStruct((2, 1, FREQ_CHANNELS, base), BF16),
        ),
        [
            pltpu.VMEM((wide * tiles * 8, LANES), F32),
            pltpu.VMEM((stations // LANES, stations, LANES), F32),
            pltpu.VMEM((STATS, stations, stations), F32),
            pltpu.VMEM((stations, 3 * stations), BF16),
            pltpu.VMEM((groups, 8, LANES), F32),
            pltpu.VMEM((groups, 8, LANES), F32),
            pltpu.VMEM((ROUNDS, stations, LANES), F32),
            pltpu.VMEM((ROUNDS, stations, LANES), F32),
            pltpu.VMEM((2, 1, FREQ_CHANNELS, base), BF16),
            pltpu.SemaphoreType.DMA((output_parts(tiles),)),
        ],
        "solve",
        [VMEM] * 8,
        16,
        moved=tiles * 256 * LANES * 6,
        out_specs=(
            pl.BlockSpec(memory_space=VMEM),
            pl.BlockSpec(memory_space=pltpu.MemorySpace.HBM),
        ),
    )(
        gathered,
        observed,
        model,
        modes,
        kept,
        counts,
        station_order.reshape(1, stations),
        expand,
    )
    return gains, residual


def solution(mesh):
    placed = (
        P(None, None, ("band", "wide"), None),
        P("band"),
        P("wide"),
        P(),
        P(),
        P(),
        P(),
        P(("band", "wide")),
    )
    return jax.shard_map(
        body,
        mesh=mesh,
        in_specs=placed,
        out_specs=(P(None, "band"), P(None, None, "band", "wide")),
        check_vma=False,
    )
```

```python
import math

import jax
import jax.numpy as jnp
import numpy as np
from jax import lax
from jax.experimental import pallas as pl
from jax.experimental.pallas import tpu as pltpu
from jax.sharding import PartitionSpec as P

GROUP = 64
FREQ_CHANNELS = 128
MODES = 16
CAL_ITERS = 3
ROUNDS = 3
STATS = 7
PAIRS = 4
LANES = 128
UNROLL = 8
PACK_PARTS = 4
PLACES_FLOPS = 4 * 10**9
VMEM = pltpu.MemorySpace.VMEM
SMEM = pltpu.MemorySpace.SMEM
F32 = jnp.float32
BF16 = jnp.bfloat16


def row_groups_of(row, groups):
    block = row >> 6
    first = jnp.zeros_like(block)
    start = jnp.zeros_like(block)
    edge = 0
    for group in range(1, groups):
        edge += groups - group + 1
        past = (block >= edge).astype(jnp.int32)
        first = first + past
        start = start + past * (groups - group + 1)
    return first, block - start + first


def basis_tables():
    mid = np.arange(FREQ_CHANNELS)[:, None] + 0.5
    order = np.arange(MODES)[None, :]
    scale = np.where(order == 0, math.sqrt(1.0 / FREQ_CHANNELS), math.sqrt(2.0 / FREQ_CHANNELS))
    basis = (scale * np.cos(math.pi / FREQ_CHANNELS * mid * order)).astype(np.float32)
    high = basis.astype(BF16)
    low = (basis - high.astype(np.float32)).astype(BF16)
    return np.concatenate([high, low], axis=1).T, np.concatenate([high, high, low], axis=1)


def output_parts(tiles):
    sizes = []
    for left in (tiles - early_tiles(tiles), early_tiles(tiles)):
        while left:
            sizes.append(-(-left // 2))
            left -= sizes[-1]
    return sizes


def turn_trig(turns):
    quarter = jnp.floor(turns * 4.0 + 0.5)
    angle = (turns - 0.25 * quarter) * (2.0 * math.pi)
    square = angle * angle
    sine = angle * (
        1.0
        + square
        * (-1.0 / 6 + square * (1.0 / 120 + square * (-1.0 / 5040 + square * (1.0 / 362880))))
    )
    cosine = 1.0 + square * (
        -0.5
        + square
        * (1.0 / 24 + square * (-1.0 / 720 + square * (1.0 / 40320 + square * (-1.0 / 3628800))))
    )
    phase = quarter - 4.0 * jnp.floor(quarter * 0.25)
    odd = (phase == 1.0) | (phase == 3.0)
    cos_out = jnp.where(odd, sine, cosine)
    sin_out = jnp.where(odd, cosine, sine)
    cos_out = jnp.where((phase == 1.0) | (phase == 2.0), -cos_out, cos_out)
    sin_out = jnp.where(phase >= 2.0, -sin_out, sin_out)
    return cos_out, sin_out


def early_tiles(tiles):
    return tiles * 3 // 10


def pack_early_kernel(wide, base, source, centre, *rest):
    targets, (held, flux, in_sems, out_sems, flux_sem) = rest[:4], rest[4:]
    chan = centre.shape[0]
    rank = lax.axis_index("wide")
    quarter = wide // 4
    late = base - early_tiles(base // LANES) * LANES
    size = base - late
    bring = [
        pltpu.make_async_copy(
            source.at[side, :, :, pl.ds(late, size)],
            held.at[:, :, pl.ds(side * size, size)],
            in_sems.at[side],
        )
        for side in range(2)
    ]
    fetch = pltpu.make_async_copy(centre, flux, flux_sem)
    fetch.start()
    for copy in bring:
        copy.start()
    fetch.wait()
    row = lax.broadcasted_iota(jnp.int32, (chan, LANES), 0)
    lane = lax.broadcasted_iota(jnp.int32, (chan, LANES), 1)
    value = jnp.zeros(row.shape, F32)
    for c in range(chan):
        value = jnp.where(row == c, flux[c], value)
    high = value.astype(BF16).astype(F32)
    middle = (value - high).astype(BF16).astype(F32)
    low = value - high - middle
    parts = jnp.where(lane == 0, high, jnp.where(lane == 1, middle, jnp.where(lane == 2, low, 0.0)))
    held[:, :, 2 * size : 2 * size + LANES] = jnp.broadcast_to(
        parts.astype(BF16)[None], (wide, chan, LANES)
    )
    for copy in bring:
        copy.wait()
    send = [
        pltpu.make_async_copy(
            held.at[rank ^ flip], targets[flip // quarter].at[flip % quarter], out_sems.at[flip]
        )
        for flip in range(wide)
    ]
    for copy in send:
        copy.start()
    for copy in send:
        copy.wait()


def pack_kernel(wide, base, source, after, target, held, in_sems, out_sems):
    del after
    size = base - early_tiles(base // LANES) * LANES
    share = wide // PACK_PARTS
    peers = [pl.ds(part * share, share) for part in range(PACK_PARTS)]
    bring = [
        [
            pltpu.make_async_copy(
                source.at[side, peers[part], :, pl.ds(0, size)],
                held.at[peers[part], :, pl.ds(side * size, size)],
                in_sems.at[part, side],
            )
            for side in range(2)
        ]
        for part in range(PACK_PARTS)
    ]
    send = [
        pltpu.make_async_copy(held.at[peers[part]], target.at[peers[part]], out_sems.at[part])
        for part in range(PACK_PARTS)
    ]
    for pair in bring:
        for copy in pair:
            copy.start()
    for pair, copy in zip(bring, send):
        for came in pair:
            came.wait()
        copy.start()
    for copy in send:
        copy.wait()


def column_groups(groups, tiles, first_row):
    last_row = first_row + (2 * tiles - 1)
    return [row_groups_of(row, groups)[1] * GROUP for row in (first_row, last_row)]


def places_kernel(groups, tiles, padded, order, xy, after, pos_x, pos_y):
    del after
    first_row = lax.axis_index("wide") * (2 * tiles)
    col_a, col_b = column_groups(groups, tiles, first_row)
    pos_x[...] = jnp.zeros_like(pos_x)
    pos_y[...] = jnp.zeros_like(pos_y)

    def place(slot, position):
        station = order[position]
        pos_x[pl.ds(slot, 1), :] = jnp.full((1, LANES), xy[0, station], F32)
        pos_y[pl.ds(slot, 1), :] = jnp.full((1, LANES), xy[1, station], F32)

    def place_row(t, carry):
        for half in range(2):
            row = first_row + 2 * t + half
            place(half * padded + t, row_groups_of(row, groups)[0] * GROUP + (row & 63))
        return carry

    def place_col(j, carry):
        place(2 * padded + j, col_a + j)
        place(2 * padded + GROUP + j, col_b + j)
        return carry

    lax.fori_loop(0, tiles, place_row, 0, unroll=10)
    lax.fori_loop(0, GROUP, place_col, 0, unroll=16)


def predict_kernel(
    groups,
    tiles,
    padded,
    pos_x,
    pos_y,
    lm,
    flux,
    real_out,
    imag_out,
    real,
    imag,
    row_c,
    row_s,
    row_dc,
    row_ds,
    row_lc,
    row_ls,
    col_c,
    col_s,
    col_dc,
    col_ds,
    col_lc,
    col_ls,
    left_a,
    right_a,
    left_b,
    right_b,
):
    comps = lm.shape[1]
    first_row = lax.axis_index("wide") * (2 * tiles)
    edge = jnp.minimum((((first_row >> 6) + 1) * GROUP - first_row) >> 1, tiles)
    step = 0.25 / FREQ_CHANNELS
    rows = 2 * padded
    weight = flux[...] * (1.0 / math.sqrt(comps))
    for k in range(0, comps, LANES):
        lane = slice(k, k + LANES)
        axis_l = lm[0:1, lane]
        axis_m = lm[1:2, lane]
        turns = pos_x[0:rows, :] * axis_l + pos_y[0:rows, :] * axis_m
        cosine, sine = turn_trig(turns)
        row_c[:, lane] = cosine * weight[:, lane]
        row_s[:, lane] = sine * weight[:, lane]
        row_dc[:, lane], row_ds[:, lane] = turn_trig(turns * step)
        row_lc[:, lane], row_ls[:, lane] = turn_trig(turns * (UNROLL * step))
        turns = (
            pos_x[rows : rows + LANES, :] * axis_l + pos_y[rows : rows + LANES, :] * axis_m
        ).T
        col_c[lane, :], col_s[lane, :] = turn_trig(turns)
        col_dc[lane, :], col_ds[lane, :] = turn_trig(turns * step)
        col_lc[lane, :], col_ls[lane, :] = turn_trig(turns * (UNROLL * step))

    def channels(c, s, dc, ds, leap_c, leap_s):
        twice = dc + dc
        out = [(c, s), (c * dc - s * ds, s * dc + c * ds)]
        while len(out) < UNROLL:
            out.append(tuple(twice * now - before for now, before in zip(out[-1], out[-2])))
        return out, (c * leap_c - s * leap_s, s * leap_c + c * leap_s)

    def fill_col(right, k):
        part = slice(k, k + 16)
        state = [table[part, :] for table in (col_c, col_s, col_dc, col_ds, col_lc, col_ls)]
        values, (col_c[part, :], col_s[part, :]) = channels(*state)
        for u, (c, s) in enumerate(values):
            right[u, part, 0:LANES] = c.astype(BF16)
            right[u, part, LANES : 2 * LANES] = s.astype(BF16)

    def fill_row(left, r, k):
        part, low = slice(r, r + 16), slice(rows + r, rows + r + 16)
        lane = slice(k, k + LANES)
        state = [table[part, lane] for table in (row_c, row_s, row_dc, row_ds, row_lc, row_ls)]
        values, (row_c[part, lane], row_s[part, lane]) = channels(*state)
        for u, (c, s) in enumerate(values):
            left[u, part, lane] = c.astype(BF16)
            left[u, low, lane] = s.astype(BF16)

    def fill_steps(left, right):
        steps = [lambda k=k: fill_col(right, k) for k in range(0, comps, 16)]
        return steps + [
            lambda r=r, k=k: fill_row(left, r, k)
            for r in range(0, rows, 16)
            for k in range(0, comps, LANES)
        ]

    first_half = lax.broadcasted_iota(jnp.int32, (padded, LANES), 1) < GROUP
    in_a = lax.broadcasted_iota(jnp.int32, (padded, LANES), 0) < edge

    def multiply(left, right, group, u):
        product = jnp.dot(left[u], right[u], preferred_element_type=F32)
        channel = group * UNROLL + u
        with_cos, with_sin = product[:, 0:LANES], product[:, LANES : 2 * LANES]
        sums = (
            (with_cos[0:rows] + with_sin[rows : 2 * rows], real),
            (with_cos[rows : 2 * rows] - with_sin[0:rows], imag),
        )
        for side, out in sums:
            even, odd = side[0:padded], side[padded : 2 * padded]
            even = jnp.where(in_a, even, pltpu.roll(even, GROUP, 1))
            odd = jnp.where(in_a, pltpu.roll(odd, GROUP, 1), odd)
            out[pl.ds(channel, padded, stride=FREQ_CHANNELS), :] = jnp.where(first_half, even, odd)

    for step in fill_steps(left_a, right_a):
        step()

    def group_pass(now, later, group):
        steps = fill_steps(*later)
        share = -(-len(steps) // UNROLL)
        for u in range(UNROLL):
            multiply(*now, group, u)
            for step in steps[u * share : (u + 1) * share]:
                step()

    def two_groups(pair, carry):
        group_pass((left_a, right_a), (left_b, right_b), 2 * pair)
        group_pass((left_b, right_b), (left_a, right_a), 2 * pair + 1)
        return carry

    lax.fori_loop(0, FREQ_CHANNELS // (2 * UNROLL), two_groups, 0)
    size = tiles * FREQ_CHANNELS
    real_out[...] = real[0:size, :]
    imag_out[...] = imag[0:size, :].astype(BF16)


def tile_weights(groups, tiles, first_row, t, kept):
    lane = lax.broadcasted_iota(jnp.int32, (1, LANES), 1)
    row = first_row + 2 * t
    first, second = row_groups_of(row, groups)
    inside = (row & 63) + (lane >> 6)
    usable = (first != second) | (inside < (lane & 63))
    mask = kept[pl.ds((first_row >> 1) + t, 1), :].astype(F32)
    return jnp.where(usable, mask, 0.0)


def tile_lanes(t, size=LANES, offset=0):
    return pl.ds(pl.multiple_of(offset + t * size, size), size)


def late_sides(observed, tiles, t):
    return [
        observed[:, :, tile_lanes(t, LANES, side * tiles * LANES)]
        .astype(F32)
        .reshape(FREQ_CHANNELS, LANES)
        for side in range(2)
    ]


def early_lanes(early, key, lanes):
    blocks = [early[key ^ at, :, lanes].astype(F32) for at in range(early.shape[0])]
    return jnp.concatenate(blocks)


def early_sides(early, key, tiles, t):
    return [early_lanes(early, key, tile_lanes(t, LANES, side * tiles * LANES)) for side in range(2)]


def stats_kernel(
    groups, tiles, by_flip, observed, early, real, imag, kept, counts, fit, stats, model, modes, shift, rows, paired
):
    rank = lax.axis_index("wide")
    first_row = rank * (2 * tiles)
    mode = lax.broadcasted_iota(jnp.int32, (MODES, LANES), 0)
    key = rank if by_flip else 0
    ahead = early_tiles(tiles)
    rest = tiles - ahead
    tail = early_lanes(early, key, pl.ds(2 * ahead * LANES, LANES))
    shift[...] = jnp.broadcast_to(jnp.sum(tail, axis=1, keepdims=True), tail.shape)

    def one(t, sides):
        obs_re, obs_im = sides
        half = tile_lanes(t, FREQ_CHANNELS)
        mod_re16, mod_im16 = (real[half, :] + shift[...]).astype(BF16), imag[half, :]
        both = pl.multiple_of(2 * t * FREQ_CHANNELS, FREQ_CHANNELS)
        model[pl.ds(both, FREQ_CHANNELS), :] = mod_re16
        model[pl.ds(both + FREQ_CHANNELS, FREQ_CHANNELS), :] = mod_im16
        mod_re, mod_im = mod_re16.astype(F32), mod_im16.astype(F32)

        def total(terms):
            return jnp.sum(terms, axis=0, keepdims=True)

        cross_re = total(obs_re * mod_re + obs_im * mod_im)
        cross_im = total(obs_im * mod_re - obs_re * mod_im)
        power = total(mod_re * mod_re + mod_im * mod_im)
        sides = [obs_re.astype(BF16), obs_im.astype(BF16), mod_re16, mod_im16]
        raw = jnp.dot(fit[...], jnp.concatenate(sides, axis=1), preferred_element_type=F32)
        raw = raw[0:MODES] + raw[MODES : 2 * MODES]
        modes[tile_lanes(t, MODES), :] = raw
        v_re, v_im, m_re, m_im = (raw[:, LANES * i : LANES * (i + 1)] for i in range(4))
        inside = (mode < counts[pl.ds(t, 1), :]).astype(F32)
        vv = total(inside * (v_re * v_re + v_im * v_im))
        vm_re = total(inside * (v_re * m_re + v_im * m_im))
        vm_im = total(inside * (v_im * m_re - v_re * m_im))
        mm = total(inside * (m_re * m_re + m_im * m_im))
        weight = tile_weights(groups, tiles, first_row, t, kept)
        parts = [cross_re, cross_im, vv, vm_re, vm_im, power, mm, jnp.zeros((1, LANES), F32)]
        rows[tile_lanes(t, 8), :] = jnp.concatenate(parts) * weight

    def one_late(t, carry):
        one(t, late_sides(observed, rest, t))
        return carry

    def one_early(t, carry):
        one(rest + t, early_sides(early, key, ahead, t))
        return carry

    lax.fori_loop(0, rest, one_late, 0, unroll=rest // 2 if rest % 2 == 0 else rest)
    lax.fori_loop(0, ahead, one_early, 0, unroll=ahead)
    first_half = lax.broadcasted_iota(jnp.int32, (tiles, LANES), 1) < GROUP
    for pair in range(PAIRS):
        one_stat = rows[pl.ds(2 * pair, tiles, stride=8), :]
        other = rows[pl.ds(2 * pair + 1, tiles, stride=8), :]
        even = jnp.where(first_half, one_stat, pltpu.roll(other, GROUP, 1))
        odd = jnp.where(first_half, pltpu.roll(one_stat, GROUP, 1), other)
        paired[pl.ds(2 * tiles * pair, tiles, stride=2), :] = even
        paired[pl.ds(2 * tiles * pair + 1, tiles, stride=2), :] = odd
    stats[...] = paired[...].astype(BF16)


def solve_kernel(
    groups,
    tiles,
    by_flip,
    wide,
    gathered,
    observed,
    early,
    model,
    modes,
    kept,
    counts,
    order,
    expand,
    gains,
    residual,
    flat,
    full,
    weights,
    row_gain_re,
    row_gain_im,
    col_gain_re,
    col_gain_im,
    left_out,
    out_sems,
):
    stations = groups * GROUP
    rank = lax.axis_index("wide")
    first_row = rank * (2 * tiles)
    halves = stations // LANES
    count = 2 * tiles
    for k, flip in enumerate(gather_order(wide)):
        start = pl.multiple_of((rank ^ flip) * count, count & -count)
        values = gathered[k].astype(F32)
        for pair in range(PAIRS):
            flat[pair, pl.ds(start, count), :] = values[pair * count : (pair + 1) * count]
    block_id = {}
    for first in range(groups):
        for second in range(first, groups):
            block_id[first, second] = len(block_id)
    lane64 = lax.broadcasted_iota(jnp.int32, (GROUP, LANES), 1) < GROUP

    def placed_block(stat, first, half):
        pair, side = stat // 2, stat % 2
        sides = []
        for at in range(2):
            index = block_id.get((first, 2 * half + at))
            if index is None:
                sides.append(jnp.zeros((GROUP, LANES), F32))
                continue
            block = flat[pair, GROUP * index : GROUP * (index + 1), :]
            sides.append(block if at == side else pltpu.roll(block, GROUP, 1))
        return jnp.where(lane64, sides[0], sides[1])

    for stat in range(STATS):
        sign = -1.0 if stat in (1, 4) else 1.0
        for a in range(halves):
            rows_a = slice(LANES * a, LANES * (a + 1))
            for b in range(a, halves):
                rows_b = slice(LANES * b, LANES * (b + 1))
                block = jnp.concatenate([placed_block(stat, 2 * a + i, b) for i in range(2)])
                turned = block.T * sign
                if a == b:
                    full[stat, rows_a, rows_a] = block + turned
                else:
                    full[stat, rows_a, rows_b] = block
                    full[stat, rows_b, rows_a] = turned

    gain_re = jnp.ones((1, stations), F32)
    gain_im = jnp.zeros((1, stations), F32)
    for round_id in range(ROUNDS):

        def build(step, carry):
            rows = pl.ds(pl.multiple_of(step * 16, 16), 16)
            vm_re, vm_im, mm = full[3, rows, :], full[4, rows, :], full[6, rows, :]
            if round_id == 0:
                cross_re, cross_im, power = full[0, rows, :], full[1, rows, :], full[5, rows, :]
                full[0, rows, :] = cross_re - vm_re
                full[1, rows, :] = cross_im - vm_im
                full[5, rows, :] = power - mm
            else:
                vv = full[2, rows, :]
                col_re = jnp.concatenate([col_gain_re[round_id - 1, rows, :]] * halves, axis=1)
                col_im = jnp.concatenate([col_gain_im[round_id - 1, rows, :]] * halves, axis=1)
                rest_re = 1.0 - (col_re * gain_re + col_im * gain_im)
                rest_im = col_re * gain_im - col_im * gain_re
                turn_re = rest_re * vm_re + rest_im * vm_im
                turn_im = rest_re * vm_im - rest_im * vm_re
                mm = vv + (rest_re * rest_re + rest_im * rest_im) * mm + (turn_re + turn_re)
                vm_re, vm_im = vv + turn_re, turn_im
                if round_id + 1 < ROUNDS:
                    full[3, rows, :], full[4, rows, :], full[6, rows, :] = vm_re, vm_im, mm
                cross_re, cross_im = full[0, rows, :] + vm_re, full[1, rows, :] + vm_im
                power = full[5, rows, :] + mm
            for part, value in enumerate((cross_re, cross_im, power)):
                weights[rows, part * stations : (part + 1) * stations] = value.astype(BF16)
            return carry

        lax.fori_loop(0, stations // 16, build, 0, unroll=4)
        row8 = lax.broadcasted_iota(jnp.int32, (8, stations), 0)
        for iteration in range(CAL_ITERS):
            norm = gain_re * gain_re + gain_im * gain_im
            left = jnp.where(row8 == 0, gain_re, jnp.where(row8 == 1, gain_im, norm))
            high = left.astype(BF16).astype(F32)
            left = jnp.concatenate([high, left - high]).astype(BF16)
            raw = jnp.dot(left, weights[...], preferred_element_type=F32)
            raw = raw[0:8] + raw[8:16]
            with_re, with_im = raw[:, 0:stations], raw[:, stations : 2 * stations]
            below = raw[2:3, 2 * stations : 3 * stations]
            next_re = (with_re[0:1] + with_im[1:2]) / below
            next_im = (with_re[1:2] - with_im[0:1]) / below
            if iteration % 2 == 1:
                next_re = 0.5 * (next_re + gain_re)
                next_im = 0.5 * (next_im + gain_im)
            gain_re, gain_im = next_re, next_im
        lane1 = lax.broadcasted_iota(jnp.int32, (1, LANES), 1) < GROUP
        for value, row_gain, col_gain in (
            (gain_re, row_gain_re, col_gain_re),
            (gain_im, row_gain_im, col_gain_im),
        ):
            for half in range(halves):
                part = value[:, LANES * half : LANES * (half + 1)]
                turned = pltpu.roll(jnp.broadcast_to(part, (8, LANES)), GROUP, 1)[0:1]
                row_gain[2 * half, round_id : round_id + 1, :] = jnp.where(lane1, part, turned)
                row_gain[2 * half + 1, round_id : round_id + 1, :] = jnp.where(lane1, turned, part)
                col_gain[round_id, LANES * half : LANES * (half + 1), :] = jnp.broadcast_to(
                    part, (LANES, LANES)
                ).T

    mode = lax.broadcasted_iota(jnp.int32, (MODES, LANES), 0)
    lane_half = lax.broadcasted_iota(jnp.int32, (1, LANES), 1) < GROUP

    key = rank if by_flip else 0
    ahead = early_tiles(tiles)
    rest = tiles - ahead

    def tile(t, get_sides):
        row = first_row + 2 * t
        first, second = row_groups_of(row, groups)
        station = first * GROUP + (row & 63)

        def row_side(table, round_id):
            low, high = table[round_id, pl.ds(station, 1), :], table[round_id, pl.ds(station + 1, 1), :]
            return jnp.where(lane_half, low, high)

        q_res, q_ims = row_gain_re[second], row_gain_im[second]
        a_re, a_im = jnp.zeros((1, LANES), F32), jnp.zeros((1, LANES), F32)
        b_re, b_im = jnp.ones((1, LANES), F32), jnp.zeros((1, LANES), F32)
        for round_id in range(ROUNDS):
            p_re, p_im = row_side(col_gain_re, round_id), row_side(col_gain_im, round_id)
            q_re, q_im = q_res[round_id : round_id + 1], q_ims[round_id : round_id + 1]
            prod_re = p_re * q_re + p_im * q_im
            prod_im = p_im * q_re - p_re * q_im
            if round_id + 1 == ROUNDS:
                break
            rest_re, rest_im = 1.0 - prod_re, -prod_im
            a_re, a_im = 1.0 + rest_re * a_re - rest_im * a_im, rest_re * a_im + rest_im * a_re
            b_re, b_im = rest_re * b_re - rest_im * b_im, rest_re * b_im + rest_im * b_re
        b_re = b_re - 1.0
        inside = (mode < counts[pl.ds(t, 1), :]).astype(F32)
        raw = modes[tile_lanes(t, MODES), :]
        v_re, v_im, m_re, m_im = (raw[:, LANES * i : LANES * (i + 1)] for i in range(4))
        f_re = inside * (a_re * v_re - a_im * v_im + b_re * m_re - b_im * m_im)
        f_im = inside * (a_re * v_im + a_im * v_re + b_re * m_im + b_im * m_re)
        both = jnp.concatenate([f_re, f_im], axis=1)
        high = both.astype(BF16)
        low = (both - high.astype(F32)).astype(BF16)
        fitted = jnp.dot(
            expand[...], jnp.concatenate([high, low, high]), preferred_element_type=F32
        )
        start = pl.multiple_of(2 * t * FREQ_CHANNELS, FREQ_CHANNELS)
        mod_re = model[pl.ds(start, FREQ_CHANNELS), :].astype(F32) + fitted[:, 0:LANES]
        mod_im = model[pl.ds(start + FREQ_CHANNELS, FREQ_CHANNELS), :].astype(F32)
        mod_im = mod_im + fitted[:, LANES : 2 * LANES]
        obs_re, obs_im = get_sides()
        weight = tile_weights(groups, tiles, first_row, t, kept)
        left_re = weight * (obs_re - (prod_re * mod_re - prod_im * mod_im))
        left_im = weight * (obs_im - (prod_re * mod_im + prod_im * mod_re))
        left_out[0, 0, :, tile_lanes(t)] = left_re.astype(BF16)
        left_out[1, 0, :, tile_lanes(t)] = left_im.astype(BF16)

    def tile_late(t, carry):
        tile(t, lambda: late_sides(observed, rest, t))
        return carry

    def tile_early(t, carry):
        tile(t, lambda: early_sides(early, key, ahead, t - rest))
        return carry

    copies = []
    done = 0
    for part, size in enumerate(output_parts(tiles)):
        lax.fori_loop(done, done + size, tile_late if done < rest else tile_early, 0, unroll=size)
        lanes = pl.ds(done * LANES, size * LANES)
        copies.append(
            pltpu.make_async_copy(
                left_out.at[:, :, :, lanes], residual.at[:, :, :, lanes], out_sems.at[part]
            )
        )
        copies[-1].start()
        done += size
    hot = (
        lax.broadcasted_iota(jnp.int32, (stations, stations), 0) == order[...]
    ).astype(BF16)
    pieces = []
    for value in (gain_re, gain_im):
        high = value.astype(BF16).astype(F32)
        middle = (value - high).astype(BF16).astype(F32)
        pieces += [high, middle, value - high - middle]
    row16 = lax.broadcasted_iota(jnp.int32, (16, stations), 0)
    left = jnp.zeros((16, stations), F32)
    for at, piece in enumerate(pieces):
        left = jnp.where(row16 == at, piece, left)
    spread = lax.dot_general(
        left.astype(BF16), hot, (((1,), (1,)), ((), ())), preferred_element_type=F32
    )
    gains[0:1, :] = spread[0:1] + spread[1:2] + spread[2:3]
    gains[1:2, :] = spread[3:4] + spread[4:5] + spread[5:6]
    for copy in copies:
        copy.wait()


def call(kernel, out_shape, scratch, name, in_spaces, mib, flops=0, moved=0, out_specs=None):
    return pl.pallas_call(
        kernel,
        out_shape=out_shape,
        in_specs=[pl.BlockSpec(memory_space=space) for space in in_spaces],
        out_specs=out_specs or jax.tree.map(lambda _: pl.BlockSpec(memory_space=VMEM), out_shape),
        scratch_shapes=scratch,
        compiler_params=pltpu.CompilerParams(vmem_limit_bytes=mib << 20),
        cost_estimate=pl.CostEstimate(flops=flops, bytes_accessed=moved, transcendentals=0),
        name=name,
    )


def exchange(block, distance, wide):
    return lax.ppermute(block, "wide", [(i, i ^ distance) for i in range(wide)])


def gather_order(wide):
    order = [0, wide // 2, 3 * wide // 4, wide // 4]
    distance = wide // 8
    while distance:
        order += [place ^ distance for place in order]
        distance //= 2
    return order


def send_quarters(blocks, wide):
    quarter = wide // 4
    return [blocks[0]] + [exchange(blocks[at], at * quarter, wide) for at in (1, 2, 3)]


def exchange_early(held, wide, places, predicted):
    distance = wide // 8
    held, _ = lax.optimization_barrier((held, places))
    held = jnp.stack(held)
    while distance:
        split = held.reshape(held.shape[0], 2, distance, *held.shape[2:])
        other = exchange(split[:, 1], distance, wide)
        other, predicted = lax.optimization_barrier((other, predicted))
        held = jnp.stack([split[:, 0], other], axis=1)
        held = held.reshape(-1, distance, *held.shape[3:])
        distance //= 2
    return held[:, 0]


def gather_stats(stats, wide):
    held = jnp.stack([stats] + [exchange(stats, flip, wide) for flip in gather_order(wide)[1:4]])
    distance = wide // 8
    while distance:
        held = jnp.concatenate([held, exchange(held, distance, wide)])
        distance //= 2
    return held


def body(
    visibilities,
    kept_baseline_mask,
    fitted_mode_count,
    station_order,
    station_xy,
    comp_lm,
    comp_flux,
    centre_flux,
):
    wide = lax.axis_size("wide")
    local_chan = visibilities.shape[2]
    total = visibilities.shape[3]
    base = total // wide
    tiles = base // LANES
    padded = -(-tiles // 8) * 8
    stations = station_order.shape[0]
    groups = stations // GROUP
    comps = comp_lm.shape[1]
    rows = 2 * padded
    fit, expand = (jnp.asarray(table) for table in basis_tables())
    kept = kept_baseline_mask.reshape(total // LANES, LANES)
    counts = fitted_mode_count.reshape(tiles, LANES)

    ahead = early_tiles(tiles)
    blocks = visibilities.reshape(2, local_chan, wide, base).transpose(0, 2, 1, 3)
    hbm = pl.BlockSpec(memory_space=pltpu.MemorySpace.HBM)
    early_width = 2 * ahead * LANES + LANES
    early = pl.pallas_call(
        lambda *refs: pack_early_kernel(wide, base, *refs),
        out_shape=(jax.ShapeDtypeStruct((wide // 4, local_chan, early_width), BF16),) * 4,
        in_specs=[hbm] * 2,
        out_specs=(hbm,) * 4,
        scratch_shapes=[
            pltpu.VMEM((wide, local_chan, early_width), BF16),
            pltpu.SMEM((local_chan,), F32),
            pltpu.SemaphoreType.DMA((2,)),
            pltpu.SemaphoreType.DMA((wide,)),
            pltpu.SemaphoreType.DMA,
        ],
        compiler_params=pltpu.CompilerParams(vmem_limit_bytes=60 << 20),
        name="pack_early",
    )(blocks, centre_flux)
    late_width = 2 * (tiles - ahead) * LANES
    packed = pl.pallas_call(
        lambda *refs: pack_kernel(wide, base, *refs),
        out_shape=jax.ShapeDtypeStruct((wide, local_chan, late_width), BF16),
        in_specs=[hbm] * 2,
        out_specs=hbm,
        scratch_shapes=[
            pltpu.VMEM((wide, local_chan, late_width), BF16),
            pltpu.SemaphoreType.DMA((PACK_PARTS, 2)),
            pltpu.SemaphoreType.DMA((PACK_PARTS,)),
        ],
        compiler_params=pltpu.CompilerParams(vmem_limit_bytes=60 << 20),
        name="pack",
    )(blocks, early[0])
    early = send_quarters(early, wide)
    packed, early[1] = lax.optimization_barrier((packed, early[1]))
    observed = lax.all_to_all(packed, "wide", 0, 0, tiled=True)
    observed = observed.reshape(FREQ_CHANNELS // 8, 8, late_width)
    places = call(
        lambda *refs: places_kernel(groups, tiles, padded, *refs),
        (jax.ShapeDtypeStruct((rows + LANES, LANES), F32),) * 2,
        [],
        "places",
        [SMEM, SMEM, pltpu.MemorySpace.HBM],
        12,
        PLACES_FLOPS,
        (rows + LANES) * LANES * 8,
    )(station_order, station_xy.reshape(2, stations), packed)

    state_row = pltpu.VMEM((rows, comps), F32)
    state_col = pltpu.VMEM((comps, LANES), F32)
    left = pltpu.VMEM((UNROLL, 2 * rows, comps), BF16)
    right = pltpu.VMEM((UNROLL, comps, 2 * LANES), BF16)
    real, imag = call(
        lambda *refs: predict_kernel(groups, tiles, padded, *refs),
        (
            jax.ShapeDtypeStruct((tiles * FREQ_CHANNELS, LANES), F32),
            jax.ShapeDtypeStruct((tiles * FREQ_CHANNELS, LANES), BF16),
        ),
        [pltpu.VMEM((padded * FREQ_CHANNELS, LANES), F32)] * 2
        + [state_row] * 6
        + [state_col] * 6
        + [left, right, left, right],
        "predict",
        [VMEM] * 4,
        20,
        FREQ_CHANNELS * 2 * 2 * rows * 2 * comps * 256,
        padded * 256 * LANES * 4,
    )(*places, comp_lm, comp_flux.reshape(1, comps))
    early = exchange_early(early, wide, places[0], real)
    by_flip = local_chan == 8
    if not by_flip:
        early = early[lax.axis_index("wide") ^ jnp.arange(wide)]
        early = early.reshape(FREQ_CHANNELS // 8, 8, early_width)
    stats, model, modes = call(
        lambda *refs: stats_kernel(groups, tiles, by_flip, *refs),
        (
            jax.ShapeDtypeStruct((PAIRS * 2 * tiles, LANES), BF16),
            jax.ShapeDtypeStruct((tiles * 2 * FREQ_CHANNELS, LANES), BF16),
            jax.ShapeDtypeStruct((tiles * MODES, 4 * LANES), F32),
        ),
        [
            pltpu.VMEM((FREQ_CHANNELS, LANES), F32),
            pltpu.VMEM((tiles * 8, LANES), F32),
            pltpu.VMEM((PAIRS * 2 * tiles, LANES), F32),
        ],
        "stats",
        [VMEM] * 7,
        12,
        moved=tiles * 256 * LANES * 8,
    )(observed, early, real, imag, kept, counts, fit)
    gathered = gather_stats(stats, wide)
    gains, residual = call(
        lambda *refs: solve_kernel(groups, tiles, by_flip, wide, *refs),
        (
            jax.ShapeDtypeStruct((2, stations), F32),
            jax.ShapeDtypeStruct((2, 1, FREQ_CHANNELS, base), BF16),
        ),
        [
            pltpu.VMEM((PAIRS, wide * 2 * tiles, LANES), F32),
            pltpu.VMEM((STATS, stations, stations), F32),
            pltpu.VMEM((stations, 3 * stations), BF16),
            pltpu.VMEM((groups, 8, LANES), F32),
            pltpu.VMEM((groups, 8, LANES), F32),
            pltpu.VMEM((ROUNDS, stations, LANES), F32),
            pltpu.VMEM((ROUNDS, stations, LANES), F32),
            pltpu.VMEM((2, 1, FREQ_CHANNELS, base), BF16),
            pltpu.SemaphoreType.DMA((len(output_parts(tiles)),)),
        ],
        "solve",
        [VMEM] * 9,
        16,
        moved=tiles * 256 * LANES * 6,
        out_specs=(
            pl.BlockSpec(memory_space=VMEM),
            pl.BlockSpec(memory_space=pltpu.MemorySpace.HBM),
        ),
    )(
        gathered,
        observed,
        early,
        model,
        modes,
        kept,
        counts,
        station_order.reshape(1, stations),
        expand,
    )
    return gains, residual


def solution(mesh):
    placed = (
        P(None, None, ("band", "wide"), None),
        P("band"),
        P("wide"),
        P(),
        P(),
        P(),
        P(),
        P(("band", "wide")),
    )
    return jax.shard_map(
        body,
        mesh=mesh,
        in_specs=placed,
        out_specs=(P(None, "band"), P(None, None, "band", "wide")),
        check_vma=False,
    )
```

```python
import math

import jax
import jax.numpy as jnp
import numpy as np
from jax import lax
from jax.experimental import pallas as pl
from jax.experimental.pallas import tpu as pltpu
from jax.sharding import PartitionSpec as P

GROUP = 64
FREQ_CHANNELS = 128
MODES = 16
CAL_ITERS = 3
ROUNDS = 3
STATS = 7
PAIRS = 4
LANES = 128
UNROLL = 8
PACK_PARTS = 4
PLACES_FLOPS = 4 * 10**9
VMEM = pltpu.MemorySpace.VMEM
SMEM = pltpu.MemorySpace.SMEM
F32 = jnp.float32
BF16 = jnp.bfloat16


def row_groups_of(row, groups):
    block = row >> 6
    first = jnp.zeros_like(block)
    start = jnp.zeros_like(block)
    edge = 0
    for group in range(1, groups):
        edge += groups - group + 1
        past = (block >= edge).astype(jnp.int32)
        first = first + past
        start = start + past * (groups - group + 1)
    return first, block - start + first


def basis_tables():
    mid = np.arange(FREQ_CHANNELS)[:, None] + 0.5
    order = np.arange(MODES)[None, :]
    scale = np.where(order == 0, math.sqrt(1.0 / FREQ_CHANNELS), math.sqrt(2.0 / FREQ_CHANNELS))
    basis = (scale * np.cos(math.pi / FREQ_CHANNELS * mid * order)).astype(np.float32)
    high = basis.astype(BF16)
    low = (basis - high.astype(np.float32)).astype(BF16)
    return np.concatenate([high, low], axis=1).T, np.concatenate([high, high, low], axis=1)


def output_parts(tiles):
    sizes = []
    for left in (tiles - early_tiles(tiles), early_tiles(tiles)):
        while left:
            sizes.append(-(-left // 2))
            left -= sizes[-1]
    return sizes


def turn_trig(turns):
    quarter = jnp.floor(turns * 4.0 + 0.5)
    angle = (turns - 0.25 * quarter) * (2.0 * math.pi)
    square = angle * angle
    sine = angle * (
        1.0
        + square
        * (-1.0 / 6 + square * (1.0 / 120 + square * (-1.0 / 5040 + square * (1.0 / 362880))))
    )
    cosine = 1.0 + square * (
        -0.5
        + square
        * (1.0 / 24 + square * (-1.0 / 720 + square * (1.0 / 40320 + square * (-1.0 / 3628800))))
    )
    phase = quarter - 4.0 * jnp.floor(quarter * 0.25)
    odd = (phase == 1.0) | (phase == 3.0)
    cos_out = jnp.where(odd, sine, cosine)
    sin_out = jnp.where(odd, cosine, sine)
    cos_out = jnp.where((phase == 1.0) | (phase == 2.0), -cos_out, cos_out)
    sin_out = jnp.where(phase >= 2.0, -sin_out, sin_out)
    return cos_out, sin_out


def early_tiles(tiles):
    return tiles * 3 // 10


def pack_early_kernel(wide, base, source, *rest):
    targets, (held, in_sems, out_sems) = rest[:4], rest[4:]
    rank = lax.axis_index("wide")
    quarter = wide // 4
    late = base - early_tiles(base // LANES) * LANES
    size = base - late
    bring = [
        pltpu.make_async_copy(
            source.at[side, :, :, pl.ds(late, size)],
            held.at[:, :, pl.ds(side * size, size)],
            in_sems.at[side],
        )
        for side in range(2)
    ]
    for copy in bring:
        copy.start()
    for copy in bring:
        copy.wait()
    send = [
        pltpu.make_async_copy(
            held.at[rank ^ flip], targets[flip // quarter].at[flip % quarter], out_sems.at[flip]
        )
        for flip in range(wide)
    ]
    for copy in send:
        copy.start()
    for copy in send:
        copy.wait()


def pack_kernel(wide, base, source, centre, after, target, held, flux, in_sems, out_sems, flux_sem):
    del after
    chan = centre.shape[0]
    size = base - early_tiles(base // LANES) * LANES
    share = wide // PACK_PARTS
    peers = [pl.ds(part * share, share) for part in range(PACK_PARTS)]
    bring = [
        [
            pltpu.make_async_copy(
                source.at[side, peers[part], :, pl.ds(0, size)],
                held.at[peers[part], :, pl.ds(side * size, size)],
                in_sems.at[part, side],
            )
            for side in range(2)
        ]
        for part in range(PACK_PARTS)
    ]
    send = [
        pltpu.make_async_copy(held.at[peers[part]], target.at[peers[part]], out_sems.at[part])
        for part in range(PACK_PARTS)
    ]
    fetch = pltpu.make_async_copy(centre, flux, flux_sem)
    fetch.start()
    for pair in bring:
        for copy in pair:
            copy.start()
    fetch.wait()
    row = lax.broadcasted_iota(jnp.int32, (chan, LANES), 0)
    lane = lax.broadcasted_iota(jnp.int32, (chan, LANES), 1)
    value = jnp.zeros(row.shape, F32)
    for c in range(chan):
        value = jnp.where(row == c, flux[c], value)
    high = value.astype(BF16).astype(F32)
    middle = (value - high).astype(BF16).astype(F32)
    low = value - high - middle
    parts = jnp.where(lane == 0, high, jnp.where(lane == 1, middle, jnp.where(lane == 2, low, 0.0)))
    held[:, :, 2 * size : 2 * size + LANES] = jnp.broadcast_to(
        parts.astype(BF16)[None], (wide, chan, LANES)
    )
    for pair, copy in zip(bring, send):
        for came in pair:
            came.wait()
        copy.start()
    for copy in send:
        copy.wait()


def column_groups(groups, tiles, first_row):
    last_row = first_row + (2 * tiles - 1)
    return [row_groups_of(row, groups)[1] * GROUP for row in (first_row, last_row)]


def places_kernel(groups, tiles, padded, order, xy, after, pos_x, pos_y):
    del after
    first_row = lax.axis_index("wide") * (2 * tiles)
    col_a, col_b = column_groups(groups, tiles, first_row)
    pos_x[...] = jnp.zeros_like(pos_x)
    pos_y[...] = jnp.zeros_like(pos_y)

    def place(slot, position):
        station = order[position]
        pos_x[pl.ds(slot, 1), :] = jnp.full((1, LANES), xy[0, station], F32)
        pos_y[pl.ds(slot, 1), :] = jnp.full((1, LANES), xy[1, station], F32)

    def place_row(t, carry):
        for half in range(2):
            row = first_row + 2 * t + half
            place(half * padded + t, row_groups_of(row, groups)[0] * GROUP + (row & 63))
        return carry

    def place_col(j, carry):
        place(2 * padded + j, col_a + j)
        place(2 * padded + GROUP + j, col_b + j)
        return carry

    lax.fori_loop(0, tiles, place_row, 0, unroll=10)
    lax.fori_loop(0, GROUP, place_col, 0, unroll=16)


def predict_kernel(
    groups,
    tiles,
    padded,
    pos_x,
    pos_y,
    lm,
    flux,
    real_out,
    imag_out,
    real,
    imag,
    row_c,
    row_s,
    row_dc,
    row_ds,
    row_lc,
    row_ls,
    col_c,
    col_s,
    col_dc,
    col_ds,
    col_lc,
    col_ls,
    left_a,
    right_a,
    left_b,
    right_b,
):
    comps = lm.shape[1]
    first_row = lax.axis_index("wide") * (2 * tiles)
    edge = jnp.minimum((((first_row >> 6) + 1) * GROUP - first_row) >> 1, tiles)
    step = 0.25 / FREQ_CHANNELS
    rows = 2 * padded
    weight = flux[...] * (1.0 / math.sqrt(comps))
    for k in range(0, comps, LANES):
        lane = slice(k, k + LANES)
        axis_l = lm[0:1, lane]
        axis_m = lm[1:2, lane]
        turns = pos_x[0:rows, :] * axis_l + pos_y[0:rows, :] * axis_m
        cosine, sine = turn_trig(turns)
        row_c[:, lane] = cosine * weight[:, lane]
        row_s[:, lane] = sine * weight[:, lane]
        row_dc[:, lane], row_ds[:, lane] = turn_trig(turns * step)
        row_lc[:, lane], row_ls[:, lane] = turn_trig(turns * (UNROLL * step))
        turns = (
            pos_x[rows : rows + LANES, :] * axis_l + pos_y[rows : rows + LANES, :] * axis_m
        ).T
        col_c[lane, :], col_s[lane, :] = turn_trig(turns)
        col_dc[lane, :], col_ds[lane, :] = turn_trig(turns * step)
        col_lc[lane, :], col_ls[lane, :] = turn_trig(turns * (UNROLL * step))

    def channels(c, s, dc, ds, leap_c, leap_s):
        twice = dc + dc
        out = [(c, s), (c * dc - s * ds, s * dc + c * ds)]
        while len(out) < UNROLL:
            out.append(tuple(twice * now - before for now, before in zip(out[-1], out[-2])))
        return out, (c * leap_c - s * leap_s, s * leap_c + c * leap_s)

    def fill_col(right, k):
        part = slice(k, k + 16)
        state = [table[part, :] for table in (col_c, col_s, col_dc, col_ds, col_lc, col_ls)]
        values, (col_c[part, :], col_s[part, :]) = channels(*state)
        for u, (c, s) in enumerate(values):
            right[u, part, 0:LANES] = c.astype(BF16)
            right[u, part, LANES : 2 * LANES] = s.astype(BF16)

    def fill_row(left, r, k):
        part, low = slice(r, r + 16), slice(rows + r, rows + r + 16)
        lane = slice(k, k + LANES)
        state = [table[part, lane] for table in (row_c, row_s, row_dc, row_ds, row_lc, row_ls)]
        values, (row_c[part, lane], row_s[part, lane]) = channels(*state)
        for u, (c, s) in enumerate(values):
            left[u, part, lane] = c.astype(BF16)
            left[u, low, lane] = s.astype(BF16)

    def fill_steps(left, right):
        steps = [lambda k=k: fill_col(right, k) for k in range(0, comps, 16)]
        return steps + [
            lambda r=r, k=k: fill_row(left, r, k)
            for r in range(0, rows, 16)
            for k in range(0, comps, LANES)
        ]

    first_half = lax.broadcasted_iota(jnp.int32, (padded, LANES), 1) < GROUP
    in_a = lax.broadcasted_iota(jnp.int32, (padded, LANES), 0) < edge

    def multiply(left, right, group, u):
        product = jnp.dot(left[u], right[u], preferred_element_type=F32)
        channel = group * UNROLL + u
        with_cos, with_sin = product[:, 0:LANES], product[:, LANES : 2 * LANES]
        sums = (
            (with_cos[0:rows] + with_sin[rows : 2 * rows], real),
            (with_cos[rows : 2 * rows] - with_sin[0:rows], imag),
        )
        for side, out in sums:
            even, odd = side[0:padded], side[padded : 2 * padded]
            even = jnp.where(in_a, even, pltpu.roll(even, GROUP, 1))
            odd = jnp.where(in_a, pltpu.roll(odd, GROUP, 1), odd)
            out[pl.ds(channel, padded, stride=FREQ_CHANNELS), :] = jnp.where(first_half, even, odd)

    for step in fill_steps(left_a, right_a):
        step()

    def group_pass(now, later, group):
        steps = fill_steps(*later)
        share = -(-len(steps) // UNROLL)
        for u in range(UNROLL):
            multiply(*now, group, u)
            for step in steps[u * share : (u + 1) * share]:
                step()

    def two_groups(pair, carry):
        group_pass((left_a, right_a), (left_b, right_b), 2 * pair)
        group_pass((left_b, right_b), (left_a, right_a), 2 * pair + 1)
        return carry

    lax.fori_loop(0, FREQ_CHANNELS // (2 * UNROLL), two_groups, 0)
    size = tiles * FREQ_CHANNELS
    real_out[...] = real[0:size, :]
    imag_out[...] = imag[0:size, :].astype(BF16)


def tile_weights(groups, tiles, first_row, t, kept):
    lane = lax.broadcasted_iota(jnp.int32, (1, LANES), 1)
    row = first_row + 2 * t
    first, second = row_groups_of(row, groups)
    inside = (row & 63) + (lane >> 6)
    usable = (first != second) | (inside < (lane & 63))
    mask = kept[pl.ds((first_row >> 1) + t, 1), :].astype(F32)
    return jnp.where(usable, mask, 0.0)


def tile_lanes(t, size=LANES, offset=0):
    return pl.ds(pl.multiple_of(offset + t * size, size), size)


def late_sides(observed, tiles, t):
    return [
        observed[:, :, tile_lanes(t, LANES, side * tiles * LANES)]
        .astype(F32)
        .reshape(FREQ_CHANNELS, LANES)
        for side in range(2)
    ]


def early_lanes(early, key, lanes):
    blocks = [early[key ^ at, :, lanes].astype(F32) for at in range(early.shape[0])]
    return jnp.concatenate(blocks)


def early_sides(early, key, tiles, t):
    return [early_lanes(early, key, tile_lanes(t, LANES, side * tiles * LANES)) for side in range(2)]


def tile_stats(groups, tiles, begin, count, sides_of, shift, real, imag, kept, counts, fit, model, modes, rows):
    first_row = lax.axis_index("wide") * (2 * tiles)
    mode = lax.broadcasted_iota(jnp.int32, (MODES, LANES), 0)

    def one(at, carry):
        t = begin + at
        obs_re, obs_im = sides_of(at)
        half = tile_lanes(t, FREQ_CHANNELS)
        mod_re16, mod_im16 = (real[half, :] + shift[...]).astype(BF16), imag[half, :]
        both = pl.multiple_of(2 * at * FREQ_CHANNELS, FREQ_CHANNELS)
        model[pl.ds(both, FREQ_CHANNELS), :] = mod_re16
        model[pl.ds(both + FREQ_CHANNELS, FREQ_CHANNELS), :] = mod_im16
        mod_re, mod_im = mod_re16.astype(F32), mod_im16.astype(F32)

        def total(terms):
            return jnp.sum(terms, axis=0, keepdims=True)

        cross_re = total(obs_re * mod_re + obs_im * mod_im)
        cross_im = total(obs_im * mod_re - obs_re * mod_im)
        power = total(mod_re * mod_re + mod_im * mod_im)
        sides = [obs_re.astype(BF16), obs_im.astype(BF16), mod_re16, mod_im16]
        raw = jnp.dot(fit[...], jnp.concatenate(sides, axis=1), preferred_element_type=F32)
        raw = raw[0:MODES] + raw[MODES : 2 * MODES]
        modes[tile_lanes(at, MODES), :] = raw
        v_re, v_im, m_re, m_im = (raw[:, LANES * i : LANES * (i + 1)] for i in range(4))
        inside = (mode < counts[pl.ds(t, 1), :]).astype(F32)
        vv = total(inside * (v_re * v_re + v_im * v_im))
        vm_re = total(inside * (v_re * m_re + v_im * m_im))
        vm_im = total(inside * (v_im * m_re - v_re * m_im))
        mm = total(inside * (m_re * m_re + m_im * m_im))
        weight = tile_weights(groups, tiles, first_row, t, kept)
        parts = [cross_re, cross_im, vv, vm_re, vm_im, power, mm, jnp.zeros((1, LANES), F32)]
        rows[tile_lanes(at, 8), :] = jnp.concatenate(parts) * weight
        return carry

    lax.fori_loop(0, count, one, 0, unroll=count)


def late_stats_kernel(
    groups, tiles, observed, real, imag, kept, counts, fit, rows, model, modes, shift
):
    rest = tiles - early_tiles(tiles)
    tail = observed[:, :, 2 * rest * LANES : (2 * rest + 1) * LANES].astype(F32)
    tail = tail.reshape(FREQ_CHANNELS, LANES)
    shift[...] = jnp.broadcast_to(jnp.sum(tail, axis=1, keepdims=True), tail.shape)

    def sides(at):
        return late_sides(observed, rest, at)

    tile_stats(groups, tiles, 0, rest, sides, shift, real, imag, kept, counts, fit, model, modes, rows)


def early_stats_kernel(
    groups,
    tiles,
    by_flip,
    early,
    late_rows,
    shift,
    real,
    imag,
    kept,
    counts,
    fit,
    stats,
    model,
    modes,
    rows,
    paired,
):
    key = lax.axis_index("wide") if by_flip else 0
    ahead = early_tiles(tiles)
    rest = tiles - ahead
    rows[0 : 8 * rest, :] = late_rows[...]

    def sides(at):
        return early_sides(early, key, ahead, at)

    late = rows.at[8 * rest : 8 * tiles]
    tile_stats(groups, tiles, rest, ahead, sides, shift, real, imag, kept, counts, fit, model, modes, late)
    first_half = lax.broadcasted_iota(jnp.int32, (tiles, LANES), 1) < GROUP
    for pair in range(PAIRS):
        one_stat = rows[pl.ds(2 * pair, tiles, stride=8), :]
        other = rows[pl.ds(2 * pair + 1, tiles, stride=8), :]
        even = jnp.where(first_half, one_stat, pltpu.roll(other, GROUP, 1))
        odd = jnp.where(first_half, pltpu.roll(one_stat, GROUP, 1), other)
        paired[pl.ds(2 * tiles * pair, tiles, stride=2), :] = even
        paired[pl.ds(2 * tiles * pair + 1, tiles, stride=2), :] = odd
    stats[...] = paired[...].astype(BF16)


def solve_kernel(
    groups,
    tiles,
    by_flip,
    wide,
    gathered,
    observed,
    early,
    late_model,
    early_model,
    late_modes,
    early_modes,
    kept,
    counts,
    order,
    expand,
    gains,
    residual,
    flat,
    full,
    weights,
    row_gain_re,
    row_gain_im,
    col_gain_re,
    col_gain_im,
    left_out,
    out_sems,
):
    stations = groups * GROUP
    rank = lax.axis_index("wide")
    first_row = rank * (2 * tiles)
    halves = stations // LANES
    count = 2 * tiles
    for k, flip in enumerate(gather_order(wide)):
        start = pl.multiple_of((rank ^ flip) * count, count & -count)
        values = gathered[k].astype(F32)
        for pair in range(PAIRS):
            flat[pair, pl.ds(start, count), :] = values[pair * count : (pair + 1) * count]
    block_id = {}
    for first in range(groups):
        for second in range(first, groups):
            block_id[first, second] = len(block_id)
    lane64 = lax.broadcasted_iota(jnp.int32, (GROUP, LANES), 1) < GROUP

    def placed_block(stat, first, half):
        pair, side = stat // 2, stat % 2
        sides = []
        for at in range(2):
            index = block_id.get((first, 2 * half + at))
            if index is None:
                sides.append(jnp.zeros((GROUP, LANES), F32))
                continue
            block = flat[pair, GROUP * index : GROUP * (index + 1), :]
            sides.append(block if at == side else pltpu.roll(block, GROUP, 1))
        return jnp.where(lane64, sides[0], sides[1])

    for stat in range(STATS):
        sign = -1.0 if stat in (1, 4) else 1.0
        for a in range(halves):
            rows_a = slice(LANES * a, LANES * (a + 1))
            for b in range(a, halves):
                rows_b = slice(LANES * b, LANES * (b + 1))
                block = jnp.concatenate([placed_block(stat, 2 * a + i, b) for i in range(2)])
                turned = block.T * sign
                if a == b:
                    full[stat, rows_a, rows_a] = block + turned
                else:
                    full[stat, rows_a, rows_b] = block
                    full[stat, rows_b, rows_a] = turned

    gain_re = jnp.ones((1, stations), F32)
    gain_im = jnp.zeros((1, stations), F32)
    for round_id in range(ROUNDS):

        def build(step, carry):
            rows = pl.ds(pl.multiple_of(step * 16, 16), 16)
            vm_re, vm_im, mm = full[3, rows, :], full[4, rows, :], full[6, rows, :]
            if round_id == 0:
                cross_re, cross_im, power = full[0, rows, :], full[1, rows, :], full[5, rows, :]
                full[0, rows, :] = cross_re - vm_re
                full[1, rows, :] = cross_im - vm_im
                full[5, rows, :] = power - mm
            else:
                vv = full[2, rows, :]
                col_re = jnp.concatenate([col_gain_re[round_id - 1, rows, :]] * halves, axis=1)
                col_im = jnp.concatenate([col_gain_im[round_id - 1, rows, :]] * halves, axis=1)
                rest_re = 1.0 - (col_re * gain_re + col_im * gain_im)
                rest_im = col_re * gain_im - col_im * gain_re
                turn_re = rest_re * vm_re + rest_im * vm_im
                turn_im = rest_re * vm_im - rest_im * vm_re
                mm = vv + (rest_re * rest_re + rest_im * rest_im) * mm + (turn_re + turn_re)
                vm_re, vm_im = vv + turn_re, turn_im
                if round_id + 1 < ROUNDS:
                    full[3, rows, :], full[4, rows, :], full[6, rows, :] = vm_re, vm_im, mm
                cross_re, cross_im = full[0, rows, :] + vm_re, full[1, rows, :] + vm_im
                power = full[5, rows, :] + mm
            for part, value in enumerate((cross_re, cross_im, power)):
                weights[rows, part * stations : (part + 1) * stations] = value.astype(BF16)
            return carry

        lax.fori_loop(0, stations // 16, build, 0, unroll=4)
        row8 = lax.broadcasted_iota(jnp.int32, (8, stations), 0)
        for iteration in range(CAL_ITERS):
            norm = gain_re * gain_re + gain_im * gain_im
            left = jnp.where(row8 == 0, gain_re, jnp.where(row8 == 1, gain_im, norm))
            high = left.astype(BF16).astype(F32)
            left = jnp.concatenate([high, left - high]).astype(BF16)
            raw = jnp.dot(left, weights[...], preferred_element_type=F32)
            raw = raw[0:8] + raw[8:16]
            with_re, with_im = raw[:, 0:stations], raw[:, stations : 2 * stations]
            below = raw[2:3, 2 * stations : 3 * stations]
            next_re = (with_re[0:1] + with_im[1:2]) / below
            next_im = (with_re[1:2] - with_im[0:1]) / below
            if iteration % 2 == 1:
                next_re = 0.5 * (next_re + gain_re)
                next_im = 0.5 * (next_im + gain_im)
            gain_re, gain_im = next_re, next_im
        lane1 = lax.broadcasted_iota(jnp.int32, (1, LANES), 1) < GROUP
        for value, row_gain, col_gain in (
            (gain_re, row_gain_re, col_gain_re),
            (gain_im, row_gain_im, col_gain_im),
        ):
            for half in range(halves):
                part = value[:, LANES * half : LANES * (half + 1)]
                turned = pltpu.roll(jnp.broadcast_to(part, (8, LANES)), GROUP, 1)[0:1]
                row_gain[2 * half, round_id : round_id + 1, :] = jnp.where(lane1, part, turned)
                row_gain[2 * half + 1, round_id : round_id + 1, :] = jnp.where(lane1, turned, part)
                col_gain[round_id, LANES * half : LANES * (half + 1), :] = jnp.broadcast_to(
                    part, (LANES, LANES)
                ).T

    mode = lax.broadcasted_iota(jnp.int32, (MODES, LANES), 0)
    lane_half = lax.broadcasted_iota(jnp.int32, (1, LANES), 1) < GROUP

    key = rank if by_flip else 0
    ahead = early_tiles(tiles)
    rest = tiles - ahead

    def tile(t, at, get_sides, model, modes):
        row = first_row + 2 * t
        first, second = row_groups_of(row, groups)
        station = first * GROUP + (row & 63)

        def row_side(table, round_id):
            low, high = table[round_id, pl.ds(station, 1), :], table[round_id, pl.ds(station + 1, 1), :]
            return jnp.where(lane_half, low, high)

        q_res, q_ims = row_gain_re[second], row_gain_im[second]
        a_re, a_im = jnp.zeros((1, LANES), F32), jnp.zeros((1, LANES), F32)
        b_re, b_im = jnp.ones((1, LANES), F32), jnp.zeros((1, LANES), F32)
        for round_id in range(ROUNDS):
            p_re, p_im = row_side(col_gain_re, round_id), row_side(col_gain_im, round_id)
            q_re, q_im = q_res[round_id : round_id + 1], q_ims[round_id : round_id + 1]
            prod_re = p_re * q_re + p_im * q_im
            prod_im = p_im * q_re - p_re * q_im
            if round_id + 1 == ROUNDS:
                break
            rest_re, rest_im = 1.0 - prod_re, -prod_im
            a_re, a_im = 1.0 + rest_re * a_re - rest_im * a_im, rest_re * a_im + rest_im * a_re
            b_re, b_im = rest_re * b_re - rest_im * b_im, rest_re * b_im + rest_im * b_re
        b_re = b_re - 1.0
        inside = (mode < counts[pl.ds(t, 1), :]).astype(F32)
        raw = modes[tile_lanes(at, MODES), :]
        v_re, v_im, m_re, m_im = (raw[:, LANES * i : LANES * (i + 1)] for i in range(4))
        f_re = inside * (a_re * v_re - a_im * v_im + b_re * m_re - b_im * m_im)
        f_im = inside * (a_re * v_im + a_im * v_re + b_re * m_im + b_im * m_re)
        both = jnp.concatenate([f_re, f_im], axis=1)
        high = both.astype(BF16)
        low = (both - high.astype(F32)).astype(BF16)
        fitted = jnp.dot(
            expand[...], jnp.concatenate([high, low, high]), preferred_element_type=F32
        )
        start = pl.multiple_of(2 * at * FREQ_CHANNELS, FREQ_CHANNELS)
        mod_re = model[pl.ds(start, FREQ_CHANNELS), :].astype(F32) + fitted[:, 0:LANES]
        mod_im = model[pl.ds(start + FREQ_CHANNELS, FREQ_CHANNELS), :].astype(F32)
        mod_im = mod_im + fitted[:, LANES : 2 * LANES]
        obs_re, obs_im = get_sides()
        weight = tile_weights(groups, tiles, first_row, t, kept)
        left_re = weight * (obs_re - (prod_re * mod_re - prod_im * mod_im))
        left_im = weight * (obs_im - (prod_re * mod_im + prod_im * mod_re))
        left_out[0, 0, :, tile_lanes(t)] = left_re.astype(BF16)
        left_out[1, 0, :, tile_lanes(t)] = left_im.astype(BF16)

    def tile_late(t, carry):
        tile(t, t, lambda: late_sides(observed, rest, t), late_model, late_modes)
        return carry

    def tile_early(t, carry):
        at = t - rest
        tile(t, at, lambda: early_sides(early, key, ahead, at), early_model, early_modes)
        return carry

    copies = []
    done = 0
    for part, size in enumerate(output_parts(tiles)):
        lax.fori_loop(done, done + size, tile_late if done < rest else tile_early, 0, unroll=size)
        lanes = pl.ds(done * LANES, size * LANES)
        copies.append(
            pltpu.make_async_copy(
                left_out.at[:, :, :, lanes], residual.at[:, :, :, lanes], out_sems.at[part]
            )
        )
        copies[-1].start()
        done += size
    hot = (
        lax.broadcasted_iota(jnp.int32, (stations, stations), 0) == order[...]
    ).astype(BF16)
    pieces = []
    for value in (gain_re, gain_im):
        high = value.astype(BF16).astype(F32)
        middle = (value - high).astype(BF16).astype(F32)
        pieces += [high, middle, value - high - middle]
    row16 = lax.broadcasted_iota(jnp.int32, (16, stations), 0)
    left = jnp.zeros((16, stations), F32)
    for at, piece in enumerate(pieces):
        left = jnp.where(row16 == at, piece, left)
    spread = lax.dot_general(
        left.astype(BF16), hot, (((1,), (1,)), ((), ())), preferred_element_type=F32
    )
    gains[0:1, :] = spread[0:1] + spread[1:2] + spread[2:3]
    gains[1:2, :] = spread[3:4] + spread[4:5] + spread[5:6]
    for copy in copies:
        copy.wait()


def call(kernel, out_shape, scratch, name, in_spaces, mib, flops=0, moved=0, out_specs=None):
    return pl.pallas_call(
        kernel,
        out_shape=out_shape,
        in_specs=[pl.BlockSpec(memory_space=space) for space in in_spaces],
        out_specs=out_specs or jax.tree.map(lambda _: pl.BlockSpec(memory_space=VMEM), out_shape),
        scratch_shapes=scratch,
        compiler_params=pltpu.CompilerParams(vmem_limit_bytes=mib << 20),
        cost_estimate=pl.CostEstimate(flops=flops, bytes_accessed=moved, transcendentals=0),
        name=name,
    )


def exchange(block, distance, wide):
    return lax.ppermute(block, "wide", [(i, i ^ distance) for i in range(wide)])


def gather_order(wide):
    order = [0, wide // 2, 3 * wide // 4, wide // 4]
    distance = wide // 8
    while distance:
        order += [place ^ distance for place in order]
        distance //= 2
    return order


def send_quarters(blocks, wide):
    quarter = wide // 4
    return [blocks[0]] + [exchange(blocks[at], at * quarter, wide) for at in (1, 2, 3)]


def exchange_early(held, wide, places, predicted):
    distance = wide // 8
    held, _ = lax.optimization_barrier((held, places))
    held = jnp.stack(held)
    while distance:
        split = held.reshape(held.shape[0], 2, distance, *held.shape[2:])
        other = exchange(split[:, 1], distance, wide)
        other, predicted = lax.optimization_barrier((other, predicted))
        held = jnp.stack([split[:, 0], other], axis=1)
        held = held.reshape(-1, distance, *held.shape[3:])
        distance //= 2
    return held[:, 0]


def gather_stats(stats, wide):
    held = jnp.stack([stats] + [exchange(stats, flip, wide) for flip in gather_order(wide)[1:4]])
    distance = wide // 8
    while distance:
        held = jnp.concatenate([held, exchange(held, distance, wide)])
        distance //= 2
    return held


def body(
    visibilities,
    kept_baseline_mask,
    fitted_mode_count,
    station_order,
    station_xy,
    comp_lm,
    comp_flux,
    centre_flux,
):
    wide = lax.axis_size("wide")
    local_chan = visibilities.shape[2]
    total = visibilities.shape[3]
    base = total // wide
    tiles = base // LANES
    padded = -(-tiles // 8) * 8
    stations = station_order.shape[0]
    groups = stations // GROUP
    comps = comp_lm.shape[1]
    rows = 2 * padded
    fit, expand = (jnp.asarray(table) for table in basis_tables())
    kept = kept_baseline_mask.reshape(total // LANES, LANES)
    counts = fitted_mode_count.reshape(tiles, LANES)

    ahead = early_tiles(tiles)
    blocks = visibilities.reshape(2, local_chan, wide, base).transpose(0, 2, 1, 3)
    hbm = pl.BlockSpec(memory_space=pltpu.MemorySpace.HBM)
    early_width = 2 * ahead * LANES
    early = pl.pallas_call(
        lambda *refs: pack_early_kernel(wide, base, *refs),
        out_shape=(jax.ShapeDtypeStruct((wide // 4, local_chan, early_width), BF16),) * 4,
        in_specs=[hbm],
        out_specs=(hbm,) * 4,
        scratch_shapes=[
            pltpu.VMEM((wide, local_chan, early_width), BF16),
            pltpu.SemaphoreType.DMA((2,)),
            pltpu.SemaphoreType.DMA((wide,)),
        ],
        compiler_params=pltpu.CompilerParams(vmem_limit_bytes=60 << 20),
        name="pack_early",
    )(blocks)
    late_width = 2 * (tiles - ahead) * LANES + LANES
    packed = pl.pallas_call(
        lambda *refs: pack_kernel(wide, base, *refs),
        out_shape=jax.ShapeDtypeStruct((wide, local_chan, late_width), BF16),
        in_specs=[hbm] * 3,
        out_specs=hbm,
        scratch_shapes=[
            pltpu.VMEM((wide, local_chan, late_width), BF16),
            pltpu.SMEM((local_chan,), F32),
            pltpu.SemaphoreType.DMA((PACK_PARTS, 2)),
            pltpu.SemaphoreType.DMA((PACK_PARTS,)),
            pltpu.SemaphoreType.DMA,
        ],
        compiler_params=pltpu.CompilerParams(vmem_limit_bytes=60 << 20),
        name="pack",
    )(blocks, centre_flux, early[0])
    early = send_quarters(early, wide)
    packed, early[1] = lax.optimization_barrier((packed, early[1]))
    observed = lax.all_to_all(packed, "wide", 0, 0, tiled=True)
    observed = observed.reshape(FREQ_CHANNELS // 8, 8, late_width)
    places = call(
        lambda *refs: places_kernel(groups, tiles, padded, *refs),
        (jax.ShapeDtypeStruct((rows + LANES, LANES), F32),) * 2,
        [],
        "places",
        [SMEM, SMEM, pltpu.MemorySpace.HBM],
        12,
        PLACES_FLOPS,
        (rows + LANES) * LANES * 8,
    )(station_order, station_xy.reshape(2, stations), packed)

    state_row = pltpu.VMEM((rows, comps), F32)
    state_col = pltpu.VMEM((comps, LANES), F32)
    left = pltpu.VMEM((UNROLL, 2 * rows, comps), BF16)
    right = pltpu.VMEM((UNROLL, comps, 2 * LANES), BF16)
    real, imag = call(
        lambda *refs: predict_kernel(groups, tiles, padded, *refs),
        (
            jax.ShapeDtypeStruct((tiles * FREQ_CHANNELS, LANES), F32),
            jax.ShapeDtypeStruct((tiles * FREQ_CHANNELS, LANES), BF16),
        ),
        [pltpu.VMEM((padded * FREQ_CHANNELS, LANES), F32)] * 2
        + [state_row] * 6
        + [state_col] * 6
        + [left, right, left, right],
        "predict",
        [VMEM] * 4,
        20,
        FREQ_CHANNELS * 2 * 2 * rows * 2 * comps * 256,
        padded * 256 * LANES * 4,
    )(*places, comp_lm, comp_flux.reshape(1, comps))
    early = exchange_early(early, wide, places[0], real)
    by_flip = local_chan == 8
    if not by_flip:
        early = early[lax.axis_index("wide") ^ jnp.arange(wide)]
        early = early.reshape(FREQ_CHANNELS // 8, 8, early_width)

    def tables(count):
        return (
            jax.ShapeDtypeStruct((count * 2 * FREQ_CHANNELS, LANES), BF16),
            jax.ShapeDtypeStruct((count * MODES, 4 * LANES), F32),
        )

    rest = tiles - ahead
    late_rows, late_model, late_modes, shift = call(
        lambda *refs: late_stats_kernel(groups, tiles, *refs),
        (
            jax.ShapeDtypeStruct((rest * 8, LANES), F32),
            *tables(rest),
            jax.ShapeDtypeStruct((FREQ_CHANNELS, LANES), F32),
        ),
        [],
        "late_stats",
        [VMEM] * 6,
        12,
        moved=rest * 256 * LANES * 8,
    )(observed, real, imag, kept, counts, fit)
    stats, early_model, early_modes = call(
        lambda *refs: early_stats_kernel(groups, tiles, by_flip, *refs),
        (jax.ShapeDtypeStruct((PAIRS * 2 * tiles, LANES), BF16), *tables(ahead)),
        [pltpu.VMEM((tiles * 8, LANES), F32), pltpu.VMEM((PAIRS * 2 * tiles, LANES), F32)],
        "early_stats",
        [VMEM] * 8,
        12,
        moved=ahead * 256 * LANES * 8,
    )(early, late_rows, shift, real, imag, kept, counts, fit)
    gathered = gather_stats(stats, wide)
    gains, residual = call(
        lambda *refs: solve_kernel(groups, tiles, by_flip, wide, *refs),
        (
            jax.ShapeDtypeStruct((2, stations), F32),
            jax.ShapeDtypeStruct((2, 1, FREQ_CHANNELS, base), BF16),
        ),
        [
            pltpu.VMEM((PAIRS, wide * 2 * tiles, LANES), F32),
            pltpu.VMEM((STATS, stations, stations), F32),
            pltpu.VMEM((stations, 3 * stations), BF16),
            pltpu.VMEM((groups, 8, LANES), F32),
            pltpu.VMEM((groups, 8, LANES), F32),
            pltpu.VMEM((ROUNDS, stations, LANES), F32),
            pltpu.VMEM((ROUNDS, stations, LANES), F32),
            pltpu.VMEM((2, 1, FREQ_CHANNELS, base), BF16),
            pltpu.SemaphoreType.DMA((len(output_parts(tiles)),)),
        ],
        "solve",
        [VMEM] * 11,
        16,
        moved=tiles * 256 * LANES * 6,
        out_specs=(
            pl.BlockSpec(memory_space=VMEM),
            pl.BlockSpec(memory_space=pltpu.MemorySpace.HBM),
        ),
    )(
        gathered,
        observed,
        early,
        late_model,
        early_model,
        late_modes,
        early_modes,
        kept,
        counts,
        station_order.reshape(1, stations),
        expand,
    )
    return gains, residual


def solution(mesh):
    placed = (
        P(None, None, ("band", "wide"), None),
        P("band"),
        P("wide"),
        P(),
        P(),
        P(),
        P(),
        P(("band", "wide")),
    )
    return jax.shard_map(
        body,
        mesh=mesh,
        in_specs=placed,
        out_specs=(P(None, "band"), P(None, None, "band", "wide")),
        check_vma=False,
    )
```

```python
import math

import jax
import jax.numpy as jnp
import numpy as np
from jax import lax
from jax.experimental import pallas as pl
from jax.experimental.pallas import tpu as pltpu
from jax.sharding import PartitionSpec as P

GROUP = 64
FREQ_CHANNELS = 128
MODES = 16
CAL_ITERS = 3
ROUNDS = 3
STATS = 7
PAIRS = 4
LANES = 128
UNROLL = 8
PACK_PARTS = 4
PLACES_FLOPS = 4 * 10**9
VMEM = pltpu.MemorySpace.VMEM
SMEM = pltpu.MemorySpace.SMEM
F32 = jnp.float32
BF16 = jnp.bfloat16


def row_groups_of(row, groups):
    block = row >> 6
    first = jnp.zeros_like(block)
    start = jnp.zeros_like(block)
    edge = 0
    for group in range(1, groups):
        edge += groups - group + 1
        past = (block >= edge).astype(jnp.int32)
        first = first + past
        start = start + past * (groups - group + 1)
    return first, block - start + first


def basis_tables():
    mid = np.arange(FREQ_CHANNELS)[:, None] + 0.5
    order = np.arange(MODES)[None, :]
    scale = np.where(order == 0, math.sqrt(1.0 / FREQ_CHANNELS), math.sqrt(2.0 / FREQ_CHANNELS))
    basis = (scale * np.cos(math.pi / FREQ_CHANNELS * mid * order)).astype(np.float32)
    high = basis.astype(BF16)
    low = (basis - high.astype(np.float32)).astype(BF16)
    return np.concatenate([high, low], axis=1).T, np.concatenate([high, high, low], axis=1)


def output_parts(tiles):
    sizes = []
    for left in (tiles - early_tiles(tiles), early_tiles(tiles)):
        while left:
            sizes.append(-(-left // 2))
            left -= sizes[-1]
    return sizes


def turn_trig(turns):
    quarter = jnp.floor(turns * 4.0 + 0.5)
    angle = (turns - 0.25 * quarter) * (2.0 * math.pi)
    square = angle * angle
    sine = angle * (
        1.0
        + square
        * (-1.0 / 6 + square * (1.0 / 120 + square * (-1.0 / 5040 + square * (1.0 / 362880))))
    )
    cosine = 1.0 + square * (
        -0.5
        + square
        * (1.0 / 24 + square * (-1.0 / 720 + square * (1.0 / 40320 + square * (-1.0 / 3628800))))
    )
    phase = quarter - 4.0 * jnp.floor(quarter * 0.25)
    odd = (phase == 1.0) | (phase == 3.0)
    cos_out = jnp.where(odd, sine, cosine)
    sin_out = jnp.where(odd, cosine, sine)
    cos_out = jnp.where((phase == 1.0) | (phase == 2.0), -cos_out, cos_out)
    sin_out = jnp.where(phase >= 2.0, -sin_out, sin_out)
    return cos_out, sin_out


def early_tiles(tiles):
    return tiles * 3 // 10


def pack_early_kernel(wide, base, source, *rest):
    targets, (held, in_sems, out_sems) = rest[:4], rest[4:]
    rank = lax.axis_index("wide")
    quarter = wide // 4
    late = base - early_tiles(base // LANES) * LANES
    size = base - late
    bring = [
        pltpu.make_async_copy(
            source.at[side, :, :, pl.ds(late, size)],
            held.at[:, :, pl.ds(side * size, size)],
            in_sems.at[side],
        )
        for side in range(2)
    ]
    for copy in bring:
        copy.start()
    for copy in bring:
        copy.wait()
    send = [
        pltpu.make_async_copy(
            held.at[rank ^ flip], targets[flip // quarter].at[flip % quarter], out_sems.at[flip]
        )
        for flip in range(wide)
    ]
    for copy in send:
        copy.start()
    for copy in send:
        copy.wait()


def pack_kernel(wide, base, source, centre, after, target, held, flux, in_sems, out_sems, flux_sem):
    del after
    chan = centre.shape[0]
    size = base - early_tiles(base // LANES) * LANES
    share = wide // PACK_PARTS
    peers = [pl.ds(part * share, share) for part in range(PACK_PARTS)]
    bring = [
        [
            pltpu.make_async_copy(
                source.at[side, peers[part], :, pl.ds(0, size)],
                held.at[peers[part], :, pl.ds(side * size, size)],
                in_sems.at[part, side],
            )
            for side in range(2)
        ]
        for part in range(PACK_PARTS)
    ]
    send = [
        pltpu.make_async_copy(held.at[peers[part]], target.at[peers[part]], out_sems.at[part])
        for part in range(PACK_PARTS)
    ]
    fetch = pltpu.make_async_copy(centre, flux, flux_sem)
    fetch.start()
    for pair in bring:
        for copy in pair:
            copy.start()
    fetch.wait()
    row = lax.broadcasted_iota(jnp.int32, (chan, LANES), 0)
    lane = lax.broadcasted_iota(jnp.int32, (chan, LANES), 1)
    value = jnp.zeros(row.shape, F32)
    for c in range(chan):
        value = jnp.where(row == c, flux[c], value)
    high = value.astype(BF16).astype(F32)
    middle = (value - high).astype(BF16).astype(F32)
    low = value - high - middle
    parts = jnp.where(lane == 0, high, jnp.where(lane == 1, middle, jnp.where(lane == 2, low, 0.0)))
    held[:, :, 2 * size : 2 * size + LANES] = jnp.broadcast_to(
        parts.astype(BF16)[None], (wide, chan, LANES)
    )
    for pair, copy in zip(bring, send):
        for came in pair:
            came.wait()
        copy.start()
    for copy in send:
        copy.wait()


def column_groups(groups, tiles, first_row):
    last_row = first_row + (2 * tiles - 1)
    return [row_groups_of(row, groups)[1] * GROUP for row in (first_row, last_row)]


def places_kernel(groups, tiles, padded, order, xy, after, pos_x, pos_y):
    del after
    first_row = lax.axis_index("wide") * (2 * tiles)
    col_a, col_b = column_groups(groups, tiles, first_row)
    pos_x[...] = jnp.zeros_like(pos_x)
    pos_y[...] = jnp.zeros_like(pos_y)

    def place(slot, position):
        station = order[position]
        pos_x[pl.ds(slot, 1), :] = jnp.full((1, LANES), xy[0, station], F32)
        pos_y[pl.ds(slot, 1), :] = jnp.full((1, LANES), xy[1, station], F32)

    def place_row(t, carry):
        for half in range(2):
            row = first_row + 2 * t + half
            place(half * padded + t, row_groups_of(row, groups)[0] * GROUP + (row & 63))
        return carry

    def place_col(j, carry):
        place(2 * padded + j, col_a + j)
        place(2 * padded + GROUP + j, col_b + j)
        return carry

    lax.fori_loop(0, tiles, place_row, 0, unroll=10)
    lax.fori_loop(0, GROUP, place_col, 0, unroll=16)


def predict_kernel(
    groups,
    tiles,
    padded,
    pos_x,
    pos_y,
    lm,
    flux,
    real_out,
    imag_out,
    real,
    imag,
    row_c,
    row_s,
    row_dc,
    row_ds,
    row_lc,
    row_ls,
    col_c,
    col_s,
    col_dc,
    col_ds,
    col_lc,
    col_ls,
    left_a,
    right_a,
    left_b,
    right_b,
):
    comps = lm.shape[1]
    first_row = lax.axis_index("wide") * (2 * tiles)
    edge = jnp.minimum((((first_row >> 6) + 1) * GROUP - first_row) >> 1, tiles)
    step = 0.25 / FREQ_CHANNELS
    rows = 2 * padded
    weight = flux[...] * (1.0 / math.sqrt(comps))
    for k in range(0, comps, LANES):
        lane = slice(k, k + LANES)
        axis_l = lm[0:1, lane]
        axis_m = lm[1:2, lane]
        turns = pos_x[0:rows, :] * axis_l + pos_y[0:rows, :] * axis_m
        cosine, sine = turn_trig(turns)
        row_c[:, lane] = cosine * weight[:, lane]
        row_s[:, lane] = sine * weight[:, lane]
        row_dc[:, lane], row_ds[:, lane] = turn_trig(turns * step)
        row_lc[:, lane], row_ls[:, lane] = turn_trig(turns * (UNROLL * step))
        turns = (
            pos_x[rows : rows + LANES, :] * axis_l + pos_y[rows : rows + LANES, :] * axis_m
        ).T
        col_c[lane, :], col_s[lane, :] = turn_trig(turns)
        col_dc[lane, :], col_ds[lane, :] = turn_trig(turns * step)
        col_lc[lane, :], col_ls[lane, :] = turn_trig(turns * (UNROLL * step))

    def channels(c, s, dc, ds, leap_c, leap_s):
        twice = dc + dc
        out = [(c, s), (c * dc - s * ds, s * dc + c * ds)]
        while len(out) < UNROLL:
            out.append(tuple(twice * now - before for now, before in zip(out[-1], out[-2])))
        return out, (c * leap_c - s * leap_s, s * leap_c + c * leap_s)

    def fill_col(right, k):
        part = slice(k, k + 16)
        state = [table[part, :] for table in (col_c, col_s, col_dc, col_ds, col_lc, col_ls)]
        values, (col_c[part, :], col_s[part, :]) = channels(*state)
        for u, (c, s) in enumerate(values):
            right[u, part, 0:LANES] = c.astype(BF16)
            right[u, part, LANES : 2 * LANES] = s.astype(BF16)

    def fill_row(left, r, k):
        part, low = slice(r, r + 16), slice(rows + r, rows + r + 16)
        lane = slice(k, k + LANES)
        state = [table[part, lane] for table in (row_c, row_s, row_dc, row_ds, row_lc, row_ls)]
        values, (row_c[part, lane], row_s[part, lane]) = channels(*state)
        for u, (c, s) in enumerate(values):
            left[u, part, lane] = c.astype(BF16)
            left[u, low, lane] = s.astype(BF16)

    def fill_steps(left, right):
        steps = [lambda k=k: fill_col(right, k) for k in range(0, comps, 16)]
        return steps + [
            lambda r=r, k=k: fill_row(left, r, k)
            for r in range(0, rows, 16)
            for k in range(0, comps, LANES)
        ]

    first_half = lax.broadcasted_iota(jnp.int32, (padded, LANES), 1) < GROUP
    in_a = lax.broadcasted_iota(jnp.int32, (padded, LANES), 0) < edge

    def multiply(left, right, group, u):
        product = jnp.dot(left[u], right[u], preferred_element_type=F32)
        channel = group * UNROLL + u
        with_cos, with_sin = product[:, 0:LANES], product[:, LANES : 2 * LANES]
        sums = (
            (with_cos[0:rows] + with_sin[rows : 2 * rows], real),
            (with_cos[rows : 2 * rows] - with_sin[0:rows], imag),
        )
        for side, out in sums:
            even, odd = side[0:padded], side[padded : 2 * padded]
            even = jnp.where(in_a, even, pltpu.roll(even, GROUP, 1))
            odd = jnp.where(in_a, pltpu.roll(odd, GROUP, 1), odd)
            out[pl.ds(channel, padded, stride=FREQ_CHANNELS), :] = jnp.where(first_half, even, odd)

    for step in fill_steps(left_a, right_a):
        step()

    def group_pass(now, later, group):
        steps = fill_steps(*later)
        share = -(-len(steps) // UNROLL)
        for u in range(UNROLL):
            multiply(*now, group, u)
            for step in steps[u * share : (u + 1) * share]:
                step()

    def two_groups(pair, carry):
        group_pass((left_a, right_a), (left_b, right_b), 2 * pair)
        group_pass((left_b, right_b), (left_a, right_a), 2 * pair + 1)
        return carry

    lax.fori_loop(0, FREQ_CHANNELS // (2 * UNROLL), two_groups, 0)
    size = tiles * FREQ_CHANNELS
    real_out[...] = real[0:size, :]
    imag_out[...] = imag[0:size, :].astype(BF16)


def tile_weights(groups, tiles, first_row, t, kept):
    lane = lax.broadcasted_iota(jnp.int32, (1, LANES), 1)
    row = first_row + 2 * t
    first, second = row_groups_of(row, groups)
    inside = (row & 63) + (lane >> 6)
    usable = (first != second) | (inside < (lane & 63))
    mask = kept[pl.ds((first_row >> 1) + t, 1), :].astype(F32)
    return jnp.where(usable, mask, 0.0)


def tile_lanes(t, size=LANES, offset=0):
    return pl.ds(pl.multiple_of(offset + t * size, size), size)


def late_sides(observed, tiles, t):
    return [
        observed[:, :, tile_lanes(t, LANES, side * tiles * LANES)]
        .astype(F32)
        .reshape(FREQ_CHANNELS, LANES)
        for side in range(2)
    ]


def early_lanes(early, key, lanes):
    blocks = [early[key ^ at, :, lanes].astype(F32) for at in range(early.shape[0])]
    return jnp.concatenate(blocks)


def early_sides(early, key, tiles, t):
    return [early_lanes(early, key, tile_lanes(t, LANES, side * tiles * LANES)) for side in range(2)]


def tile_stats(groups, tiles, begin, count, sides_of, shift, real, imag, kept, counts, fit, model, modes, rows):
    first_row = lax.axis_index("wide") * (2 * tiles)
    mode = lax.broadcasted_iota(jnp.int32, (MODES, LANES), 0)

    def one(at, carry):
        t = begin + at
        obs_re, obs_im = sides_of(at)
        half = tile_lanes(t, FREQ_CHANNELS)
        mod_re16, mod_im16 = (real[half, :] + shift[...]).astype(BF16), imag[half, :]
        both = pl.multiple_of(2 * at * FREQ_CHANNELS, FREQ_CHANNELS)
        model[pl.ds(both, FREQ_CHANNELS), :] = mod_re16
        model[pl.ds(both + FREQ_CHANNELS, FREQ_CHANNELS), :] = mod_im16
        mod_re, mod_im = mod_re16.astype(F32), mod_im16.astype(F32)

        def total(terms):
            return jnp.sum(terms, axis=0, keepdims=True)

        cross_re = total(obs_re * mod_re + obs_im * mod_im)
        cross_im = total(obs_im * mod_re - obs_re * mod_im)
        power = total(mod_re * mod_re + mod_im * mod_im)
        sides = [obs_re.astype(BF16), obs_im.astype(BF16), mod_re16, mod_im16]
        raw = jnp.dot(fit[...], jnp.concatenate(sides, axis=1), preferred_element_type=F32)
        raw = raw[0:MODES] + raw[MODES : 2 * MODES]
        modes[tile_lanes(at, MODES), :] = raw
        v_re, v_im, m_re, m_im = (raw[:, LANES * i : LANES * (i + 1)] for i in range(4))
        inside = (mode < counts[pl.ds(t, 1), :]).astype(F32)
        vv = total(inside * (v_re * v_re + v_im * v_im))
        vm_re = total(inside * (v_re * m_re + v_im * m_im))
        vm_im = total(inside * (v_im * m_re - v_re * m_im))
        mm = total(inside * (m_re * m_re + m_im * m_im))
        weight = tile_weights(groups, tiles, first_row, t, kept)
        parts = [cross_re, cross_im, vv, vm_re, vm_im, power, mm, jnp.zeros((1, LANES), F32)]
        rows[tile_lanes(at, 8), :] = jnp.concatenate(parts) * weight
        return carry

    lax.fori_loop(0, count, one, 0, unroll=count)


def late_stats_kernel(
    groups, tiles, observed, real, imag, kept, counts, fit, rows, model, modes, shift
):
    rest = tiles - early_tiles(tiles)
    tail = observed[:, :, 2 * rest * LANES : (2 * rest + 1) * LANES].astype(F32)
    tail = tail.reshape(FREQ_CHANNELS, LANES)
    shift[...] = jnp.broadcast_to(jnp.sum(tail, axis=1, keepdims=True), tail.shape)

    def sides(at):
        return late_sides(observed, rest, at)

    tile_stats(groups, tiles, 0, rest, sides, shift, real, imag, kept, counts, fit, model, modes, rows)


def early_stats_kernel(
    groups,
    tiles,
    by_flip,
    early,
    late_rows,
    shift,
    real,
    imag,
    kept,
    counts,
    fit,
    stats,
    model,
    modes,
    rows,
    paired,
):
    key = lax.axis_index("wide") if by_flip else 0
    ahead = early_tiles(tiles)
    rest = tiles - ahead
    rows[0 : 8 * rest, :] = late_rows[...]

    def sides(at):
        return early_sides(early, key, ahead, at)

    late = rows.at[8 * rest : 8 * tiles]
    tile_stats(groups, tiles, rest, ahead, sides, shift, real, imag, kept, counts, fit, model, modes, late)
    first_half = lax.broadcasted_iota(jnp.int32, (tiles, LANES), 1) < GROUP
    for pair in range(PAIRS):
        one_stat = rows[pl.ds(2 * pair, tiles, stride=8), :]
        other = rows[pl.ds(2 * pair + 1, tiles, stride=8), :]
        even = jnp.where(first_half, one_stat, pltpu.roll(other, GROUP, 1))
        odd = jnp.where(first_half, pltpu.roll(one_stat, GROUP, 1), other)
        paired[pl.ds(2 * tiles * pair, tiles, stride=2), :] = even
        paired[pl.ds(2 * tiles * pair + 1, tiles, stride=2), :] = odd
    stats[...] = paired[0 : PAIRS * 2 * tiles, :].astype(BF16)


def solve_kernel(
    groups,
    tiles,
    by_flip,
    wide,
    gathered,
    observed,
    early,
    late_model,
    early_model,
    late_modes,
    early_modes,
    kept,
    counts,
    order,
    expand,
    gains,
    residual,
    flat,
    full,
    weights,
    row_gain_re,
    row_gain_im,
    col_gain_re,
    col_gain_im,
    left_out,
    out_sems,
):
    stations = groups * GROUP
    rank = lax.axis_index("wide")
    first_row = rank * (2 * tiles)
    halves = stations // LANES
    count = 2 * tiles
    for k, flip in enumerate(gather_order(wide)):
        start = pl.multiple_of((rank ^ flip) * count, count & -count)
        values = gathered[k].astype(F32)
        for pair in range(PAIRS):
            flat[pair, pl.ds(start, count), :] = values[pair * count : (pair + 1) * count]
    block_id = {}
    for first in range(groups):
        for second in range(first, groups):
            block_id[first, second] = len(block_id)
    lane64 = lax.broadcasted_iota(jnp.int32, (GROUP, LANES), 1) < GROUP

    def placed_block(stat, first, half):
        pair, side = stat // 2, stat % 2
        sides = []
        for at in range(2):
            index = block_id.get((first, 2 * half + at))
            if index is None:
                sides.append(jnp.zeros((GROUP, LANES), F32))
                continue
            block = flat[pair, GROUP * index : GROUP * (index + 1), :]
            sides.append(block if at == side else pltpu.roll(block, GROUP, 1))
        return jnp.where(lane64, sides[0], sides[1])

    for stat in range(STATS):
        sign = -1.0 if stat in (1, 4) else 1.0
        for a in range(halves):
            rows_a = slice(LANES * a, LANES * (a + 1))
            for b in range(a, halves):
                rows_b = slice(LANES * b, LANES * (b + 1))
                block = jnp.concatenate([placed_block(stat, 2 * a + i, b) for i in range(2)])
                turned = block.T * sign
                if a == b:
                    full[stat, rows_a, rows_a] = block + turned
                else:
                    full[stat, rows_a, rows_b] = block
                    full[stat, rows_b, rows_a] = turned

    gain_re = jnp.ones((1, stations), F32)
    gain_im = jnp.zeros((1, stations), F32)
    for round_id in range(ROUNDS):

        def build(step, carry):
            rows = pl.ds(pl.multiple_of(step * 16, 16), 16)
            vm_re, vm_im, mm = full[3, rows, :], full[4, rows, :], full[6, rows, :]
            if round_id == 0:
                cross_re, cross_im, power = full[0, rows, :], full[1, rows, :], full[5, rows, :]
                full[0, rows, :] = cross_re - vm_re
                full[1, rows, :] = cross_im - vm_im
                full[5, rows, :] = power - mm
            else:
                vv = full[2, rows, :]
                col_re = jnp.concatenate([col_gain_re[round_id - 1, rows, :]] * halves, axis=1)
                col_im = jnp.concatenate([col_gain_im[round_id - 1, rows, :]] * halves, axis=1)
                rest_re = 1.0 - (col_re * gain_re + col_im * gain_im)
                rest_im = col_re * gain_im - col_im * gain_re
                turn_re = rest_re * vm_re + rest_im * vm_im
                turn_im = rest_re * vm_im - rest_im * vm_re
                mm = vv + (rest_re * rest_re + rest_im * rest_im) * mm + (turn_re + turn_re)
                vm_re, vm_im = vv + turn_re, turn_im
                if round_id + 1 < ROUNDS:
                    full[3, rows, :], full[4, rows, :], full[6, rows, :] = vm_re, vm_im, mm
                cross_re, cross_im = full[0, rows, :] + vm_re, full[1, rows, :] + vm_im
                power = full[5, rows, :] + mm
            for part, value in enumerate((cross_re, cross_im, power)):
                weights[rows, part * stations : (part + 1) * stations] = value.astype(BF16)
            return carry

        lax.fori_loop(0, stations // 16, build, 0, unroll=4)
        row8 = lax.broadcasted_iota(jnp.int32, (8, stations), 0)
        for iteration in range(CAL_ITERS):
            norm = gain_re * gain_re + gain_im * gain_im
            left = jnp.where(row8 == 0, gain_re, jnp.where(row8 == 1, gain_im, norm))
            high = left.astype(BF16).astype(F32)
            left = jnp.concatenate([high, left - high]).astype(BF16)
            raw = jnp.dot(left, weights[...], preferred_element_type=F32)
            raw = raw[0:8] + raw[8:16]
            with_re, with_im = raw[:, 0:stations], raw[:, stations : 2 * stations]
            below = raw[2:3, 2 * stations : 3 * stations]
            next_re = (with_re[0:1] + with_im[1:2]) / below
            next_im = (with_re[1:2] - with_im[0:1]) / below
            if iteration % 2 == 1:
                next_re = 0.5 * (next_re + gain_re)
                next_im = 0.5 * (next_im + gain_im)
            gain_re, gain_im = next_re, next_im
        lane1 = lax.broadcasted_iota(jnp.int32, (1, LANES), 1) < GROUP
        for value, row_gain, col_gain in (
            (gain_re, row_gain_re, col_gain_re),
            (gain_im, row_gain_im, col_gain_im),
        ):
            for half in range(halves):
                part = value[:, LANES * half : LANES * (half + 1)]
                turned = pltpu.roll(jnp.broadcast_to(part, (8, LANES)), GROUP, 1)[0:1]
                row_gain[2 * half, round_id : round_id + 1, :] = jnp.where(lane1, part, turned)
                row_gain[2 * half + 1, round_id : round_id + 1, :] = jnp.where(lane1, turned, part)
                col_gain[round_id, LANES * half : LANES * (half + 1), :] = jnp.broadcast_to(
                    part, (LANES, LANES)
                ).T

    mode = lax.broadcasted_iota(jnp.int32, (MODES, LANES), 0)
    lane_half = lax.broadcasted_iota(jnp.int32, (1, LANES), 1) < GROUP

    key = rank if by_flip else 0
    ahead = early_tiles(tiles)
    rest = tiles - ahead

    def tile(t, at, get_sides, model, modes):
        row = first_row + 2 * t
        first, second = row_groups_of(row, groups)
        station = first * GROUP + (row & 63)

        def row_side(table, round_id):
            low, high = table[round_id, pl.ds(station, 1), :], table[round_id, pl.ds(station + 1, 1), :]
            return jnp.where(lane_half, low, high)

        q_res, q_ims = row_gain_re[second], row_gain_im[second]
        a_re, a_im = jnp.zeros((1, LANES), F32), jnp.zeros((1, LANES), F32)
        b_re, b_im = jnp.ones((1, LANES), F32), jnp.zeros((1, LANES), F32)
        for round_id in range(ROUNDS):
            p_re, p_im = row_side(col_gain_re, round_id), row_side(col_gain_im, round_id)
            q_re, q_im = q_res[round_id : round_id + 1], q_ims[round_id : round_id + 1]
            prod_re = p_re * q_re + p_im * q_im
            prod_im = p_im * q_re - p_re * q_im
            if round_id + 1 == ROUNDS:
                break
            rest_re, rest_im = 1.0 - prod_re, -prod_im
            a_re, a_im = 1.0 + rest_re * a_re - rest_im * a_im, rest_re * a_im + rest_im * a_re
            b_re, b_im = rest_re * b_re - rest_im * b_im, rest_re * b_im + rest_im * b_re
        b_re = b_re - 1.0
        inside = (mode < counts[pl.ds(t, 1), :]).astype(F32)
        raw = modes[tile_lanes(at, MODES), :]
        v_re, v_im, m_re, m_im = (raw[:, LANES * i : LANES * (i + 1)] for i in range(4))
        f_re = inside * (a_re * v_re - a_im * v_im + b_re * m_re - b_im * m_im)
        f_im = inside * (a_re * v_im + a_im * v_re + b_re * m_im + b_im * m_re)
        both = jnp.concatenate([f_re, f_im], axis=1)
        high = both.astype(BF16)
        low = (both - high.astype(F32)).astype(BF16)
        fitted = jnp.dot(
            expand[...], jnp.concatenate([high, low, high]), preferred_element_type=F32
        )
        start = pl.multiple_of(2 * at * FREQ_CHANNELS, FREQ_CHANNELS)
        mod_re = model[pl.ds(start, FREQ_CHANNELS), :].astype(F32) + fitted[:, 0:LANES]
        mod_im = model[pl.ds(start + FREQ_CHANNELS, FREQ_CHANNELS), :].astype(F32)
        mod_im = mod_im + fitted[:, LANES : 2 * LANES]
        obs_re, obs_im = get_sides()
        weight = tile_weights(groups, tiles, first_row, t, kept)
        left_re = weight * (obs_re - (prod_re * mod_re - prod_im * mod_im))
        left_im = weight * (obs_im - (prod_re * mod_im + prod_im * mod_re))
        left_out[0, 0, :, tile_lanes(t)] = left_re.astype(BF16)
        left_out[1, 0, :, tile_lanes(t)] = left_im.astype(BF16)

    def tile_late(t, carry):
        tile(t, t, lambda: late_sides(observed, rest, t), late_model, late_modes)
        return carry

    def tile_early(t, carry):
        at = t - rest
        tile(t, at, lambda: early_sides(early, key, ahead, at), early_model, early_modes)
        return carry

    copies = []
    done = 0
    for part, size in enumerate(output_parts(tiles)):
        lax.fori_loop(done, done + size, tile_late if done < rest else tile_early, 0, unroll=size)
        lanes = pl.ds(done * LANES, size * LANES)
        copies.append(
            pltpu.make_async_copy(
                left_out.at[:, :, :, lanes], residual.at[:, :, :, lanes], out_sems.at[part]
            )
        )
        copies[-1].start()
        done += size
    hot = (
        lax.broadcasted_iota(jnp.int32, (stations, stations), 0) == order[...]
    ).astype(BF16)
    pieces = []
    for value in (gain_re, gain_im):
        high = value.astype(BF16).astype(F32)
        middle = (value - high).astype(BF16).astype(F32)
        pieces += [high, middle, value - high - middle]
    row16 = lax.broadcasted_iota(jnp.int32, (16, stations), 0)
    left = jnp.zeros((16, stations), F32)
    for at, piece in enumerate(pieces):
        left = jnp.where(row16 == at, piece, left)
    spread = lax.dot_general(
        left.astype(BF16), hot, (((1,), (1,)), ((), ())), preferred_element_type=F32
    )
    gains[0:1, :] = spread[0:1] + spread[1:2] + spread[2:3]
    gains[1:2, :] = spread[3:4] + spread[4:5] + spread[5:6]
    for copy in copies:
        copy.wait()


def call(kernel, out_shape, scratch, name, in_spaces, mib, flops=0, moved=0, out_specs=None):
    return pl.pallas_call(
        kernel,
        out_shape=out_shape,
        in_specs=[pl.BlockSpec(memory_space=space) for space in in_spaces],
        out_specs=out_specs or jax.tree.map(lambda _: pl.BlockSpec(memory_space=VMEM), out_shape),
        scratch_shapes=scratch,
        compiler_params=pltpu.CompilerParams(vmem_limit_bytes=mib << 20),
        cost_estimate=pl.CostEstimate(flops=flops, bytes_accessed=moved, transcendentals=0),
        name=name,
    )


def exchange(block, distance, wide):
    return lax.ppermute(block, "wide", [(i, i ^ distance) for i in range(wide)])


def gather_order(wide):
    order = [0, wide // 2, 3 * wide // 4, wide // 4]
    distance = wide // 8
    while distance:
        order += [place ^ distance for place in order]
        distance //= 2
    return order


def send_quarters(blocks, wide):
    quarter = wide // 4
    return [blocks[0]] + [exchange(blocks[at], at * quarter, wide) for at in (1, 2, 3)]


def exchange_early(held, wide, places, predicted):
    distance = wide // 8
    held, _ = lax.optimization_barrier((held, places))
    held = jnp.stack(held)
    while distance:
        split = held.reshape(held.shape[0], 2, distance, *held.shape[2:])
        other = exchange(split[:, 1], distance, wide)
        other, predicted = lax.optimization_barrier((other, predicted))
        held = jnp.stack([split[:, 0], other], axis=1)
        held = held.reshape(-1, distance, *held.shape[3:])
        distance //= 2
    return held[:, 0]


def gather_stats(stats, wide):
    held = jnp.stack([stats] + [exchange(stats, flip, wide) for flip in gather_order(wide)[1:4]])
    distance = wide // 8
    while distance:
        held = jnp.concatenate([held, exchange(held, distance, wide)])
        distance //= 2
    return held


def body(
    visibilities,
    kept_baseline_mask,
    fitted_mode_count,
    station_order,
    station_xy,
    comp_lm,
    comp_flux,
    centre_flux,
):
    wide = lax.axis_size("wide")
    local_chan = visibilities.shape[2]
    total = visibilities.shape[3]
    base = total // wide
    tiles = base // LANES
    padded = -(-tiles // 8) * 8
    stations = station_order.shape[0]
    groups = stations // GROUP
    comps = comp_lm.shape[1]
    rows = 2 * padded
    fit, expand = (jnp.asarray(table) for table in basis_tables())
    kept = kept_baseline_mask.reshape(total // LANES, LANES)
    counts = fitted_mode_count.reshape(tiles, LANES)

    ahead = early_tiles(tiles)
    blocks = visibilities.reshape(2, local_chan, wide, base).transpose(0, 2, 1, 3)
    hbm = pl.BlockSpec(memory_space=pltpu.MemorySpace.HBM)
    early_width = 2 * ahead * LANES
    early = pl.pallas_call(
        lambda *refs: pack_early_kernel(wide, base, *refs),
        out_shape=(jax.ShapeDtypeStruct((wide // 4, local_chan, early_width), BF16),) * 4,
        in_specs=[hbm],
        out_specs=(hbm,) * 4,
        scratch_shapes=[
            pltpu.VMEM((wide, local_chan, early_width), BF16),
            pltpu.SemaphoreType.DMA((2,)),
            pltpu.SemaphoreType.DMA((wide,)),
        ],
        compiler_params=pltpu.CompilerParams(vmem_limit_bytes=60 << 20),
        name="pack_early",
    )(blocks)
    late_width = 2 * (tiles - ahead) * LANES + LANES
    packed = pl.pallas_call(
        lambda *refs: pack_kernel(wide, base, *refs),
        out_shape=jax.ShapeDtypeStruct((wide, local_chan, late_width), BF16),
        in_specs=[hbm] * 3,
        out_specs=hbm,
        scratch_shapes=[
            pltpu.VMEM((wide, local_chan, late_width), BF16),
            pltpu.SMEM((local_chan,), F32),
            pltpu.SemaphoreType.DMA((PACK_PARTS, 2)),
            pltpu.SemaphoreType.DMA((PACK_PARTS,)),
            pltpu.SemaphoreType.DMA,
        ],
        compiler_params=pltpu.CompilerParams(vmem_limit_bytes=60 << 20),
        name="pack",
    )(blocks, centre_flux, early[0])
    early = send_quarters(early, wide)
    packed, early[1] = lax.optimization_barrier((packed, early[1]))
    observed = lax.all_to_all(packed, "wide", 0, 0, tiled=True)
    observed = observed.reshape(FREQ_CHANNELS // 8, 8, late_width)
    places = call(
        lambda *refs: places_kernel(groups, tiles, padded, *refs),
        (jax.ShapeDtypeStruct((rows + LANES, LANES), F32),) * 2,
        [],
        "places",
        [SMEM, SMEM, pltpu.MemorySpace.HBM],
        12,
        PLACES_FLOPS,
        (rows + LANES) * LANES * 8,
    )(station_order, station_xy.reshape(2, stations), packed)

    state_row = pltpu.VMEM((rows, comps), F32)
    state_col = pltpu.VMEM((comps, LANES), F32)
    left = pltpu.VMEM((UNROLL, 2 * rows, comps), BF16)
    right = pltpu.VMEM((UNROLL, comps, 2 * LANES), BF16)
    real, imag = call(
        lambda *refs: predict_kernel(groups, tiles, padded, *refs),
        (
            jax.ShapeDtypeStruct((tiles * FREQ_CHANNELS, LANES), F32),
            jax.ShapeDtypeStruct((tiles * FREQ_CHANNELS, LANES), BF16),
        ),
        [pltpu.VMEM((padded * FREQ_CHANNELS, LANES), F32)] * 2
        + [state_row] * 6
        + [state_col] * 6
        + [left, right, left, right],
        "predict",
        [VMEM] * 4,
        20,
        FREQ_CHANNELS * 2 * 2 * rows * 2 * comps * 256,
        padded * 256 * LANES * 4,
    )(*places, comp_lm, comp_flux.reshape(1, comps))
    early = exchange_early(early, wide, places[0], real)
    by_flip = local_chan == 8
    if not by_flip:
        early = early[lax.axis_index("wide") ^ jnp.arange(wide)]
        early = early.reshape(FREQ_CHANNELS // 8, 8, early_width)

    def tables(count):
        return (
            jax.ShapeDtypeStruct((count * 2 * FREQ_CHANNELS, LANES), BF16),
            jax.ShapeDtypeStruct((count * MODES, 4 * LANES), F32),
        )

    rest = tiles - ahead
    late_rows, late_model, late_modes, shift = call(
        lambda *refs: late_stats_kernel(groups, tiles, *refs),
        (
            jax.ShapeDtypeStruct((rest * 8, LANES), F32),
            *tables(rest),
            jax.ShapeDtypeStruct((FREQ_CHANNELS, LANES), F32),
        ),
        [],
        "late_stats",
        [VMEM] * 6,
        12,
        moved=rest * 256 * LANES * 8,
    )(observed, real, imag, kept, counts, fit)
    stats, early_model, early_modes = call(
        lambda *refs: early_stats_kernel(groups, tiles, by_flip, *refs),
        (jax.ShapeDtypeStruct((PAIRS * 2 * tiles, LANES), BF16), *tables(ahead)),
        [pltpu.VMEM((padded * 8, LANES), F32), pltpu.VMEM((PAIRS * 2 * padded, LANES), F32)],
        "early_stats",
        [VMEM] * 8,
        12,
        moved=ahead * 256 * LANES * 8,
    )(early, late_rows, shift, real, imag, kept, counts, fit)
    gathered = gather_stats(stats, wide)
    gains, residual = call(
        lambda *refs: solve_kernel(groups, tiles, by_flip, wide, *refs),
        (
            jax.ShapeDtypeStruct((2, stations), F32),
            jax.ShapeDtypeStruct((2, 1, FREQ_CHANNELS, base), BF16),
        ),
        [
            pltpu.VMEM((PAIRS, wide * 2 * tiles, LANES), F32),
            pltpu.VMEM((STATS, stations, stations), F32),
            pltpu.VMEM((stations, 3 * stations), BF16),
            pltpu.VMEM((groups, 8, LANES), F32),
            pltpu.VMEM((groups, 8, LANES), F32),
            pltpu.VMEM((ROUNDS, stations, LANES), F32),
            pltpu.VMEM((ROUNDS, stations, LANES), F32),
            pltpu.VMEM((2, 1, FREQ_CHANNELS, base), BF16),
            pltpu.SemaphoreType.DMA((len(output_parts(tiles)),)),
        ],
        "solve",
        [VMEM] * 11,
        16,
        moved=tiles * 256 * LANES * 6,
        out_specs=(
            pl.BlockSpec(memory_space=VMEM),
            pl.BlockSpec(memory_space=pltpu.MemorySpace.HBM),
        ),
    )(
        gathered,
        observed,
        early,
        late_model,
        early_model,
        late_modes,
        early_modes,
        kept,
        counts,
        station_order.reshape(1, stations),
        expand,
    )
    return gains, residual


def solution(mesh):
    placed = (
        P(None, None, ("band", "wide"), None),
        P("band"),
        P("wide"),
        P(),
        P(),
        P(),
        P(),
        P(("band", "wide")),
    )
    return jax.shard_map(
        body,
        mesh=mesh,
        in_specs=placed,
        out_specs=(P(None, "band"), P(None, None, "band", "wide")),
        check_vma=False,
    )
```
